32 devices in a mesh: batch: 2 (over core), seq: 16 (over z, y, x).
Axes of the slice: x: 2, y: 2, z: 4, core: 2. Of those that a mesh axis runs over, the one named last changes fastest.
Arguments:
- tokens: bfloat16 [2, 2, 4096, 1024], P(None, 'batch', 'seq'), may hold values from -6 to 6
- cotangent: bfloat16 [2, 2, 4096, 1024], P(None, 'batch', 'seq'), may hold values from -6 to 6
- lengths: int32 [2, 2], P(None, 'batch'), may hold values from 1024 to 4096, as said below
- random_blocks: int32 [2, 2, 64, 16, 3], P(None, 'batch'), may hold values from 0 to 63, as said below
- query_key_value_weight: bfloat16 [1024, 3072], P('seq', 'batch'), may hold values from -0.1875 to 0.1875
- output_weight: bfloat16 [1024, 1024], P('seq', 'batch'), may hold values from -2 to 2
- up_weight: bfloat16 [1024, 4096], P('seq', 'batch'), may hold values from -0.1875 to 0.1875
- down_weight: bfloat16 [4096, 1024], P('seq', 'batch'), may hold values from -0.09375 to 0.09375
- out_bias: float32 [1024], replicated, may hold values from -3 to 3
- up_bias: float32 [4096], replicated, may hold values from -3 to 3
- down_bias: float32 [1024], replicated, may hold values from -3 to 3
- gain_attn: float32 [1024], replicated, may hold values from 0.1 to 1.9
- shift_attn: float32 [1024], replicated, may hold values from -3 to 3
- gain_ffn: float32 [1024], replicated, may hold values from 0.1 to 1.9
- shift_ffn: float32 [1024], replicated, may hold values from -3 to 3
Outputs:
- output: bfloat16 [2, 2, 4096, 1024], P(None, 'batch', 'seq')
- input_grad: float32 [2, 2, 4096, 1024], P(None, 'batch', 'seq')
- grad_qkv: float32 [1024, 3072], P('seq', 'batch')
- output_weight_gradient: float32 [1024, 1024], P('seq', 'batch')
- grad_up: float32 [1024, 4096], P('seq', 'batch')
- down_weight_gradient: float32 [4096, 1024], P('seq', 'batch')
- grad_out_bias: float32 [1024], replicated
- grad_up_bias: float32 [4096], replicated
- grad_down_bias: float32 [1024], replicated
- grad_gain_attn: float32 [1024], replicated
- grad_shift_attn: float32 [1024], replicated
- grad_gain_ffn: float32 [1024], replicated
- grad_shift_ffn: float32 [1024], replicated
The draws below stay inside these ranges and needn't reach their ends.
Inputs may be any that keep to these rules, and one draw needn't show every extreme that they name: `lengths`: multiples of 64. Among the 2 sequences of each index of batch, one has 4096 tokens. `random_blocks`: split the blocks of a sequence into 16 groups of 4 consecutive blocks. For each micro-batch, sequence and group of query blocks, its 192 entries name blocks of each group exactly 12 times.
All inputs are finite; a program needn't handle non-finite values.
Results may differ from the reference program's by a relative error of at most 0.02.
Values may be sent and summed in bfloat16 or wider, within the bound.
No kernel may reach another device: no remote copies, remote signals or barrier semaphores. Data moves between devices by JAX's collectives and lax.ppermute only.
A program may use at most 384 MiB of HBM per device.

```python
import functools
import jax
import jax.numpy as jnp
from jax import lax

D = 1024
H = 16
FF = 4096
HD = 64
BLOCK = 64
NGLOB = 2
NRAND = 3
BLK_DEV = 4
MB = 2
SPG = 1
NBLK = 64
SLOT = 4096
SEQS = 2
N_BATCH = 2
N_SEQ = 16


def draw_lengths(key, part):
    key = jax.random.fold_in(key, 11)
    per_group = MB * SPG
    first_key, second_key = jax.random.split(key, 2)
    blocks = jax.random.randint(first_key, (N_BATCH, per_group), NBLK // 4, NBLK + 1)
    full_at = jax.random.randint(second_key, (N_BATCH, 1), 0, per_group)
    places = jnp.arange(per_group)[None, :]
    blocks = jnp.where(places == full_at, NBLK, blocks)
    blocks = blocks.reshape(N_BATCH, MB, SPG).transpose(1, 0, 2).reshape(MB, SEQS)
    return (blocks * BLOCK).astype(jnp.int32)


def draw_random_blocks(key, part):
    key = jax.random.fold_in(key, 23)
    requests = BLK_DEV * H * NRAND
    row_count = MB * SEQS * N_SEQ
    first_key, second_key = jax.random.split(key)
    base = jnp.broadcast_to(jnp.arange(requests, dtype=jnp.int32), (row_count, requests))
    mixed = jax.random.permutation(first_key, base, axis=1, independent=True)
    source = mixed % N_SEQ
    within = jax.random.randint(second_key, (row_count, requests), 0, BLK_DEV)
    chosen = source * BLK_DEV + within
    return chosen.reshape(MB, SEQS, NBLK, H, NRAND).astype(jnp.int32)


def block_scale(stream_key, extent, shards, low, top_value):
    level = 1.0
    for position, shards_of in shards:
        heights = jax.random.uniform(jax.random.fold_in(jax.random.fold_in(stream_key, 6), position), (shards_of,), jnp.float32, low / len(shards), top_value / len(shards))
        level = level * jnp.repeat(jnp.exp(heights), extent[position] // shards_of).reshape((-1,) + (1,) * (len(extent) - 1 - position))
    return level


def scatter_about(rng, extent, scale, reach, shards=(), kind=jnp.bfloat16):
    array = scale * jax.random.normal(rng, extent, jnp.float32)
    if shards:
        array = array * block_scale(rng, extent, shards, -0.22, 0.18)
    return jnp.clip(array, -reach, reach).astype(kind)


def setup_inputs(seed: int = 0) -> dict:
    streams_of = jax.random.split(jax.random.key(seed), 16)
    return {
        "tokens": scatter_about(streams_of[0], (MB, SEQS, SLOT, D), 1.0, 6.0, ((1, 2), (2, 16))),
        "cotangent": scatter_about(streams_of[1], (MB, SEQS, SLOT, D), 1.0, 6.0, ((1, 2), (2, 16))),
        "lengths": draw_lengths(jax.random.fold_in(streams_of[15], 71), 0),
        "random_blocks": draw_random_blocks(jax.random.fold_in(streams_of[15], 71), 0),
        "query_key_value_weight": scatter_about(streams_of[4], (D, 3 * D), D ** -0.5, 0.1875, ((0, 16), (1, 2))),
        "output_weight": scatter_about(streams_of[5], (D, D), (4 * D // (8 * BLOCK)) ** -0.5, 2.0, ((0, 16), (1, 2))),
        "up_weight": scatter_about(streams_of[6], (D, FF), D ** -0.5, 0.1875, ((0, 16), (1, 2))),
        "down_weight": scatter_about(streams_of[7], (FF, D), FF ** -0.5, 0.09375, ((0, 16), (1, 2))),
        "out_bias": scatter_about(streams_of[8], (D,), 0.5, 3.0, (), jnp.float32),
        "up_bias": scatter_about(streams_of[9], (FF,), 0.5, 3.0, (), jnp.float32),
        "down_bias": scatter_about(streams_of[10], (D,), 0.5, 3.0, (), jnp.float32),
        "gain_attn": jnp.clip(1.0 + 0.18 * jax.random.normal(streams_of[11], (D,), jnp.float32), 0.1, 1.9),
        "shift_attn": scatter_about(streams_of[12], (D,), 0.5, 3.0, (), jnp.float32),
        "gain_ffn": jnp.clip(1.0 + 0.18 * jax.random.normal(streams_of[13], (D,), jnp.float32), 0.1, 1.9),
        "shift_ffn": scatter_about(streams_of[14], (D,), 0.5, 3.0, (), jnp.float32),
    }


EPS = 1e-05
BIG = 1e+30
HIGH = lax.Precision.HIGHEST

@jax.custom_vjp
def low(v):
    return lax.optimization_barrier(v.astype(jnp.bfloat16)).astype(jnp.float32)

@jax.custom_vjp
def low_back(v):
    return v

def low_keep(v):
    return (low(v), None)

def low_pass(kept, grad):
    return (grad,)

def back_keep(v):
    return (v, None)

def back_low(kept, grad):
    return (low(grad),)
low.defvjp(low_keep, low_pass)
low_back.defvjp(back_keep, back_low)

def normalize(value, gain, shift):
    centre = lax.optimization_barrier(jnp.mean(value, axis=-1, keepdims=True))
    centered = value - centre
    spread = lax.optimization_barrier(jnp.mean(centered * centered, axis=-1, keepdims=True))
    return centered * lax.rsqrt(spread + EPS) * gain + shift

def softmax_mix(scores, allowed, values):
    masked = jnp.where(allowed, scores, -BIG)
    highest = lax.optimization_barrier(jnp.max(masked, axis=-1, keepdims=True))
    log_total = jnp.log(lax.optimization_barrier(jnp.sum(jnp.exp(masked - highest), axis=-1, keepdims=True))) + highest
    weights = low(jnp.exp(masked - log_total))
    return jnp.einsum('hqk,hkd->qhd', weights, values, precision=HIGH)

def attend_global(first_queries, keys_flat, values_flat, key_valid):
    scores = low_back(jnp.einsum('qhd,hkd->hqk', first_queries, keys_flat, precision=HIGH) * HD ** (-0.5))
    mixed = softmax_mix(scores, key_valid[None, None, :], values_flat)
    return mixed.reshape(first_queries.shape[0], H * HD)

def attend_sparse(queries, keys_all, values_all, key_valid, table, block_index):
    blocks_total = queries.shape[0]
    beside_all = block_index + jnp.arange(-1, 2).astype(jnp.int32)
    fixed = jnp.concatenate([jnp.arange(NGLOB).astype(jnp.int32), beside_all])
    fixed_ok = jnp.concatenate([jnp.ones((NGLOB,), dtype=jnp.bool_), beside_all < blocks_total])
    chosen = jnp.concatenate([jnp.broadcast_to(fixed, (H, NGLOB + 3)), table[block_index].astype(jnp.int32)], axis=1)
    usable = jnp.concatenate([jnp.broadcast_to(fixed_ok, (H, NGLOB + 3)), jnp.ones((H, NRAND), dtype=jnp.bool_)], axis=1)
    chosen = jnp.minimum(chosen, blocks_total - 1)
    head_ids = jnp.arange(H).astype(jnp.int32)[:, None]
    picked_keys = keys_all[head_ids, chosen].reshape(H, -1, HD)
    picked_values = values_all[head_ids, chosen].reshape(H, -1, HD)
    allowed = (usable[:, :, None] & key_valid[chosen]).reshape(H, -1)
    scores = low_back(jnp.einsum('qhd,hkd->hqk', queries[block_index], picked_keys, precision=HIGH) * HD ** (-0.5))
    return softmax_mix(scores, allowed[:, None, :], picked_values).reshape(BLOCK, H * HD)

def sequence_forward(hidden, table, limit, query_key_value_weight, output_weight, up_weight, down_weight, out_bias, up_bias, down_bias, gain_attn, shift_attn, gain_ffn, shift_ffn):
    slots_total = hidden.shape[0]
    width = hidden.shape[1]
    blocks_total = slots_total // BLOCK
    normed_one = low(normalize(hidden, gain_attn, shift_attn))
    projected_rows = jnp.dot(normed_one, query_key_value_weight, precision=HIGH)
    queries = low(low_back(projected_rows[:, :width]))
    keys = low(low_back(projected_rows[:, width:2 * width]))
    values = low(low_back(projected_rows[:, 2 * width:]))
    key_valid = jnp.arange(slots_total) < limit
    query_blocks = queries.reshape(blocks_total, BLOCK, H, HD)
    key_blocks = keys.reshape(blocks_total, BLOCK, H, HD).transpose(2, 0, 1, 3)
    value_blocks = values.reshape(blocks_total, BLOCK, H, HD).transpose(2, 0, 1, 3)
    first_queries = queries[:NGLOB * BLOCK].reshape(NGLOB * BLOCK, H, HD)
    keys_flat = keys.reshape(slots_total, H, HD).transpose(1, 0, 2)
    values_flat = values.reshape(slots_total, H, HD).transpose(1, 0, 2)
    global_part = jax.checkpoint(attend_global)(first_queries, keys_flat, values_flat, key_valid)
    sparse_fn = jax.checkpoint(functools.partial(attend_sparse, query_blocks, key_blocks, value_blocks, key_valid.reshape(blocks_total, BLOCK), table))
    sparse_part = lax.map(sparse_fn, jnp.arange(NGLOB, blocks_total).astype(jnp.int32))
    attended = low(low_back(jnp.concatenate([global_part, sparse_part.reshape(-1, width)], axis=0)))
    middle = hidden + low_back(jnp.dot(attended, output_weight, precision=HIGH) + out_bias)
    normed_two = low(normalize(middle, gain_ffn, shift_ffn))
    before = low_back(jnp.dot(normed_two, up_weight, precision=HIGH) + up_bias)
    activated = low(jax.nn.gelu(before, approximate=True))
    return middle + jnp.dot(activated, down_weight, precision=HIGH) + down_bias

def reference(tokens, cotangent, lengths, random_blocks, query_key_value_weight, output_weight, up_weight, down_weight, out_bias, up_bias, down_bias, gain_attn, shift_attn, gain_ffn, shift_ffn):
    params = tuple((member.astype(jnp.float32) for member in (query_key_value_weight, output_weight, up_weight, down_weight, out_bias, up_bias, down_bias, gain_attn, shift_attn, gain_ffn, shift_ffn)))
    inputs = tokens.reshape(-1, SLOT, D).astype(jnp.float32)
    seeds = cotangent.reshape(-1, SLOT, D).astype(jnp.float32)
    tables = random_blocks.reshape(-1, NBLK, H, NRAND)
    limits = lengths.reshape(-1)

    def advance(carry, item):
        hidden, seed_grad, table, limit = item

        def forward(value, *weights):
            return sequence_forward(value, table, limit, *weights)
        result, pull = jax.vjp(forward, hidden, *params)
        grads = pull(seed_grad)
        summed = tuple((total + extra for total, extra in zip(carry, grads[1:])))
        return (summed, (result.astype(jnp.bfloat16), grads[0]))
    start = tuple((jnp.zeros(member.shape, jnp.float32) for member in params))
    totals, (results, input_grads) = lax.scan(advance, start, (inputs, seeds, tables, limits))
    full_shape = (MB, SEQS, SLOT, D)
    return (results.reshape(full_shape), input_grads.reshape(full_shape), totals[0], totals[1], totals[2], totals[3], totals[4], totals[5], totals[6], totals[7], totals[8], totals[9], totals[10])
```

```python
import functools

import jax
import jax.numpy as jnp
from jax import lax
from jax.experimental import pallas as pl
from jax.experimental.pallas import tpu as pltpu
from jax.sharding import PartitionSpec as P

H = 16
HD = 64
BLOCK = 64
NGLOB = 2
NRAND = 3

EPS = 1e-05
BIG = 1e30
SCALE = HD ** (-0.5)
GELU_C = 0.7978845608028654
GELU_A = 0.044715
BF = jnp.bfloat16
F32 = jnp.float32
VMEM_LIMIT = 56 * 1024 * 1024

WHOLE = pl.BlockSpec(memory_space=pltpu.VMEM)
SMEM = pl.BlockSpec(memory_space=pltpu.SMEM)


def nn(a, b):
    return lax.dot_general(a, b, (((1,), (0,)), ((), ())), preferred_element_type=F32)


def nt(a, b):
    return lax.dot_general(a, b, (((1,), (1,)), ((), ())), preferred_element_type=F32)


def tn(a, b):
    return lax.dot_general(a, b, (((0,), (0,)), ((), ())), preferred_element_type=F32)


def params():
    return pltpu.CompilerParams(vmem_limit_bytes=VMEM_LIMIT)


def cost(flops, nbytes, trans=0):
    return pl.CostEstimate(flops=int(flops), bytes_accessed=int(nbytes), transcendentals=int(trans))


def constant(shape):
    return pl.BlockSpec(shape, lambda i: (0,) * len(shape))


def norm_stats(value):
    centre = jnp.mean(value, axis=-1, keepdims=True)
    centered = value - centre
    spread = jnp.mean(centered * centered, axis=-1, keepdims=True)
    rstd = lax.rsqrt(spread + EPS)
    return centered * rstd, rstd


def project_kernel(x_ref, gain_ref, shift_ref, w_ref, qkv_ref, h_ref, *, micros, local, lanes):
    fb = w_ref.shape[3]
    width = x_ref.shape[1]

    @pl.when(pl.program_id(0) == 0)
    def _():
        xhat, _ = norm_stats(x_ref[...].astype(F32))
        h_ref[...] = (xhat * gain_ref[...] + shift_ref[...]).astype(BF)

    y = nn(h_ref[...], w_ref[0].reshape(width, fb)).astype(BF)
    for m in range(micros):
        for i in range(fb // lanes):
            qkv_ref[m, i, 0] = y[m * local : (m + 1) * local, i * lanes : (i + 1) * lanes]


def project(x, gain, shift, w, micros, local, lanes):
    nb, n, _, fb = w.shape
    rows, width = x.shape
    groups = width // lanes
    kr = width // n
    kernel = functools.partial(project_kernel, micros=micros, local=local, lanes=lanes)
    return pl.pallas_call(
        kernel,
        grid=(3 * nb,),
        in_specs=[
            constant((rows, width)),
            constant((1, width)),
            constant((1, width)),
            pl.BlockSpec((1, n, kr, fb), lambda g: (g // 3, 0, g % 3, 0)),
        ],
        out_specs=[
            pl.BlockSpec((micros, fb // lanes, 1, local, lanes), lambda g: (0, g % nb, g // nb, 0, 0)),
            constant((rows, width)),
        ],
        out_shape=[
            jax.ShapeDtypeStruct((micros, groups, 3, local, lanes), BF),
            jax.ShapeDtypeStruct((rows, width), BF),
        ],
        compiler_params=params(),
        cost_estimate=cost(6 * rows * width * width, 14 * width * width),
        name="project",
    )(x, gain, shift, w)


def lane_item(shape):
    return lax.broadcasted_iota(jnp.int32, shape, len(shape) - 1) // HD


def block_diagonal(value, per):
    if per == 1:
        return value
    item = lane_item(value.shape)
    zero = jnp.zeros_like(value)
    return jnp.concatenate([jnp.where(item == i, value, zero) for i in range(per)], axis=0)


def take_diagonal(full, per):
    if per == 1:
        return full
    item = lane_item((BLOCK, full.shape[1]))
    out = full[:BLOCK]
    for i in range(1, per):
        out = jnp.where(item == i, full[i * BLOCK : (i + 1) * BLOCK], out)
    return out


def pick(ref, part, blocks, bpd):
    out = ref[blocks[0] // bpd, part, blocks[0] % bpd]
    item = lane_item(out.shape)
    for i in range(1, len(blocks)):
        out = jnp.where(item == i, ref[blocks[i] // bpd, part, blocks[i] % bpd], out)
    return out


def key_lists(b, table_ref, limit, nblk, per):
    shared = [0, 1, b - 1, b, jnp.minimum(b + 1, nblk - 1)]
    lists = [[s] for s in shared]
    biases = [
        None,
        None,
        jnp.where((b - 1) * BLOCK < limit, 0.0, -BIG),
        jnp.where(b * BLOCK < limit, 0.0, -BIG),
        jnp.where(((b + 1) * BLOCK < limit) & (b + 1 < nblk), 0.0, -BIG),
    ]
    item = lane_item((1, per * HD))
    for r in range(NRAND):
        blocks = [table_ref[b * per * NRAND + i * NRAND + r] for i in range(per)]
        bias = jnp.where(blocks[0] * BLOCK < limit, 0.0, -BIG)
        for i in range(1, per):
            bias = jnp.where(item == i, jnp.where(blocks[i] * BLOCK < limit, 0.0, -BIG), bias)
        lists.append(blocks)
        biases.append(bias)
    return lists, biases


def masked_scores(keys, queries, biases):
    s = nt(keys, queries)
    parts = []
    for i, bias in enumerate(biases):
        part = s[i * BLOCK : (i + 1) * BLOCK]
        parts.append(part if bias is None else part + bias)
    return jnp.concatenate(parts, axis=0)


def global_keys(ref, part, c, bpd, chunk):
    span = chunk // (bpd * BLOCK)
    return ref[pl.ds(c * span, span), part].reshape(chunk, ref.shape[4])


def attend_kernel(table_ref, limit_ref, qkv_ref, out_ref, lse_ref, s_ref, *, per, bpd, nblk):
    limit = limit_ref[0]
    lanes = per * HD
    chunk = 2 * bpd * BLOCK
    chunks = nblk * BLOCK // chunk

    def query(b):
        q = qkv_ref[b // bpd, 0, b % bpd] * jnp.asarray(SCALE, BF)
        return block_diagonal(q, per)

    both = jnp.concatenate([query(g) for g in range(NGLOB)], axis=0)
    rowid = lax.broadcasted_iota(jnp.int32, (chunk, NGLOB * lanes), 0)

    def score(c, top):
        s = nt(global_keys(qkv_ref, 1, c, bpd, chunk), both)
        s = jnp.where(c * chunk + rowid < limit, s, -BIG)
        s_ref[pl.ds(c * chunk, chunk), :] = s
        return jnp.maximum(top, jnp.max(s, axis=0, keepdims=True))

    top = lax.fori_loop(0, chunks, score, jnp.full((1, NGLOB * lanes), -BIG, F32))

    def total(c, sums):
        p = jnp.exp(s_ref[pl.ds(c * chunk, chunk), :] - top)
        s_ref[pl.ds(c * chunk, chunk), :] = p
        return sums + jnp.sum(p, axis=0, keepdims=True)

    sums = lax.fori_loop(0, chunks, total, jnp.zeros((1, NGLOB * lanes), F32))
    inv = 1.0 / sums
    lse = top + jnp.log(sums)
    for g in range(NGLOB):
        lse_ref[pl.ds(g, 1), :] = lse[:, g * lanes : (g + 1) * lanes]

    def mix(c, acc):
        w = (s_ref[pl.ds(c * chunk, chunk), :] * inv).astype(BF)
        return acc + tn(w, global_keys(qkv_ref, 2, c, bpd, chunk))

    acc = lax.fori_loop(0, chunks, mix, jnp.zeros((NGLOB * lanes, lanes), F32))
    for g in range(NGLOB):
        out_ref[g // bpd, g % bpd] = take_diagonal(acc[g * lanes : (g + 1) * lanes], per).astype(BF)

    def sparse(b, carry):
        lists, biases = key_lists(b, table_ref, limit, nblk, per)
        keys = jnp.concatenate([pick(qkv_ref, 1, blocks, bpd) for blocks in lists], axis=0)
        values = jnp.concatenate([pick(qkv_ref, 2, blocks, bpd) for blocks in lists], axis=0)
        s = masked_scores(keys, query(b), biases)
        top = jnp.max(s, axis=0, keepdims=True)
        p = jnp.exp(s - top)
        sums = jnp.sum(p, axis=0, keepdims=True)
        w = (p * (1.0 / sums)).astype(BF)
        lse_ref[pl.ds(b, 1), :] = top + jnp.log(sums)
        out_ref[b // bpd, b % bpd] = take_diagonal(tn(w, values), per).astype(BF)
        return carry

    lax.fori_loop(NGLOB, nblk, sparse, 0, unroll=2)


def attend(qkv, table, limit, per):
    n, _, bpd, _, lanes = qkv.shape
    nblk = n * bpd
    kernel = functools.partial(attend_kernel, per=per, bpd=bpd, nblk=nblk)
    return pl.pallas_call(
        kernel,
        in_specs=[SMEM, SMEM, WHOLE],
        out_specs=[WHOLE, WHOLE],
        out_shape=[
            jax.ShapeDtypeStruct((n, bpd, BLOCK, lanes), BF),
            jax.ShapeDtypeStruct((nblk, lanes), F32),
        ],
        scratch_shapes=[pltpu.VMEM((nblk * BLOCK, NGLOB * lanes), F32)],
        compiler_params=params(),
        cost_estimate=cost(40e9, 4e6, 1e7),
        name="attend",
    )(table, limit, qkv)


def attend_back_kernel(
    table_ref, limit_ref, qkv_ref, dout_ref, lse_ref, grad_ref, dk_ref, dv_ref, w_ref, dw_ref, *, per, bpd, nblk
):
    limit = limit_ref[0]
    lanes = per * HD
    chunk = 2 * bpd * BLOCK
    span = 2
    chunks = nblk * BLOCK // chunk
    scale_low = jnp.asarray(SCALE, BF)

    def query(b):
        return block_diagonal(qkv_ref[b // bpd, 0, b % bpd] * scale_low, per)

    def upstream(b):
        return block_diagonal(dout_ref[b // bpd, b % bpd], per)

    both = jnp.concatenate([query(g) for g in range(NGLOB)], axis=0)
    dboth = jnp.concatenate([upstream(g) for g in range(NGLOB)], axis=0)
    lse = jnp.concatenate([lse_ref[pl.ds(g, 1), :] for g in range(NGLOB)], axis=1)
    rowid = lax.broadcasted_iota(jnp.int32, (chunk, NGLOB * lanes), 0)

    def first(c, centre):
        s = nt(global_keys(qkv_ref, 1, c, bpd, chunk), both)
        s = jnp.where(c * chunk + rowid < limit, s, -BIG)
        w = jnp.exp(s - lse)
        dw = nt(global_keys(qkv_ref, 2, c, bpd, chunk), dboth)
        w_ref[pl.ds(c * chunk, chunk), :] = w
        dw_ref[pl.ds(c * chunk, chunk), :] = dw
        return centre + jnp.sum(w * dw, axis=0, keepdims=True)

    centre = lax.fori_loop(0, chunks, first, jnp.zeros((1, NGLOB * lanes), F32))

    def second(c, acc):
        w = w_ref[pl.ds(c * chunk, chunk), :]
        ds = (w * (dw_ref[pl.ds(c * chunk, chunk), :] - centre)).astype(BF)
        dk_ref[pl.ds(c * span, span)] = nn(ds, both).reshape(span, bpd, BLOCK, lanes)
        dv_ref[pl.ds(c * span, span)] = nn(w.astype(BF), dboth).reshape(span, bpd, BLOCK, lanes)
        return acc + tn(ds, global_keys(qkv_ref, 1, c, bpd, chunk))

    acc = lax.fori_loop(0, chunks, second, jnp.zeros((NGLOB * lanes, lanes), F32))
    for g in range(NGLOB):
        dq = take_diagonal(acc[g * lanes : (g + 1) * lanes], per) * SCALE
        grad_ref[g // bpd, 0, g % bpd] = dq.astype(BF)

    def sparse(b, carry):
        lists, biases = key_lists(b, table_ref, limit, nblk, per)
        keys = jnp.concatenate([pick(qkv_ref, 1, blocks, bpd) for blocks in lists], axis=0)
        values = jnp.concatenate([pick(qkv_ref, 2, blocks, bpd) for blocks in lists], axis=0)
        q = query(b)
        do = upstream(b)
        s = masked_scores(keys, q, biases)
        w = jnp.exp(s - lse_ref[pl.ds(b, 1), :])
        dw = nt(values, do)
        centre = jnp.sum(w * dw, axis=0, keepdims=True)
        ds = (w * (dw - centre)).astype(BF)
        grad_ref[b // bpd, 0, b % bpd] = (take_diagonal(tn(ds, keys), per) * SCALE).astype(BF)
        dk = nn(ds, q)
        dv = nn(w.astype(BF), do)
        item = lane_item((BLOCK, lanes))
        for ref, full in ((dk_ref, dk), (dv_ref, dv)):
            for k, blocks in enumerate(lists):
                part = full[k * BLOCK : (k + 1) * BLOCK]
                for i, block in enumerate(blocks):
                    term = part if len(blocks) == 1 else jnp.where(item == i, part, 0.0)
                    ref[block // bpd, block % bpd] += term
        return carry

    lax.fori_loop(NGLOB, nblk, sparse, 0, unroll=2)

    def finish(c, carry):
        grad_ref[c, 1] = dk_ref[c].astype(BF)
        grad_ref[c, 2] = dv_ref[c].astype(BF)
        return carry

    lax.fori_loop(0, nblk // bpd, finish, 0)


def attend_back(qkv, dout, lse, table, limit, per):
    n, _, bpd, _, lanes = qkv.shape
    nblk = n * bpd
    kernel = functools.partial(attend_back_kernel, per=per, bpd=bpd, nblk=nblk)
    return pl.pallas_call(
        kernel,
        in_specs=[SMEM, SMEM, WHOLE, WHOLE, WHOLE],
        out_specs=WHOLE,
        out_shape=jax.ShapeDtypeStruct((n, 3, bpd, BLOCK, lanes), BF),
        scratch_shapes=[
            pltpu.VMEM((n, bpd, BLOCK, lanes), F32),
            pltpu.VMEM((n, bpd, BLOCK, lanes), F32),
            pltpu.VMEM((nblk * BLOCK, NGLOB * lanes), F32),
            pltpu.VMEM((nblk * BLOCK, NGLOB * lanes), F32),
        ],
        compiler_params=params(),
        cost_estimate=cost(80e9, 8e6, 1e7),
        name="attend_back",
    )(table, limit, qkv, dout, lse)


def middle_kernel(
    o_ref,
    x_ref,
    g_ref,
    wo_ref,
    u_ref,
    d_ref,
    out_bias_ref,
    up_bias_ref,
    down_bias_ref,
    gain_ref,
    shift_ref,
    result_ref,
    dmid_ref,
    branch_ref,
    dout_ref,
    att_ref,
    h_ref,
    act_ref,
    pre_grad_ref,
    d_out_bias_ref,
    d_up_bias_ref,
    d_down_bias_ref,
    d_gain_ref,
    d_shift_ref,
    mid_ref,
    acc_ref,
    dh_ref,
    *,
    local,
    lanes,
):
    step = pl.program_id(0)
    micros, groups = o_ref.shape[:2]
    nb, fb = wo_ref.shape[0], wo_ref.shape[3]
    width = x_ref.shape[1]

    @pl.when(step == 0)
    def _():
        for m in range(micros):
            for i in range(groups):
                att_ref[m * local : (m + 1) * local, i * lanes : (i + 1) * lanes] = o_ref[m, i]
        att = att_ref[...]
        for b in range(nb):
            cols = slice(b * fb, (b + 1) * fb)
            y = nn(att, wo_ref[b].reshape(width, fb))
            mid_ref[:, cols] = x_ref[:, cols].astype(F32) + y + out_bias_ref[:, cols]
        mid = mid_ref[...]
        xhat, _ = norm_stats(mid)
        h_ref[...] = (xhat * gain_ref[...] + shift_ref[...]).astype(BF)
        acc_ref[...] = mid + down_bias_ref[...]
        dh_ref[...] = jnp.zeros_like(dh_ref)
        d_down_bias_ref[...] = jnp.sum(g_ref[...].astype(F32), axis=0, keepdims=True)

    up = u_ref[0].reshape(width, fb)
    pre = nn(h_ref[...], up) + up_bias_ref[...]
    square = pre * pre
    gate = jnp.tanh(GELU_C * pre * (1.0 + GELU_A * square))
    half = 0.5 * (1.0 + gate)
    act = (pre * half).astype(BF)
    slope = half + 0.5 * pre * (1.0 - gate * gate) * (GELU_C * (1.0 + 3.0 * GELU_A * square))
    act_ref[...] = act
    dact = None
    for b in range(nb):
        cols = slice(b * fb, (b + 1) * fb)
        term = nt(g_ref[:, cols], d_ref[b].reshape(fb, fb))
        dact = term if dact is None else dact + term
    pre_grad = (dact * slope).astype(BF)
    pre_grad_ref[...] = pre_grad
    d_up_bias_ref[...] = jnp.sum(pre_grad.astype(F32), axis=0, keepdims=True)
    for b in range(nb):
        cols = slice(b * fb, (b + 1) * fb)
        acc_ref[:, cols] += nn(act, d_ref[b].reshape(fb, fb))
    dh_ref[...] += nt(pre_grad, up)

    @pl.when(step == pl.num_programs(0) - 1)
    def _():
        result_ref[...] = acc_ref[...].astype(BF)
        dh = dh_ref[...]
        xhat, rstd = norm_stats(mid_ref[...])
        d_gain_ref[...] = jnp.sum(dh * xhat, axis=0, keepdims=True)
        d_shift_ref[...] = jnp.sum(dh, axis=0, keepdims=True)
        d = dh * gain_ref[...]
        inner = d - jnp.mean(d, axis=-1, keepdims=True) - xhat * jnp.mean(d * xhat, axis=-1, keepdims=True)
        dmid = g_ref[...].astype(F32) + rstd * inner
        dmid_ref[...] = dmid
        branch = dmid.astype(BF)
        branch_ref[...] = branch
        d_out_bias_ref[...] = jnp.sum(branch.astype(F32), axis=0, keepdims=True)
        dout = None
        for b in range(nb):
            term = nt(branch[:, b * fb : (b + 1) * fb], wo_ref[b].reshape(width, fb))
            dout = term if dout is None else dout + term
        dout = dout.astype(BF)
        for m in range(micros):
            for i in range(groups):
                dout_ref[m, i] = dout[m * local : (m + 1) * local, i * lanes : (i + 1) * lanes]


def middle(o, x, g, w, out_bias, up_bias, down_bias, gain, shift):
    micros, groups, local, lanes = o.shape
    rows, width = x.shape
    nb, n, _, fb = w.shape
    hidden = up_bias.shape[1]
    kr = width // n
    fr = hidden // n
    nd = fb // fr
    steps = hidden // fb
    per_b = steps // nb
    up_at = fr // kr
    out_at = up_at + per_b
    full = lambda dtype: jax.ShapeDtypeStruct((rows, width), dtype)
    vector = jax.ShapeDtypeStruct((1, width), F32)
    kernel = functools.partial(middle_kernel, local=local, lanes=lanes)
    return pl.pallas_call(
        kernel,
        grid=(steps,),
        in_specs=[
            constant((micros, groups, local, lanes)),
            constant((rows, width)),
            constant((rows, width)),
            pl.BlockSpec((nb, n, kr, fb), lambda i: (0, 0, out_at, 0)),
            pl.BlockSpec((1, n, kr, fb), lambda i: (i // per_b, 0, up_at + i % per_b, 0)),
            pl.BlockSpec((nb, nd, fr, fb), lambda i: (0, i, 0, 0)),
            constant((1, width)),
            pl.BlockSpec((1, fb), lambda i: (0, i)),
            constant((1, width)),
            constant((1, width)),
            constant((1, width)),
        ],
        out_specs=[
            constant((rows, width)),
            constant((rows, width)),
            constant((rows, width)),
            constant((micros, groups, local, lanes)),
            constant((rows, width)),
            constant((rows, width)),
            pl.BlockSpec((rows, fb), lambda i: (0, i)),
            pl.BlockSpec((rows, fb), lambda i: (0, i)),
            constant((1, width)),
            pl.BlockSpec((1, fb), lambda i: (0, i)),
            constant((1, width)),
            constant((1, width)),
            constant((1, width)),
        ],
        out_shape=[
            full(BF),
            full(F32),
            full(BF),
            jax.ShapeDtypeStruct((micros, groups, local, lanes), BF),
            full(BF),
            full(BF),
            jax.ShapeDtypeStruct((rows, hidden), BF),
            jax.ShapeDtypeStruct((rows, hidden), BF),
            vector,
            jax.ShapeDtypeStruct((1, hidden), F32),
            vector,
            vector,
            vector,
        ],
        scratch_shapes=[pltpu.VMEM((rows, width), F32)] * 3,
        compiler_params=params(),
        cost_estimate=cost(8 * rows * width * hidden + 4 * rows * width * width, 50e6),
        name="middle",
    )(o, x, g, w, w, w, out_bias, up_bias, down_bias, gain, shift)


def ffn_grads_kernel(act_ref, g_ref, h_ref, pre_grad_ref, down_ref, up_ref, ht_ref):
    nb, nd, fr, fb = down_ref.shape
    n, kr = up_ref.shape[1:3]

    @pl.when(pl.program_id(0) == 0)
    def _():
        ht_ref[...] = h_ref[...].T

    up_ref[0] = nn(ht_ref[...], pre_grad_ref[...]).astype(BF).reshape(n, kr, fb)
    act_t = act_ref[...].T
    for b in range(nb):
        y = nn(act_t, g_ref[:, b * fb : (b + 1) * fb])
        down_ref[b] = y.astype(BF).reshape(nd, fr, fb)


def ffn_grads(act, g, h, pre_grad, nb, n):
    rows, hidden = act.shape
    width = g.shape[1]
    fb = width // nb
    kr, fr = width // n, hidden // n
    steps = hidden // fb
    per_b = steps // nb
    return pl.pallas_call(
        ffn_grads_kernel,
        grid=(steps,),
        in_specs=[
            pl.BlockSpec((rows, fb), lambda i: (0, i)),
            constant((rows, width)),
            constant((rows, width)),
            pl.BlockSpec((rows, fb), lambda i: (0, i)),
        ],
        out_specs=[
            pl.BlockSpec((nb, fb // fr, fr, fb), lambda i: (0, i, 0, 0)),
            pl.BlockSpec((1, n, kr, fb), lambda i: (i // per_b, 0, i % per_b, 0)),
        ],
        out_shape=[
            jax.ShapeDtypeStruct((nb, n, fr, fb), BF),
            jax.ShapeDtypeStruct((nb, n, per_b * kr, fb), BF),
        ],
        scratch_shapes=[pltpu.VMEM((width, rows), BF)],
        compiler_params=params(),
        cost_estimate=cost(4 * rows * width * hidden, 30e6),
        name="ffn_grads",
    )(act, g, h, pre_grad)


def out_grad_kernel(att_ref, branch_ref, out_ref, at_ref):
    n, kr, fb = out_ref.shape[1:]

    @pl.when(pl.program_id(0) == 0)
    def _():
        at_ref[...] = att_ref[...].T

    out_ref[0] = nn(at_ref[...], branch_ref[...]).astype(BF).reshape(n, kr, fb)


def out_grad(att, branch, nb, n):
    rows, width = att.shape
    fb = width // nb
    kr = width // n
    return pl.pallas_call(
        out_grad_kernel,
        grid=(nb,),
        in_specs=[constant((rows, width)), pl.BlockSpec((rows, fb), lambda b: (0, b))],
        out_specs=pl.BlockSpec((1, n, kr, fb), lambda b: (b, 0, 0, 0)),
        out_shape=jax.ShapeDtypeStruct((nb, n, kr, fb), BF),
        scratch_shapes=[pltpu.VMEM((width, rows), BF)],
        compiler_params=params(),
        cost_estimate=cost(2 * rows * width * width, 5e6),
        name="out_grad",
    )(att, branch)


def qkv_grad_kernel(h_ref, grad_ref, all_ref, out_ref, ht_ref, *, local, lanes):
    micros, groups = grad_ref.shape[:2]
    n, kr, fb = out_ref.shape[1:]

    @pl.when(pl.program_id(0) == 0)
    def _():
        ht_ref[...] = h_ref[...].T
        for m in range(micros):
            for i in range(groups):
                for j in range(3):
                    col = (j * groups + i) * lanes
                    all_ref[m * local : (m + 1) * local, col : col + lanes] = grad_ref[m, i, j]

    cols = pl.ds(pl.multiple_of(pl.program_id(0) * fb, fb), fb)
    out_ref[0] = nn(ht_ref[...], all_ref[:, cols]).astype(BF).reshape(n, kr, fb)


def qkv_grad(h, grad, nb, n):
    micros, groups, _, local, lanes = grad.shape
    rows, width = h.shape
    fb = width // nb
    kr = width // n
    kernel = functools.partial(qkv_grad_kernel, local=local, lanes=lanes)
    return pl.pallas_call(
        kernel,
        grid=(3 * nb,),
        in_specs=[constant((rows, width)), constant((micros, groups, 3, local, lanes))],
        out_specs=[
            constant((rows, 3 * width)),
            pl.BlockSpec((1, n, kr, fb), lambda g: (g // 3, 0, g % 3, 0)),
        ],
        out_shape=[
            jax.ShapeDtypeStruct((rows, 3 * width), BF),
            jax.ShapeDtypeStruct((nb, n, 3 * kr, fb), BF),
        ],
        scratch_shapes=[pltpu.VMEM((width, rows), BF)],
        compiler_params=params(),
        cost_estimate=cost(6 * rows * width * width, 15e6),
        name="qkv_grad",
    )(h, grad)


def input_grad_kernel(all_ref, w_ref, x_ref, gain_ref, dmid_ref, out_ref, d_gain_ref, d_shift_ref, dh_ref):
    width = x_ref.shape[1]
    fb = w_ref.shape[3]
    term = nt(all_ref[...], w_ref[0].reshape(width, fb))

    @pl.when(pl.program_id(0) == 0)
    def _():
        dh_ref[...] = term

    @pl.when(pl.program_id(0) > 0)
    def _():
        dh_ref[...] += term

    @pl.when(pl.program_id(0) == pl.num_programs(0) - 1)
    def _():
        dh = dh_ref[...]
        xhat, rstd = norm_stats(x_ref[...].astype(F32))
        d_gain_ref[...] = jnp.sum(dh * xhat, axis=0, keepdims=True)
        d_shift_ref[...] = jnp.sum(dh, axis=0, keepdims=True)
        d = dh * gain_ref[...]
        inner = d - jnp.mean(d, axis=-1, keepdims=True) - xhat * jnp.mean(d * xhat, axis=-1, keepdims=True)
        out_ref[...] = dmid_ref[...] + rstd * inner


def input_grad(grad_all, w, x, gain, dmid):
    rows, width = x.shape
    nb, n, _, fb = w.shape
    kr = width // n
    vector = jax.ShapeDtypeStruct((1, width), F32)
    return pl.pallas_call(
        input_grad_kernel,
        grid=(3 * nb,),
        in_specs=[
            pl.BlockSpec((rows, fb), lambda g: (0, g)),
            pl.BlockSpec((1, n, kr, fb), lambda g: (g // 3, 0, g % 3, 0)),
            constant((rows, width)),
            constant((1, width)),
            constant((rows, width)),
        ],
        out_specs=[constant((rows, width)), constant((1, width)), constant((1, width))],
        out_shape=[jax.ShapeDtypeStruct((rows, width), F32), vector, vector],
        scratch_shapes=[pltpu.VMEM((rows, width), F32)],
        compiler_params=params(),
        cost_estimate=cost(6 * rows * width * width, 20e6),
        name="input_grad",
    )(grad_all, w, x, gain, dmid)


def stacked(shard, fb):
    rows, cols = shard.shape
    return shard.reshape(rows, cols // fb, fb).transpose(1, 0, 2).reshape(-1, fb)


def unstacked(stack, cols):
    fb = stack.shape[1]
    parts = cols // fb
    return stack.reshape(parts, -1, fb).transpose(1, 0, 2).reshape(-1, cols)


def body(
    tokens,
    cotangent,
    lengths,
    random_blocks,
    query_key_value_weight,
    output_weight,
    up_weight,
    down_weight,
    out_bias,
    up_bias,
    down_bias,
    gain_attn,
    shift_attn,
    gain_ffn,
    shift_ffn,
):
    n = lax.axis_size("seq")
    nb = lax.axis_size("batch")
    position = lax.axis_index("seq")
    micros, _, local, width = tokens.shape
    nblk = n * local // BLOCK
    bpd = local // BLOCK
    per = micros * H // n
    lanes = per * HD
    groups = H // per
    fb = width // nb
    both = ("batch", "seq")
    row = lambda v: v.reshape(1, -1)

    w_qkv = lax.all_gather(stacked(query_key_value_weight, fb), both)
    rest = jnp.concatenate([down_weight, stacked(up_weight, fb), output_weight], axis=0)
    w_rest = lax.all_gather(rest, both)
    w_qkv = w_qkv.reshape((nb, n) + w_qkv.shape[1:])
    w_rest = w_rest.reshape((nb, n) + w_rest.shape[1:])

    x = tokens.reshape(micros * local, width)
    g = cotangent.reshape(micros * local, width)
    micro = position * per // H
    head = position * per % H
    table = lax.dynamic_slice(
        random_blocks[:, 0], (micro, 0, head, 0), (1, nblk, per, NRAND)
    ).reshape(-1)
    limit = lax.dynamic_slice(lengths[:, 0], (micro,), (1,))

    def swap(value):
        return lax.all_to_all(value, "seq", split_axis=0, concat_axis=0, tiled=True)

    qkv, h1 = project(x, row(gain_attn), row(shift_attn), w_qkv, micros, local, lanes)
    qkv_all = swap(qkv.reshape(n, 3, local, lanes)).reshape(n, 3, bpd, BLOCK, lanes)
    mixed, lse = attend(qkv_all, table, limit, per)
    o = swap(mixed.reshape(n, local, lanes)).reshape(micros, groups, local, lanes)
    (
        result,
        dmid,
        branch,
        dout,
        att,
        h2,
        act,
        pre_grad,
        d_out_bias,
        d_up_bias,
        d_down_bias,
        d_gain_ffn,
        d_shift_ffn,
    ) = middle(
        o, x, g, w_rest, row(out_bias), row(up_bias), row(down_bias), row(gain_ffn), row(shift_ffn)
    )
    dout_all = swap(dout.reshape(n, local, lanes)).reshape(n, bpd, BLOCK, lanes)

    def scatter(grad):
        return lax.psum_scatter(
            grad.reshape((nb * n,) + grad.shape[2:]), both, scatter_dimension=0, tiled=True
        )[0].astype(F32)

    grad_down_all, grad_up_all = ffn_grads(act, g, h2, pre_grad, nb, n)
    grad_out_all = out_grad(att, branch, nb, n)
    grad_down = scatter(grad_down_all)
    grad_up = unstacked(scatter(grad_up_all), up_weight.shape[1])
    grad_out = scatter(grad_out_all)
    early = lax.psum(
        jnp.concatenate([d_out_bias, d_up_bias, d_down_bias, d_gain_ffn, d_shift_ffn], axis=1), both
    )[0]

    grads = attend_back(qkv_all, dout_all, lse, table, limit, per)
    grads_back = swap(grads.reshape(n, 3, local, lanes)).reshape(micros, groups, 3, local, lanes)
    grad_all, grad_qkv_all = qkv_grad(h1, grads_back, nb, n)
    grad_qkv = unstacked(scatter(grad_qkv_all), query_key_value_weight.shape[1])
    grad_x, d_gain_attn, d_shift_attn = input_grad(grad_all, w_qkv, x, row(gain_attn), dmid)
    late = lax.psum(jnp.concatenate([d_gain_attn, d_shift_attn], axis=1), both)[0]

    ends = [width, width + up_bias.shape[0]]
    ends += [ends[1] + width, ends[1] + 2 * width]
    s_out_bias, s_up_bias, s_down_bias, s_gain_ffn, s_shift_ffn = jnp.split(early, ends)
    return (
        result.reshape(tokens.shape),
        grad_x.reshape(tokens.shape),
        grad_qkv,
        grad_out,
        grad_up,
        grad_down,
        s_out_bias,
        s_up_bias,
        s_down_bias,
        late[:width],
        late[width:],
        s_gain_ffn,
        s_shift_ffn,
    )


def solution(mesh):
    rows = P(None, "batch", "seq", None)
    weight = P("seq", "batch")
    return jax.shard_map(
        body,
        mesh=mesh,
        in_specs=(rows, rows, P(None, "batch"), P(None, "batch", None, None, None))
        + (weight,) * 4
        + (P(),) * 7,
        out_specs=(rows, rows) + (weight,) * 4 + (P(),) * 7,
        check_vma=False,
    )
```

```python
import functools

import jax
import jax.numpy as jnp
from jax import lax
from jax.experimental import pallas as pl
from jax.experimental.pallas import tpu as pltpu
from jax.sharding import PartitionSpec as P

H = 16
HD = 64
BLOCK = 64
NGLOB = 2
NRAND = 3

EPS = 1e-05
BIG = 1e30
SCALE = HD ** (-0.5)
GELU_C = 0.7978845608028654
GELU_A = 0.044715
BF = jnp.bfloat16
F32 = jnp.float32
VMEM_LIMIT = 56 * 1024 * 1024

WHOLE = pl.BlockSpec(memory_space=pltpu.VMEM)
SMEM = pl.BlockSpec(memory_space=pltpu.SMEM)


def nn(a, b):
    return lax.dot_general(a, b, (((1,), (0,)), ((), ())), preferred_element_type=F32)


def nt(a, b):
    return lax.dot_general(a, b, (((1,), (1,)), ((), ())), preferred_element_type=F32)


def tn(a, b):
    return lax.dot_general(a, b, (((0,), (0,)), ((), ())), preferred_element_type=F32)


def params():
    return pltpu.CompilerParams(vmem_limit_bytes=VMEM_LIMIT)


def cost(flops, nbytes, trans=0):
    return pl.CostEstimate(flops=int(flops), bytes_accessed=int(nbytes), transcendentals=int(trans))


def constant(shape):
    return pl.BlockSpec(shape, lambda i: (0,) * len(shape))


def norm_stats(value):
    centre = jnp.mean(value, axis=-1, keepdims=True)
    centered = value - centre
    spread = jnp.mean(centered * centered, axis=-1, keepdims=True)
    rstd = lax.rsqrt(spread + EPS)
    return centered * rstd, rstd


def load_pieces(refs, wa_ref, wb_ref, sems):
    half = wa_ref.shape[1] // 2
    copies = []
    for i, ref in enumerate(refs):
        target = (wa_ref, wb_ref)[i % 4 // 2].at[i // 4, pl.ds(i % 2 * half, half)]
        copies.append(pltpu.make_async_copy(ref, target, sems.at[i]))
    for copy in copies:
        copy.start()
    for copy in copies:
        copy.wait()


def qkv_block(core, part, place_ref, wa_ref, wb_ref):
    n = wa_ref.shape[1]
    rows = []
    for s in range(n):
        rows.append(wa_ref[core, place_ref[s], part])
        rows.append(wb_ref[core, place_ref[n + s], part])
    return jnp.concatenate(rows, axis=0)


def piece_scratch(pieces, nb):
    half = pieces[0].shape
    full = (nb, 2 * half[0]) + half[1:]
    return [pltpu.VMEM(full, BF), pltpu.VMEM(full, BF), pltpu.SemaphoreType.DMA((len(pieces),))]


def project_kernel(place_ref, x_ref, gain_ref, shift_ref, *refs, micros, local, lanes):
    *pieces, qkv_ref, h_ref, wa_ref, wb_ref, sems = refs
    fb = wa_ref.shape[4]

    @pl.when(pl.program_id(0) == 0)
    def _():
        xhat, _ = norm_stats(x_ref[...].astype(F32))
        h_ref[...] = (xhat * gain_ref[...] + shift_ref[...]).astype(BF)
        load_pieces(pieces, wa_ref, wb_ref, sems)

    core = (pl.program_id(0) // 3) ^ place_ref[2 * wa_ref.shape[1]]
    y = nn(h_ref[...], qkv_block(core, pl.program_id(0) % 3, place_ref, wa_ref, wb_ref)).astype(BF)
    for m in range(micros):
        for i in range(fb // lanes):
            qkv_ref[m, i, 0] = y[m * local : (m + 1) * local, i * lanes : (i + 1) * lanes]


def project(place, x, gain, shift, pieces, micros, local, lanes):
    nb = len(pieces) // 4
    fb = pieces[0].shape[-1]
    rows, width = x.shape
    groups = width // lanes
    kernel = functools.partial(project_kernel, micros=micros, local=local, lanes=lanes)
    return pl.pallas_call(
        kernel,
        grid=(3 * nb,),
        in_specs=[SMEM, constant((rows, width)), constant((1, width)), constant((1, width))]
        + [pl.BlockSpec(memory_space=pl.ANY)] * len(pieces),
        out_specs=[
            pl.BlockSpec((micros, fb // lanes, 1, local, lanes), lambda g: (0, g % nb, g // nb, 0, 0)),
            constant((rows, width)),
        ],
        out_shape=[
            jax.ShapeDtypeStruct((micros, groups, 3, local, lanes), BF),
            jax.ShapeDtypeStruct((rows, width), BF),
        ],
        scratch_shapes=piece_scratch(pieces, nb),
        compiler_params=params(),
        cost_estimate=cost(6 * rows * width * width, 14 * width * width),
        name="project",
    )(place, x, gain, shift, *pieces)


def lane_item(shape):
    return lax.broadcasted_iota(jnp.int32, shape, len(shape) - 1) // HD


def block_diagonal(value, per):
    if per == 1:
        return value
    item = lane_item(value.shape)
    zero = jnp.zeros_like(value)
    return jnp.concatenate([jnp.where(item == i, value, zero) for i in range(per)], axis=0)


def take_diagonal(full, per):
    if per == 1:
        return full
    item = lane_item((BLOCK, full.shape[1]))
    out = full[:BLOCK]
    for i in range(1, per):
        out = jnp.where(item == i, full[i * BLOCK : (i + 1) * BLOCK], out)
    return out


def pick(ref, part, blocks, bpd):
    out = ref[blocks[0] // bpd, part, blocks[0] % bpd]
    item = lane_item(out.shape)
    for i in range(1, len(blocks)):
        out = jnp.where(item == i, ref[blocks[i] // bpd, part, blocks[i] % bpd], out)
    return out


def key_lists(b, table_ref, limit, nblk, per):
    shared = [0, 1, b - 1, b, jnp.minimum(b + 1, nblk - 1)]
    lists = [[s] for s in shared]
    biases = [
        None,
        None,
        jnp.where((b - 1) * BLOCK < limit, 0.0, -BIG),
        jnp.where(b * BLOCK < limit, 0.0, -BIG),
        jnp.where(((b + 1) * BLOCK < limit) & (b + 1 < nblk), 0.0, -BIG),
    ]
    item = lane_item((1, per * HD))
    for r in range(NRAND):
        blocks = [table_ref[b * per * NRAND + i * NRAND + r] for i in range(per)]
        bias = jnp.where(blocks[0] * BLOCK < limit, 0.0, -BIG)
        for i in range(1, per):
            bias = jnp.where(item == i, jnp.where(blocks[i] * BLOCK < limit, 0.0, -BIG), bias)
        lists.append(blocks)
        biases.append(bias)
    return lists, biases


def masked_scores(keys, queries, biases):
    s = nt(keys, queries)
    parts = []
    for i, bias in enumerate(biases):
        part = s[i * BLOCK : (i + 1) * BLOCK]
        parts.append(part if bias is None else part + bias)
    return jnp.concatenate(parts, axis=0)


def global_keys(ref, part, c, bpd, chunk):
    span = chunk // (bpd * BLOCK)
    return ref[pl.ds(c * span, span), part].reshape(chunk, ref.shape[4])


def attend_kernel(table_ref, limit_ref, qkv_ref, out_ref, lse_ref, s_ref, *, per, bpd, nblk):
    limit = limit_ref[0]
    lanes = per * HD
    chunk = 2 * bpd * BLOCK
    chunks = nblk * BLOCK // chunk

    def query(b):
        q = qkv_ref[b // bpd, 0, b % bpd] * jnp.asarray(SCALE, BF)
        return block_diagonal(q, per)

    both = jnp.concatenate([query(g) for g in range(NGLOB)], axis=0)
    rowid = lax.broadcasted_iota(jnp.int32, (chunk, NGLOB * lanes), 0)

    def score(c, top):
        s = nt(global_keys(qkv_ref, 1, c, bpd, chunk), both)
        s = jnp.where(c * chunk + rowid < limit, s, -BIG)
        s_ref[pl.ds(c * chunk, chunk), :] = s
        return jnp.maximum(top, jnp.max(s, axis=0, keepdims=True))

    top = lax.fori_loop(0, chunks, score, jnp.full((1, NGLOB * lanes), -BIG, F32))

    def total(c, sums):
        p = jnp.exp(s_ref[pl.ds(c * chunk, chunk), :] - top)
        s_ref[pl.ds(c * chunk, chunk), :] = p
        return sums + jnp.sum(p, axis=0, keepdims=True)

    sums = lax.fori_loop(0, chunks, total, jnp.zeros((1, NGLOB * lanes), F32))
    inv = 1.0 / sums
    lse = top + jnp.log(sums)
    for g in range(NGLOB):
        lse_ref[pl.ds(g, 1), :] = lse[:, g * lanes : (g + 1) * lanes]

    def mix(c, acc):
        w = (s_ref[pl.ds(c * chunk, chunk), :] * inv).astype(BF)
        return acc + tn(w, global_keys(qkv_ref, 2, c, bpd, chunk))

    acc = lax.fori_loop(0, chunks, mix, jnp.zeros((NGLOB * lanes, lanes), F32))
    for g in range(NGLOB):
        out_ref[g // bpd, g % bpd] = take_diagonal(acc[g * lanes : (g + 1) * lanes], per).astype(BF)

    def sparse(b, carry):
        lists, biases = key_lists(b, table_ref, limit, nblk, per)
        keys = jnp.concatenate([pick(qkv_ref, 1, blocks, bpd) for blocks in lists], axis=0)
        values = jnp.concatenate([pick(qkv_ref, 2, blocks, bpd) for blocks in lists], axis=0)
        s = masked_scores(keys, query(b), biases)
        top = jnp.max(s, axis=0, keepdims=True)
        p = jnp.exp(s - top)
        sums = jnp.sum(p, axis=0, keepdims=True)
        w = (p * (1.0 / sums)).astype(BF)
        lse_ref[pl.ds(b, 1), :] = top + jnp.log(sums)
        out_ref[b // bpd, b % bpd] = take_diagonal(tn(w, values), per).astype(BF)
        return carry

    lax.fori_loop(NGLOB, nblk, sparse, 0, unroll=2)


def attend(qkv, table, limit, per):
    n, _, bpd, _, lanes = qkv.shape
    nblk = n * bpd
    kernel = functools.partial(attend_kernel, per=per, bpd=bpd, nblk=nblk)
    return pl.pallas_call(
        kernel,
        in_specs=[SMEM, SMEM, WHOLE],
        out_specs=[WHOLE, WHOLE],
        out_shape=[
            jax.ShapeDtypeStruct((n, bpd, BLOCK, lanes), BF),
            jax.ShapeDtypeStruct((nblk, lanes), F32),
        ],
        scratch_shapes=[pltpu.VMEM((nblk * BLOCK, NGLOB * lanes), F32)],
        compiler_params=params(),
        cost_estimate=cost(40e9, 4e6, 1e7),
        name="attend",
    )(table, limit, qkv)


def attend_back_kernel(
    table_ref, limit_ref, qkv_ref, dout_ref, lse_ref, grad_ref, dk_ref, dv_ref, w_ref, dw_ref, *, per, bpd, nblk
):
    limit = limit_ref[0]
    lanes = per * HD
    chunk = 2 * bpd * BLOCK
    span = 2
    chunks = nblk * BLOCK // chunk
    scale_low = jnp.asarray(SCALE, BF)

    def query(b):
        return block_diagonal(qkv_ref[b // bpd, 0, b % bpd] * scale_low, per)

    def upstream(b):
        return block_diagonal(dout_ref[b // bpd, b % bpd], per)

    both = jnp.concatenate([query(g) for g in range(NGLOB)], axis=0)
    dboth = jnp.concatenate([upstream(g) for g in range(NGLOB)], axis=0)
    lse = jnp.concatenate([lse_ref[pl.ds(g, 1), :] for g in range(NGLOB)], axis=1)
    rowid = lax.broadcasted_iota(jnp.int32, (chunk, NGLOB * lanes), 0)

    def first(c, centre):
        s = nt(global_keys(qkv_ref, 1, c, bpd, chunk), both)
        s = jnp.where(c * chunk + rowid < limit, s, -BIG)
        w = jnp.exp(s - lse)
        dw = nt(global_keys(qkv_ref, 2, c, bpd, chunk), dboth)
        w_ref[pl.ds(c * chunk, chunk), :] = w
        dw_ref[pl.ds(c * chunk, chunk), :] = dw
        return centre + jnp.sum(w * dw, axis=0, keepdims=True)

    centre = lax.fori_loop(0, chunks, first, jnp.zeros((1, NGLOB * lanes), F32))

    def second(c, acc):
        w = w_ref[pl.ds(c * chunk, chunk), :]
        ds = (w * (dw_ref[pl.ds(c * chunk, chunk), :] - centre)).astype(BF)
        dk_ref[pl.ds(c * span, span)] = nn(ds, both).reshape(span, bpd, BLOCK, lanes)
        dv_ref[pl.ds(c * span, span)] = nn(w.astype(BF), dboth).reshape(span, bpd, BLOCK, lanes)
        return acc + tn(ds, global_keys(qkv_ref, 1, c, bpd, chunk))

    acc = lax.fori_loop(0, chunks, second, jnp.zeros((NGLOB * lanes, lanes), F32))
    for g in range(NGLOB):
        dq = take_diagonal(acc[g * lanes : (g + 1) * lanes], per) * SCALE
        grad_ref[g // bpd, 0, g % bpd] = dq.astype(BF)

    def sparse(b, carry):
        lists, biases = key_lists(b, table_ref, limit, nblk, per)
        keys = jnp.concatenate([pick(qkv_ref, 1, blocks, bpd) for blocks in lists], axis=0)
        values = jnp.concatenate([pick(qkv_ref, 2, blocks, bpd) for blocks in lists], axis=0)
        q = query(b)
        do = upstream(b)
        s = masked_scores(keys, q, biases)
        w = jnp.exp(s - lse_ref[pl.ds(b, 1), :])
        dw = nt(values, do)
        centre = jnp.sum(w * dw, axis=0, keepdims=True)
        ds = (w * (dw - centre)).astype(BF)
        grad_ref[b // bpd, 0, b % bpd] = (take_diagonal(tn(ds, keys), per) * SCALE).astype(BF)
        dk = nn(ds, q)
        dv = nn(w.astype(BF), do)
        item = lane_item((BLOCK, lanes))
        for ref, full in ((dk_ref, dk), (dv_ref, dv)):
            for k, blocks in enumerate(lists):
                part = full[k * BLOCK : (k + 1) * BLOCK]
                for i, block in enumerate(blocks):
                    term = part if len(blocks) == 1 else jnp.where(item == i, part, 0.0)
                    ref[block // bpd, block % bpd] += term
        return carry

    lax.fori_loop(NGLOB, nblk, sparse, 0, unroll=2)

    def finish(c, carry):
        grad_ref[c, 1] = dk_ref[c].astype(BF)
        grad_ref[c, 2] = dv_ref[c].astype(BF)
        return carry

    lax.fori_loop(0, nblk // bpd, finish, 0)


def attend_back(qkv, dout, lse, table, limit, per):
    n, _, bpd, _, lanes = qkv.shape
    nblk = n * bpd
    kernel = functools.partial(attend_back_kernel, per=per, bpd=bpd, nblk=nblk)
    return pl.pallas_call(
        kernel,
        in_specs=[SMEM, SMEM, WHOLE, WHOLE, WHOLE],
        out_specs=WHOLE,
        out_shape=jax.ShapeDtypeStruct((n, 3, bpd, BLOCK, lanes), BF),
        scratch_shapes=[
            pltpu.VMEM((n, bpd, BLOCK, lanes), F32),
            pltpu.VMEM((n, bpd, BLOCK, lanes), F32),
            pltpu.VMEM((nblk * BLOCK, NGLOB * lanes), F32),
            pltpu.VMEM((nblk * BLOCK, NGLOB * lanes), F32),
        ],
        compiler_params=params(),
        cost_estimate=cost(80e9, 8e6, 1e7),
        name="attend_back",
    )(table, limit, qkv, dout, lse)


MIDDLE_REFS = 16


def middle_kernel(
    place_ref,
    o_ref,
    x_ref,
    g_ref,
    out_bias_ref,
    up_bias_ref,
    down_bias_ref,
    gain_ref,
    shift_ref,
    *refs,
    local,
    lanes,
):
    *pieces, wa_ref, wb_ref, sems = refs
    count = len(pieces) - MIDDLE_REFS
    pieces, others = pieces[:count], pieces[count:]
    (
    result_ref,
    dmid_ref,
    branch_ref,
    dout_ref,
    att_ref,
    h_ref,
    act_ref,
    pre_grad_ref,
    d_out_bias_ref,
    d_up_bias_ref,
    d_down_bias_ref,
    d_gain_ref,
    d_shift_ref,
    mid_ref,
    acc_ref,
    dh_ref,
    ) = others
    step = pl.program_id(0)
    micros, groups = o_ref.shape[:2]
    nb, n, _, fb = wa_ref.shape
    width = x_ref.shape[1]
    kr = width // n
    kh = kr // 2
    fr = wa_ref.shape[2] - kh
    nd = fb // fr
    me_core = place_ref[2 * n]
    per_b = pl.num_programs(0) // nb

    def out_block(b):
        rows = []
        for s in range(n):
            rows.append(wa_ref[b ^ me_core, place_ref[s], fr : fr + kh])
            rows.append(wb_ref[b ^ me_core, place_ref[n + s], fr : fr + kh])
        return jnp.concatenate(rows, axis=0)

    def down_block(b):
        rows = [wa_ref[b ^ me_core, place_ref[step * nd + h], :fr] for h in range(nd)]
        return jnp.concatenate(rows, axis=0)

    def up_block():
        core = (step // per_b) ^ me_core
        at = pl.ds(pl.multiple_of(step % per_b * kr, kr), kr)
        return jnp.concatenate([wb_ref[core, place_ref[n + s], at] for s in range(n)], axis=0)

    @pl.when(step == 0)
    def _():
        load_pieces(pieces, wa_ref, wb_ref, sems)
        for m in range(micros):
            for i in range(groups):
                att_ref[m * local : (m + 1) * local, i * lanes : (i + 1) * lanes] = o_ref[m, i]
        att = att_ref[...]
        for b in range(nb):
            cols = slice(b * fb, (b + 1) * fb)
            y = nn(att, out_block(b))
            mid_ref[:, cols] = x_ref[:, cols].astype(F32) + y + out_bias_ref[:, cols]
        mid = mid_ref[...]
        xhat, _ = norm_stats(mid)
        h_ref[...] = (xhat * gain_ref[...] + shift_ref[...]).astype(BF)
        acc_ref[...] = mid + down_bias_ref[...]
        dh_ref[...] = jnp.zeros_like(dh_ref)
        d_down_bias_ref[...] = jnp.sum(g_ref[...].astype(F32), axis=0, keepdims=True)

    up = up_block()
    pre = nn(h_ref[...], up) + up_bias_ref[...]
    square = pre * pre
    gate = jnp.tanh(GELU_C * pre * (1.0 + GELU_A * square))
    half = 0.5 * (1.0 + gate)
    act = (pre * half).astype(BF)
    slope = half + 0.5 * pre * (1.0 - gate * gate) * (GELU_C * (1.0 + 3.0 * GELU_A * square))
    act_ref[...] = act
    dact = None
    for b in range(nb):
        cols = slice(b * fb, (b + 1) * fb)
        term = nt(g_ref[:, cols], down_block(b))
        dact = term if dact is None else dact + term
    pre_grad = (dact * slope).astype(BF)
    pre_grad_ref[0] = pre_grad
    d_up_bias_ref[...] = jnp.sum(pre_grad.astype(F32), axis=0, keepdims=True)
    for b in range(nb):
        cols = slice(b * fb, (b + 1) * fb)
        acc_ref[:, cols] += nn(act, down_block(b))
    dh_ref[...] += nt(pre_grad, up)

    @pl.when(step == pl.num_programs(0) - 1)
    def _():
        result_ref[...] = acc_ref[...].astype(BF)
        dh = dh_ref[...]
        xhat, rstd = norm_stats(mid_ref[...])
        d_gain_ref[...] = jnp.sum(dh * xhat, axis=0, keepdims=True)
        d_shift_ref[...] = jnp.sum(dh, axis=0, keepdims=True)
        d = dh * gain_ref[...]
        inner = d - jnp.mean(d, axis=-1, keepdims=True) - xhat * jnp.mean(d * xhat, axis=-1, keepdims=True)
        dmid = g_ref[...].astype(F32) + rstd * inner
        dmid_ref[...] = dmid
        branch = dmid.astype(BF)
        branch_ref[...] = branch
        d_out_bias_ref[...] = jnp.sum(branch.astype(F32), axis=0, keepdims=True)
        dout = None
        for b in range(nb):
            term = nt(branch[:, b * fb : (b + 1) * fb], out_block(b))
            dout = term if dout is None else dout + term
        dout = dout.astype(BF)
        for m in range(micros):
            for i in range(groups):
                dout_ref[m, i] = dout[m * local : (m + 1) * local, i * lanes : (i + 1) * lanes]


def middle(place, o, x, g, pieces, out_bias, up_bias, down_bias, gain, shift):
    micros, groups, local, lanes = o.shape
    rows, width = x.shape
    nb = len(pieces) // 4
    fb = pieces[0].shape[-1]
    hidden = up_bias.shape[1]
    steps = hidden // fb
    n = 2 * pieces[0].shape[0]
    per_b = steps // nb
    full = lambda dtype: jax.ShapeDtypeStruct((rows, width), dtype)
    vector = jax.ShapeDtypeStruct((1, width), F32)
    whole = lambda shape: pl.BlockSpec(shape, lambda i, place: (0,) * len(shape))
    kernel = functools.partial(middle_kernel, local=local, lanes=lanes)
    return pl.pallas_call(
        kernel,
        grid_spec=pltpu.PrefetchScalarGridSpec(
        num_scalar_prefetch=1,
        grid=(steps,),
        in_specs=[
            whole((micros, groups, local, lanes)),
            whole((rows, width)),
            whole((rows, width)),
            whole((1, width)),
            pl.BlockSpec((1, fb), lambda i, place: (0, i)),
            whole((1, width)),
            whole((1, width)),
            whole((1, width)),
        ]
        + [pl.BlockSpec(memory_space=pl.ANY)] * len(pieces),
        out_specs=[
            whole((rows, width)),
            whole((rows, width)),
            whole((rows, width)),
            whole((micros, groups, local, lanes)),
            whole((rows, width)),
            whole((rows, width)),
            pl.BlockSpec((rows, fb), lambda i, place: (0, i)),
            pl.BlockSpec((1, rows, fb), lambda i, place: ((i // per_b) ^ place[2 * n], 0, i % per_b)),
            whole((1, width)),
            pl.BlockSpec((1, fb), lambda i, place: (0, i)),
            whole((1, width)),
            whole((1, width)),
            whole((1, width)),
        ],
    scratch_shapes=[pltpu.VMEM((rows, width), F32)] * 3 + piece_scratch(pieces, nb),
        ),
        out_shape=[
            full(BF),
            full(F32),
            full(BF),
            jax.ShapeDtypeStruct((micros, groups, local, lanes), BF),
            full(BF),
            full(BF),
            jax.ShapeDtypeStruct((rows, hidden), BF),
            jax.ShapeDtypeStruct((nb, rows, hidden // nb), BF),
            vector,
            jax.ShapeDtypeStruct((1, hidden), F32),
            vector,
            vector,
            vector,
        ],
        compiler_params=params(),
        cost_estimate=cost(8 * rows * width * hidden + 4 * rows * width * width, 50e6),
        name="middle",
    )(place, o, x, g, out_bias, up_bias, down_bias, gain, shift, *pieces)


def relative_transpose(ref, target_ref, k, me, n):
    kr = target_ref.shape[1] // n
    value = ref[...].T
    for s in range(n):
        at = pl.ds(pl.multiple_of((s ^ me) * kr, kr), kr)
        target_ref[k, at, :] = value[s * kr : (s + 1) * kr]


def ffn_grads_kernel(place_ref, *refs, nb, n):
    groups = [refs[i * nb : (i + 1) * nb] for i in range(6)]
    act_refs, gc_refs, h_refs, gp_refs, att_refs, br_refs = groups
    a_send_ref, a_keep_ref, b_send_ref, b_keep_ref, ht_ref, at_ref, out_ref = refs[6 * nb :]
    step = pl.program_id(0)
    me = place_ref[2 * n + 1]
    first = n // 8
    rows_a, fb = a_send_ref.shape[1:]
    kr = ht_ref.shape[1] // n
    kh = kr // 2
    fr = rows_a - kh
    per_b = fr // kr

    @pl.when(step == 0)
    def _():
        total = None
        for k in range(nb):
            relative_transpose(h_refs[k], ht_ref, k, me, n)
            relative_transpose(att_refs[k], at_ref, k, me, n)
        for k in range(nb):
            term = nn(at_ref[k], br_refs[k][...])
            total = term if total is None else total + term
        out_ref[...] = total.astype(BF).reshape(out_ref.shape)

    send = step < 4
    z = step % 4
    down = None
    for k in range(nb):
        term = nn(act_refs[k][...].T, gc_refs[k][...])
        down = term if down is None else down + term
    down = down.astype(BF).reshape(first, fr, fb)
    base_a = (2 * z + send.astype(jnp.int32)) * first

    def put_a(ref):
        for i in range(first):
            place = i ^ (me % first)
            ref[place, :fr] = down[i]
        for i in range(first):
            ref[i, fr:] = out_ref[base_a + i, :kh]

    pl.when(send)(lambda: put_a(a_send_ref))
    pl.when(jnp.logical_not(send))(lambda: put_a(a_keep_ref))

    def put_b(ref, offset):
        firsts = [pl.multiple_of(((2 * (step % 4 // 2) + i // first) * 2 * first + 2 * (i % first) + offset) * kr, kr) for i in range(2 * first)]
        up = None
        for k in range(nb):
            rows = jnp.concatenate([ht_ref[k, pl.ds(at, kr), :] for at in firsts], axis=0)
            term = nn(rows, gp_refs[k][0])
            up = term if up is None else up + term
        up = up.astype(BF).reshape(2 * first, kr, per_b * fb)
        for i in range(2 * first):
            for q in range(per_b):
                ref[i, q * kr : (q + 1) * kr] = up[i, :, q * fb : (q + 1) * fb]
            ref[i, fr:] = out_ref[firsts[i] // kr, kh:]

    even = step % 2 == 0
    pl.when(even & send)(lambda: put_b(b_send_ref, 1))
    pl.when(even & jnp.logical_not(send))(lambda: put_b(b_keep_ref, 0))


def ffn_grads(place, act, gc, h, gp, att, br, n):
    nb = len(act)
    rows, hidden = act[0].shape
    fb = gc[0].shape[1]
    width = h[0].shape[1]
    first = n // 8
    fr = hidden // n
    kr = width // n
    rows_a = fr + kr // 2
    half = jax.ShapeDtypeStruct((n // 2, rows_a, fb), BF)
    whole = lambda shape: pl.BlockSpec(shape, lambda i, place: (0,) * len(shape))
    act_spec = pl.BlockSpec(
        (rows, first * fr), lambda i, place: (0, (2 * (i % 4) + 1 - i // 4) ^ (place[2 * n + 1] // first))
    )
    return pl.pallas_call(
        functools.partial(ffn_grads_kernel, nb=nb, n=n),
        grid_spec=pltpu.PrefetchScalarGridSpec(
            num_scalar_prefetch=1,
            grid=(8,),
            in_specs=[act_spec] * nb
            + [whole((rows, fb))] * nb
            + [whole((rows, width))] * nb
            + [whole((1, rows, hidden // nb))] * nb
            + [whole((rows, width))] * nb
            + [whole((rows, fb))] * nb,
            out_specs=[
                pl.BlockSpec((first, rows_a, fb), lambda i, place: (jnp.minimum(i, 3), 0, 0)),
                pl.BlockSpec((first, rows_a, fb), lambda i, place: (jnp.maximum(i - 4, 0), 0, 0)),
                pl.BlockSpec((2 * first, rows_a, fb), lambda i, place: (jnp.minimum(i, 3) // 2, 0, 0)),
                pl.BlockSpec((2 * first, rows_a, fb), lambda i, place: (jnp.maximum(i - 4, 0) // 2, 0, 0)),
            ],
            scratch_shapes=[
                pltpu.VMEM((nb, width, rows), BF),
                pltpu.VMEM((nb, width, rows), BF),
                pltpu.VMEM((n, kr, fb), BF),
            ],
        ),
        out_shape=[half] * 4,
        compiler_params=params(),
        cost_estimate=cost(4 * rows * width * hidden + 2 * rows * width * width, 40e6),
        name="ffn_grads",
    )(place, *act, *gc, *h, *gp, *att, *br)


def split_kernel(place_ref, grad_ref, *out_refs, n, local, lanes):
    micros, groups = grad_ref.shape[:2]
    core = place_ref[2 * n]
    count = out_refs[0].shape[1] // lanes
    for k, out_ref in enumerate(out_refs):
        for m in range(micros):
            for i in range(count):
                at = (core ^ k) * count + i
                block = grad_ref[m, at % groups, at // groups]
                out_ref[m * local : (m + 1) * local, i * lanes : (i + 1) * lanes] = block


def split_by_core(place, grad, nb, n):
    micros, groups, _, local, lanes = grad.shape
    shape = jax.ShapeDtypeStruct((micros * local, 3 * groups * lanes // nb), BF)
    return pl.pallas_call(
        functools.partial(split_kernel, n=n, local=local, lanes=lanes),
        in_specs=[SMEM, WHOLE],
        out_specs=[WHOLE] * nb,
        out_shape=[shape] * nb,
        compiler_params=params(),
        cost_estimate=cost(1e6, 6e6),
        name="split_by_core",
    )(place, grad)


def qkv_grad_kernel(place_ref, *refs, nb, n):
    h_refs, ga_refs = refs[:nb], refs[nb : 2 * nb]
    a_send_ref, a_keep_ref, b_send_ref, b_keep_ref, ht_ref = refs[2 * nb :]
    first = n // 8
    _, _, kh, fb = a_send_ref.shape

    @pl.when(pl.program_id(0) == 0)
    def _():
        for k in range(nb):
            relative_transpose(h_refs[k], ht_ref, k, place_ref[2 * n + 1], n)

    y = None
    for k in range(nb):
        term = nn(ht_ref[k], ga_refs[k][...])
        y = term if y is None else y + term
    y = y.astype(BF).reshape(4, 2 * first, 2, kh, fb)
    for z in range(4):
        for i in range(first):
            at = z * first + i
            a_send_ref[at, 0] = y[z, first + i, 0]
            a_keep_ref[at, 0] = y[z, i, 0]
            b_send_ref[at, 0] = y[z, 2 * i + 1, 1]
            b_keep_ref[at, 0] = y[z, 2 * i, 1]


def qkv_grad(place, h, ga, n):
    nb = len(h)
    rows, width = h[0].shape
    fb = ga[0].shape[1] // 3
    kh = width // n // 2
    half = jax.ShapeDtypeStruct((n // 2, 3, kh, fb), BF)
    return pl.pallas_call(
        functools.partial(qkv_grad_kernel, nb=nb, n=n),
        grid=(3,),
        in_specs=[SMEM]
        + [constant((rows, width))] * nb
        + [pl.BlockSpec((rows, fb), lambda t: (0, t))] * nb,
        out_specs=[pl.BlockSpec((n // 2, 1, kh, fb), lambda t: (0, t, 0, 0))] * 4,
        out_shape=[half] * 4,
        scratch_shapes=[pltpu.VMEM((nb, width, rows), BF)],
        compiler_params=params(),
        cost_estimate=cost(6 * rows * width * width, 15e6),
        name="qkv_grad",
    )(place, *h, *ga)


def input_grad_kernel(place_ref, x_ref, gain_ref, dmid_ref, *refs, nb):
    grad_refs = refs[:nb]
    *pieces, _, out_ref, d_gain_ref, d_shift_ref, dh_ref, wa_ref, wb_ref, sems = refs[nb:]
    step = pl.program_id(0)

    @pl.when(step == 0)
    def _():
        load_pieces(pieces, wa_ref, wb_ref, sems)

    total = None
    for k in range(nb):
        term = nt(grad_refs[k][...], qkv_block(k, step, place_ref, wa_ref, wb_ref))
        total = term if total is None else total + term

    @pl.when(step == 0)
    def _():
        dh_ref[...] = total

    @pl.when(step > 0)
    def _():
        dh_ref[...] += total

    @pl.when(step == pl.num_programs(0) - 1)
    def _():
        dh = dh_ref[...]
        xhat, rstd = norm_stats(x_ref[...].astype(F32))
        d_gain_ref[...] = jnp.sum(dh * xhat, axis=0, keepdims=True)
        d_shift_ref[...] = jnp.sum(dh, axis=0, keepdims=True)
        d = dh * gain_ref[...]
        inner = d - jnp.mean(d, axis=-1, keepdims=True) - xhat * jnp.mean(d * xhat, axis=-1, keepdims=True)
        out_ref[...] = dmid_ref[...] + rstd * inner


def input_grad(place, grads, pieces, x, gain, dmid, earlier):
    rows, width = x.shape
    nb = len(grads)
    fb = pieces[0].shape[-1]
    vector = jax.ShapeDtypeStruct((1, width), F32)
    return pl.pallas_call(
        functools.partial(input_grad_kernel, nb=nb),
        grid=(3,),
        in_specs=[SMEM, constant((rows, width)), constant((1, width)), constant((rows, width))]
        + [pl.BlockSpec((rows, fb), lambda t: (0, t))] * nb
        + [pl.BlockSpec(memory_space=pl.ANY)] * (len(pieces) + 1),
        out_specs=[constant((rows, width)), constant((1, width)), constant((1, width))],
        out_shape=[jax.ShapeDtypeStruct((rows, width), F32), vector, vector],
        scratch_shapes=[pltpu.VMEM((rows, width), F32)] + piece_scratch(pieces, nb),
        compiler_params=params(),
        cost_estimate=cost(6 * rows * width * width, 20e6),
        name="input_grad",
    )(place, x, gain, dmid, *grads, *pieces, earlier)


def swap_with(value, axis, k):
    size = lax.axis_size(axis)
    return lax.ppermute(value, axis, [(i, i ^ k) for i in range(size)])


def low_bits(n):
    return [1 << i for i in range((n // 4).bit_length() - 1)]


def direct(shard, n):
    return [swap_with(shard, "seq", k * n // 4) for k in range(1, 4)]


def move(value, step, n):
    quarter = n // 4
    if step > 0:
        return lax.ppermute(value, "seq", [(i, i + quarter) for i in range(n - quarter)])
    return lax.ppermute(value, "seq", [(i + quarter, i) for i in range(n - quarter)])


def line_gather(shard, n):
    up, down = [shard], [shard]
    for _ in range(3):
        up.append(move(up[-1], 1, n))
        down.append(move(down[-1], -1, n))
    return up[1:], down[1:]


def line_halves(shard, up, down, position, n):
    z = position // (n // 4)
    by_distance = {**{-i - 1: up[i] for i in range(3)}, **{i + 1: down[i] for i in range(3)}}
    arrived = []
    for k in range(1, 4):
        found = by_distance[k]
        for at in range(1, 4):
            found = jnp.where(z == at, by_distance[(at ^ k) - at], found)
        arrived.append(found)
    return halves(shard, arrived)


def line_reduce(total, position, n):
    z = position // (n // 4)
    block = lambda to: lax.dynamic_index_in_dim(total, z ^ jnp.clip(to, 0, 3), 0, keepdims=False)
    up, down = block(z + 3), block(z - 3)
    for step in range(1, 4):
        up, down = move(up, 1, n), move(down, -1, n)
        if step < 3:
            up = plus(block(z + 3 - step), up)
            down = plus(block(z - 3 + step), down)
    return up, down


def halves(shard, arrived):
    both = jnp.stack([shard] + arrived)
    return both[:, 0], both[:, 1]


def together(*values):
    return lax.optimization_barrier(values)


def gather_rest(part, bits):
    for bit in bits[:-1]:
        part = jnp.concatenate([part, swap_with(part, "seq", bit)])
    return part


def gather_last(part, bits):
    return [part, swap_with(part, "seq", bits[-1])]


def gather_cores(pieces, nb):
    out = list(pieces)
    for k in range(1, nb):
        out += [swap_with(piece, "batch", k) for piece in pieces]
    return out


def place_of(relative, bits, n):
    place = relative // (n // 4)
    for i, bit in enumerate(bits):
        place = place + jnp.where(relative & bit, 4 << i, 0)
    return place


def place_table(position, core, n):
    relative = jnp.arange(n, dtype=jnp.int32) ^ position
    bits = low_bits(n)
    ends = jnp.stack([core, position]).astype(jnp.int32)
    return jnp.concatenate([place_of(relative, bits, n), place_of(relative, bits[::-1], n), ends])


def plus(value, arrived):
    return (value.astype(F32) + arrived.astype(F32)).astype(BF)


def reduce_first(a_send, b_send, n):
    return swap_with(a_send, "seq", n // 8), swap_with(b_send, "seq", 1)


def split_next(total):
    m = total.shape[1] // 2
    return total[:, :m], total[:, m:]


def reduce_steps(total, bit_of, n):
    total = total.reshape((4, n // 8) + total.shape[1:])
    while total.shape[1] > 1:
        keep, send = split_next(total)
        total = plus(keep, swap_with(send, "seq", bit_of(send.shape[1])))
    return total[:, 0]


def reduce_rest(a, b, n):
    a = reduce_steps(a, lambda m: m, n)
    b = reduce_steps(b, lambda m: 2 * m, n)
    return jnp.stack([a, b], axis=1)


def reduce_direct(total, n):
    return [swap_with(total[k], "seq", k * n // 4) for k in range(1, 4)]


def reduce_last(total, arrived):
    out = total[0].astype(F32)
    for term in arrived:
        out = out + term.astype(F32)
    return out[0], out[1]


def total_over_all(value, nb, n):
    for axis, size in (("batch", nb), ("seq", n)):
        k = 1
        while k < size:
            value = value + swap_with(value, axis, k)
            k *= 2
    return value


def body(
    tokens,
    cotangent,
    lengths,
    random_blocks,
    query_key_value_weight,
    output_weight,
    up_weight,
    down_weight,
    out_bias,
    up_bias,
    down_bias,
    gain_attn,
    shift_attn,
    gain_ffn,
    shift_ffn,
):
    n = lax.axis_size("seq")
    nb = lax.axis_size("batch")
    position = lax.axis_index("seq")
    core = lax.axis_index("batch")
    micros, _, local, width = tokens.shape
    hidden = up_bias.shape[0]
    nblk = n * local // BLOCK
    bpd = local // BLOCK
    per = micros * H // n
    lanes = per * HD
    groups = H // per
    fb = width // nb
    kr = width // n
    kh = kr // 2
    fr = hidden // n
    per_b = hidden // width
    bits = low_bits(n)
    row = lambda v: v.reshape(1, -1)
    place = place_table(position, core, n)

    shard = query_key_value_weight.reshape(2, kh, 3, fb).transpose(0, 2, 1, 3)
    part_a, part_b = halves(shard, direct(shard, n))
    stacked_up = up_weight.reshape(kr, per_b, fb).transpose(1, 0, 2).reshape(per_b * kr, fb)
    rest = jnp.stack(
        [
            jnp.concatenate([down_weight, output_weight[:kh]]),
            jnp.concatenate([stacked_up, output_weight[kh:]]),
        ]
    )
    part_a, rest = together(part_a, rest)
    rest_up, rest_down = line_gather(rest, n)
    part_a = gather_rest(part_a, bits)
    part_b = gather_rest(part_b, bits[::-1])
    qkv_pieces = gather_cores(gather_last(part_a, bits) + gather_last(part_b, bits[::-1]), nb)
    x = tokens.reshape(micros * local, width)
    g = cotangent.reshape(micros * local, width)
    micro = position * per // H
    head = position * per % H
    table = lax.dynamic_slice(
        random_blocks[:, 0], (micro, 0, head, 0), (1, nblk, per, NRAND)
    ).reshape(-1)
    limit = lax.dynamic_slice(lengths[:, 0], (micro,), (1,))

    def swap(value):
        return lax.all_to_all(value, "seq", split_axis=0, concat_axis=0, tiled=True)

    def over_cores(value):
        return [value] + [swap_with(value, "batch", k) for k in range(1, nb)]

    def columns_over_cores(value, cols):
        mine = lambda c: lax.dynamic_slice_in_dim(value, c * cols, cols, axis=1)
        return [mine(core)] + [swap_with(mine(core ^ k), "batch", k) for k in range(1, nb)]

    qkv, h1 = project(place, x, row(gain_attn), row(shift_attn), qkv_pieces, micros, local, lanes)
    qkv, rest_up[2], rest_down[2] = together(qkv, rest_up[2], rest_down[2])
    rest_a, rest_b = line_halves(rest, rest_up, rest_down, position, n)
    qkv_all = swap(qkv.reshape(n, 3, local, lanes)).reshape(n, 3, bpd, BLOCK, lanes)
    rest_a = gather_rest(rest_a, bits)
    rest_b = gather_rest(rest_b, bits[::-1])
    qkv_all, rest_a, rest_b = together(qkv_all, rest_a, rest_b)
    rest_a = gather_last(rest_a, bits)
    rest_b = gather_last(rest_b, bits[::-1])
    mixed, lse = attend(qkv_all, table, limit, per)
    mixed, rest_a[1], rest_b[1] = together(mixed, rest_a[1], rest_b[1])
    rest_pieces = gather_cores(rest_a + rest_b, nb)
    o = swap(mixed.reshape(n, local, lanes)).reshape(micros, groups, local, lanes)
    (
        result,
        dmid,
        branch,
        dout,
        att,
        h2,
        act,
        pre_grad,
        d_out_bias,
        d_up_bias,
        d_down_bias,
        d_gain_ffn,
        d_shift_ffn,
    ) = middle(
        place,
        o,
        x,
        g,
        rest_pieces,
        row(out_bias),
        row(up_bias),
        row(down_bias),
        row(gain_ffn),
        row(shift_ffn),
    )
    h1_cores = over_cores(h1)
    dout_all = swap(dout.reshape(n, local, lanes)).reshape(n, bpd, BLOCK, lanes)

    parts = ffn_grads(
        place,
        over_cores(act),
        columns_over_cores(g, fb),
        over_cores(h2),
        [pre_grad] + [swap_with(pre_grad[k : k + 1], "batch", k) for k in range(1, nb)],
        over_cores(att),
        columns_over_cores(branch, fb),
        n,
    )
    dout_all, *parts = together(dout_all, *parts)
    a_send, a_keep, b_send, b_keep = parts
    first_a, first_b = reduce_first(a_send, b_send, n)
    grads = attend_back(qkv_all, dout_all, lse, table, limit, per)
    grads, first_a, first_b = together(grads, first_a, first_b)
    grads_back = swap(grads.reshape(n, 3, local, lanes)).reshape(micros, groups, 3, local, lanes)
    reduced = reduce_rest(plus(a_keep, first_a), plus(b_keep, first_b), n)
    early = [d_out_bias, d_up_bias, d_down_bias, d_gain_ffn, d_shift_ffn]
    early_sums = total_over_all(jnp.concatenate(early, axis=1), nb, n)[0]
    grads_back, early_sums, reduced = together(grads_back, early_sums, reduced)

    own_grads = split_by_core(place, grads_back, nb, n)
    rest_arrived = line_reduce(reduced, position, n)

    grad_cores = [own_grads[0]] + [swap_with(own_grads[k], "batch", k) for k in range(1, nb)]
    a_send, a_keep, b_send, b_keep = qkv_grad(place, h1_cores, grad_cores, n)
    first_a, first_b = reduce_first(a_send, b_send, n)
    grad_x, d_gain_attn, d_shift_attn = input_grad(
        place, own_grads, qkv_pieces, x, row(gain_attn), dmid, a_keep
    )
    late = jnp.concatenate([d_gain_attn, d_shift_attn], axis=1)
    late, first_a, first_b = together(late, first_a, first_b)
    late = total_over_all(late, nb, n)[0]
    qkv_reduced = reduce_rest(plus(a_keep, first_a), plus(b_keep, first_b), n)
    qkv_reduced, *rest_arrived = together(qkv_reduced, *rest_arrived)
    grad_a, grad_b = reduce_last(qkv_reduced, reduce_direct(qkv_reduced, n))
    grad_qkv = jnp.stack([grad_a, grad_b]).transpose(0, 2, 1, 3).reshape(kr, 3 * fb)
    grad_a, grad_b = reduce_last(reduced, rest_arrived)
    grad_down = grad_a[:fr]
    grad_up = grad_b[:fr].reshape(per_b, kr, fb).transpose(1, 0, 2).reshape(kr, per_b * fb)
    grad_out = jnp.concatenate([grad_a[fr:], grad_b[fr:]])
    ends = [width, width + hidden, 2 * width + hidden, 3 * width + hidden]
    s_out_bias, s_up_bias, s_down_bias, s_gain_ffn, s_shift_ffn = jnp.split(early_sums, ends)
    return (
        result.reshape(tokens.shape),
        grad_x.reshape(tokens.shape),
        grad_qkv,
        grad_out,
        grad_up,
        grad_down,
        s_out_bias,
        s_up_bias,
        s_down_bias,
        late[:width],
        late[width:],
        s_gain_ffn,
        s_shift_ffn,
    )


def solution(mesh):
    rows = P(None, "batch", "seq", None)
    weight = P("seq", "batch")
    return jax.shard_map(
        body,
        mesh=mesh,
        in_specs=(rows, rows, P(None, "batch"), P(None, "batch", None, None, None))
        + (weight,) * 4
        + (P(),) * 7,
        out_specs=(rows, rows) + (weight,) * 4 + (P(),) * 7,
        check_vma=False,
    )
```

```python
import functools

import jax
import jax.numpy as jnp
from jax import lax
from jax.experimental import pallas as pl
from jax.experimental.pallas import tpu as pltpu
from jax.sharding import PartitionSpec as P

H = 16
HD = 64
BLOCK = 64
NGLOB = 2
NRAND = 3

EPS = 1e-05
BIG = 1e30
SCALE = HD ** (-0.5)
GELU_C = 0.7978845608028654
GELU_A = 0.044715
BF = jnp.bfloat16
F32 = jnp.float32
VMEM_LIMIT = 56 * 1024 * 1024

WHOLE = pl.BlockSpec(memory_space=pltpu.VMEM)
SMEM = pl.BlockSpec(memory_space=pltpu.SMEM)


def nn(a, b):
    return lax.dot_general(a, b, (((1,), (0,)), ((), ())), preferred_element_type=F32)


def nt(a, b):
    return lax.dot_general(a, b, (((1,), (1,)), ((), ())), preferred_element_type=F32)


def tn(a, b):
    return lax.dot_general(a, b, (((0,), (0,)), ((), ())), preferred_element_type=F32)


def params():
    return pltpu.CompilerParams(vmem_limit_bytes=VMEM_LIMIT)


def cost(flops, nbytes, trans=0):
    return pl.CostEstimate(flops=int(flops), bytes_accessed=int(nbytes), transcendentals=int(trans))


def constant(shape):
    return pl.BlockSpec(shape, lambda i: (0,) * len(shape))


def norm_stats(value):
    centre = jnp.mean(value, axis=-1, keepdims=True)
    centered = value - centre
    spread = jnp.mean(centered * centered, axis=-1, keepdims=True)
    rstd = lax.rsqrt(spread + EPS)
    return centered * rstd, rstd


def load_pieces(refs, wa_ref, wb_ref, sems):
    parts = len(refs) // wa_ref.shape[0]
    copies = []
    at = 0
    for i, ref in enumerate(refs):
        if i % (parts // 2) == 0:
            at = 0
        target = (wa_ref, wb_ref)[i % parts // (parts // 2)].at[i // parts, pl.ds(at, ref.shape[0])]
        at += ref.shape[0]
        copies.append(pltpu.make_async_copy(ref, target, sems.at[i]))
    for copy in copies:
        copy.start()
    for copy in copies:
        copy.wait()


def qkv_block(core, part, place_ref, wa_ref, wb_ref):
    n = wa_ref.shape[1]
    rows = []
    for s in range(n):
        rows.append(wa_ref[core, place_ref[s], part])
        rows.append(wb_ref[core, place_ref[n + s], part])
    return jnp.concatenate(rows, axis=0)


def piece_scratch(pieces, nb, n):
    full = (nb, n) + pieces[0].shape[1:]
    return [pltpu.VMEM(full, BF), pltpu.VMEM(full, BF), pltpu.SemaphoreType.DMA((len(pieces),))]


def project_kernel(place_ref, x_ref, gain_ref, shift_ref, *refs, micros, local, lanes):
    *pieces, qkv_ref, h_ref, wa_ref, wb_ref, sems = refs
    fb = wa_ref.shape[4]

    @pl.when(pl.program_id(0) == 0)
    def _():
        xhat, _ = norm_stats(x_ref[...].astype(F32))
        h_ref[...] = (xhat * gain_ref[...] + shift_ref[...]).astype(BF)
        load_pieces(pieces, wa_ref, wb_ref, sems)

    core = (pl.program_id(0) // 3) ^ place_ref[2 * wa_ref.shape[1]]
    y = nn(h_ref[...], qkv_block(core, pl.program_id(0) % 3, place_ref, wa_ref, wb_ref)).astype(BF)
    for m in range(micros):
        for i in range(fb // lanes):
            qkv_ref[m, i, 0] = y[m * local : (m + 1) * local, i * lanes : (i + 1) * lanes]


def project(place, x, gain, shift, pieces, nb, n, micros, local, lanes):
    fb = pieces[0].shape[-1]
    rows, width = x.shape
    groups = width // lanes
    kernel = functools.partial(project_kernel, micros=micros, local=local, lanes=lanes)
    return pl.pallas_call(
        kernel,
        grid=(3 * nb,),
        in_specs=[SMEM, constant((rows, width)), constant((1, width)), constant((1, width))]
        + [pl.BlockSpec(memory_space=pl.ANY)] * len(pieces),
        out_specs=[
            pl.BlockSpec((micros, fb // lanes, 1, local, lanes), lambda g: (0, g % nb, g // nb, 0, 0)),
            constant((rows, width)),
        ],
        out_shape=[
            jax.ShapeDtypeStruct((micros, groups, 3, local, lanes), BF),
            jax.ShapeDtypeStruct((rows, width), BF),
        ],
        scratch_shapes=piece_scratch(pieces, nb, n),
        compiler_params=params(),
        cost_estimate=cost(6 * rows * width * width, 14 * width * width),
        name="project",
    )(place, x, gain, shift, *pieces)


def lane_item(shape):
    return lax.broadcasted_iota(jnp.int32, shape, len(shape) - 1) // HD


def block_diagonal(value, per):
    if per == 1:
        return value
    item = lane_item(value.shape)
    zero = jnp.zeros_like(value)
    return jnp.concatenate([jnp.where(item == i, value, zero) for i in range(per)], axis=0)


def take_diagonal(full, per):
    if per == 1:
        return full
    item = lane_item((BLOCK, full.shape[1]))
    out = full[:BLOCK]
    for i in range(1, per):
        out = jnp.where(item == i, full[i * BLOCK : (i + 1) * BLOCK], out)
    return out


def pick(ref, part, blocks, bpd):
    out = ref[blocks[0] // bpd, part, blocks[0] % bpd]
    item = lane_item(out.shape)
    for i in range(1, len(blocks)):
        out = jnp.where(item == i, ref[blocks[i] // bpd, part, blocks[i] % bpd], out)
    return out


def key_lists(b, table_ref, limit, nblk, per):
    shared = [0, 1, b - 1, b, jnp.minimum(b + 1, nblk - 1)]
    lists = [[s] for s in shared]
    biases = [
        None,
        None,
        jnp.where((b - 1) * BLOCK < limit, 0.0, -BIG),
        jnp.where(b * BLOCK < limit, 0.0, -BIG),
        jnp.where(((b + 1) * BLOCK < limit) & (b + 1 < nblk), 0.0, -BIG),
    ]
    item = lane_item((1, per * HD))
    for r in range(NRAND):
        blocks = [table_ref[b * per * NRAND + i * NRAND + r] for i in range(per)]
        bias = jnp.where(blocks[0] * BLOCK < limit, 0.0, -BIG)
        for i in range(1, per):
            bias = jnp.where(item == i, jnp.where(blocks[i] * BLOCK < limit, 0.0, -BIG), bias)
        lists.append(blocks)
        biases.append(bias)
    return lists, biases


def masked_scores(keys, queries, biases):
    s = nt(keys, queries)
    parts = []
    for i, bias in enumerate(biases):
        part = s[i * BLOCK : (i + 1) * BLOCK]
        parts.append(part if bias is None else part + bias)
    return jnp.concatenate(parts, axis=0)


def global_keys(ref, part, c, bpd, chunk):
    span = chunk // (bpd * BLOCK)
    return ref[pl.ds(c * span, span), part].reshape(chunk, ref.shape[4])


def attend_kernel(table_ref, limit_ref, qkv_ref, out_ref, lse_ref, s_ref, *, per, bpd, nblk):
    limit = limit_ref[0]
    lanes = per * HD
    chunk = 2 * bpd * BLOCK
    chunks = nblk * BLOCK // chunk

    def query(b):
        q = qkv_ref[b // bpd, 0, b % bpd] * jnp.asarray(SCALE, BF)
        return block_diagonal(q, per)

    both = jnp.concatenate([query(g) for g in range(NGLOB)], axis=0)
    rowid = lax.broadcasted_iota(jnp.int32, (chunk, NGLOB * lanes), 0)

    def score(c, top):
        s = nt(global_keys(qkv_ref, 1, c, bpd, chunk), both)
        s = jnp.where(c * chunk + rowid < limit, s, -BIG)
        s_ref[pl.ds(c * chunk, chunk), :] = s
        return jnp.maximum(top, jnp.max(s, axis=0, keepdims=True))

    top = lax.fori_loop(0, chunks, score, jnp.full((1, NGLOB * lanes), -BIG, F32))

    def total(c, sums):
        p = jnp.exp(s_ref[pl.ds(c * chunk, chunk), :] - top)
        s_ref[pl.ds(c * chunk, chunk), :] = p
        return sums + jnp.sum(p, axis=0, keepdims=True)

    sums = lax.fori_loop(0, chunks, total, jnp.zeros((1, NGLOB * lanes), F32))
    inv = 1.0 / sums
    lse = top + jnp.log(sums)
    for g in range(NGLOB):
        lse_ref[pl.ds(g, 1), :] = lse[:, g * lanes : (g + 1) * lanes]

    def mix(c, acc):
        w = (s_ref[pl.ds(c * chunk, chunk), :] * inv).astype(BF)
        return acc + tn(w, global_keys(qkv_ref, 2, c, bpd, chunk))

    acc = lax.fori_loop(0, chunks, mix, jnp.zeros((NGLOB * lanes, lanes), F32))
    for g in range(NGLOB):
        out_ref[g // bpd, g % bpd] = take_diagonal(acc[g * lanes : (g + 1) * lanes], per).astype(BF)

    def sparse(b, carry):
        lists, biases = key_lists(b, table_ref, limit, nblk, per)
        keys = jnp.concatenate([pick(qkv_ref, 1, blocks, bpd) for blocks in lists], axis=0)
        values = jnp.concatenate([pick(qkv_ref, 2, blocks, bpd) for blocks in lists], axis=0)
        s = masked_scores(keys, query(b), biases)
        top = jnp.max(s, axis=0, keepdims=True)
        p = jnp.exp(s - top)
        sums = jnp.sum(p, axis=0, keepdims=True)
        w = (p * (1.0 / sums)).astype(BF)
        lse_ref[pl.ds(b, 1), :] = top + jnp.log(sums)
        out_ref[b // bpd, b % bpd] = take_diagonal(tn(w, values), per).astype(BF)
        return carry

    lax.fori_loop(NGLOB, nblk, sparse, 0, unroll=2)


def attend(qkv, table, limit, per):
    n, _, bpd, _, lanes = qkv.shape
    nblk = n * bpd
    kernel = functools.partial(attend_kernel, per=per, bpd=bpd, nblk=nblk)
    return pl.pallas_call(
        kernel,
        in_specs=[SMEM, SMEM, WHOLE],
        out_specs=[WHOLE, WHOLE],
        out_shape=[
            jax.ShapeDtypeStruct((n, bpd, BLOCK, lanes), BF),
            jax.ShapeDtypeStruct((nblk, lanes), F32),
        ],
        scratch_shapes=[pltpu.VMEM((nblk * BLOCK, NGLOB * lanes), F32)],
        compiler_params=params(),
        cost_estimate=cost(40e9, 4e6, 1e7),
        name="attend",
    )(table, limit, qkv)


def attend_back_kernel(
    table_ref, limit_ref, qkv_ref, dout_ref, lse_ref, grad_ref, dk_ref, dv_ref, w_ref, dw_ref, *, per, bpd, nblk
):
    limit = limit_ref[0]
    lanes = per * HD
    chunk = 2 * bpd * BLOCK
    span = 2
    chunks = nblk * BLOCK // chunk
    scale_low = jnp.asarray(SCALE, BF)

    def query(b):
        return block_diagonal(qkv_ref[b // bpd, 0, b % bpd] * scale_low, per)

    def upstream(b):
        return block_diagonal(dout_ref[b // bpd, b % bpd], per)

    both = jnp.concatenate([query(g) for g in range(NGLOB)], axis=0)
    dboth = jnp.concatenate([upstream(g) for g in range(NGLOB)], axis=0)
    lse = jnp.concatenate([lse_ref[pl.ds(g, 1), :] for g in range(NGLOB)], axis=1)
    rowid = lax.broadcasted_iota(jnp.int32, (chunk, NGLOB * lanes), 0)

    def first(c, centre):
        s = nt(global_keys(qkv_ref, 1, c, bpd, chunk), both)
        s = jnp.where(c * chunk + rowid < limit, s, -BIG)
        w = jnp.exp(s - lse)
        dw = nt(global_keys(qkv_ref, 2, c, bpd, chunk), dboth)
        w_ref[pl.ds(c * chunk, chunk), :] = w
        dw_ref[pl.ds(c * chunk, chunk), :] = dw
        return centre + jnp.sum(w * dw, axis=0, keepdims=True)

    centre = lax.fori_loop(0, chunks, first, jnp.zeros((1, NGLOB * lanes), F32))

    def second(c, acc):
        w = w_ref[pl.ds(c * chunk, chunk), :]
        ds = (w * (dw_ref[pl.ds(c * chunk, chunk), :] - centre)).astype(BF)
        dk_ref[pl.ds(c * span, span)] = nn(ds, both).reshape(span, bpd, BLOCK, lanes)
        dv_ref[pl.ds(c * span, span)] = nn(w.astype(BF), dboth).reshape(span, bpd, BLOCK, lanes)
        return acc + tn(ds, global_keys(qkv_ref, 1, c, bpd, chunk))

    acc = lax.fori_loop(0, chunks, second, jnp.zeros((NGLOB * lanes, lanes), F32))
    for g in range(NGLOB):
        dq = take_diagonal(acc[g * lanes : (g + 1) * lanes], per) * SCALE
        grad_ref[g // bpd, 0, g % bpd] = dq.astype(BF)

    def sparse(b, carry):
        lists, biases = key_lists(b, table_ref, limit, nblk, per)
        keys = jnp.concatenate([pick(qkv_ref, 1, blocks, bpd) for blocks in lists], axis=0)
        values = jnp.concatenate([pick(qkv_ref, 2, blocks, bpd) for blocks in lists], axis=0)
        q = query(b)
        do = upstream(b)
        s = masked_scores(keys, q, biases)
        w = jnp.exp(s - lse_ref[pl.ds(b, 1), :])
        dw = nt(values, do)
        centre = jnp.sum(w * dw, axis=0, keepdims=True)
        ds = (w * (dw - centre)).astype(BF)
        grad_ref[b // bpd, 0, b % bpd] = (take_diagonal(tn(ds, keys), per) * SCALE).astype(BF)
        dk = nn(ds, q)
        dv = nn(w.astype(BF), do)
        item = lane_item((BLOCK, lanes))
        for ref, full in ((dk_ref, dk), (dv_ref, dv)):
            for k, blocks in enumerate(lists):
                part = full[k * BLOCK : (k + 1) * BLOCK]
                for i, block in enumerate(blocks):
                    term = part if len(blocks) == 1 else jnp.where(item == i, part, 0.0)
                    ref[block // bpd, block % bpd] += term
        return carry

    lax.fori_loop(NGLOB, nblk, sparse, 0, unroll=2)

    def finish(c, carry):
        grad_ref[c, 1] = dk_ref[c].astype(BF)
        grad_ref[c, 2] = dv_ref[c].astype(BF)
        return carry

    lax.fori_loop(0, nblk // bpd, finish, 0)


def attend_back(qkv, dout, lse, table, limit, per):
    n, _, bpd, _, lanes = qkv.shape
    nblk = n * bpd
    kernel = functools.partial(attend_back_kernel, per=per, bpd=bpd, nblk=nblk)
    return pl.pallas_call(
        kernel,
        in_specs=[SMEM, SMEM, WHOLE, WHOLE, WHOLE],
        out_specs=WHOLE,
        out_shape=jax.ShapeDtypeStruct((n, 3, bpd, BLOCK, lanes), BF),
        scratch_shapes=[
            pltpu.VMEM((n, bpd, BLOCK, lanes), F32),
            pltpu.VMEM((n, bpd, BLOCK, lanes), F32),
            pltpu.VMEM((nblk * BLOCK, NGLOB * lanes), F32),
            pltpu.VMEM((nblk * BLOCK, NGLOB * lanes), F32),
        ],
        compiler_params=params(),
        cost_estimate=cost(80e9, 8e6, 1e7),
        name="attend_back",
    )(table, limit, qkv, dout, lse)


MIDDLE_REFS = 16


def rest_places(n):
    return [s % (n // 4) * 4 + s // (n // 4) for s in range(n)]


def middle_kernel(
    place_ref,
    o_ref,
    x_ref,
    g_ref,
    out_bias_ref,
    up_bias_ref,
    down_bias_ref,
    gain_ref,
    shift_ref,
    *refs,
    local,
    lanes,
):
    *pieces, w_ref, sems = refs
    count = len(pieces) - MIDDLE_REFS
    pieces, others = pieces[:count], pieces[count:]
    (
    result_ref,
    dmid_ref,
    branch_ref,
    dout_ref,
    att_ref,
    h_ref,
    act_ref,
    pre_grad_ref,
    d_out_bias_ref,
    d_up_bias_ref,
    d_down_bias_ref,
    d_gain_ref,
    d_shift_ref,
    mid_ref,
    acc_ref,
    dh_ref,
    ) = others
    step = pl.program_id(0)
    micros, groups = o_ref.shape[:2]
    nb, n, height, fb = w_ref.shape
    width = x_ref.shape[1]
    kr = width // n
    per_b = pl.num_programs(0) // nb
    fr = per_b * kr
    nd = fb // fr
    me_core = place_ref[2 * n]
    at = rest_places(n)

    def out_block(b):
        rows = [w_ref[b ^ me_core, at[s], 2 * fr :] for s in range(n)]
        return jnp.concatenate(rows, axis=0)

    def down_block(b):
        rows = []
        for h in range(nd):
            s = step * nd + h
            rows.append(w_ref[b ^ me_core, s % (n // 4) * 4 + s // (n // 4), :fr])
        return jnp.concatenate(rows, axis=0)

    def up_block():
        core = (step // per_b) ^ me_core
        rows = pl.ds(pl.multiple_of(fr + step % per_b * kr, kr), kr)
        return jnp.concatenate([w_ref[core, at[s], rows] for s in range(n)], axis=0)

    def copies(part, rows):
        found = []
        for k, piece in enumerate(pieces):
            copy = pltpu.make_async_copy(piece.at[:, rows], w_ref.at[k, :, rows], sems.at[part, k])
            copy.start()
            found.append(copy)
        return found

    @pl.when(step == 0)
    def _():
        first = copies(0, pl.ds(2 * fr, kr))
        rest = copies(1, pl.ds(0, 2 * fr))
        for m in range(micros):
            for i in range(groups):
                att_ref[m * local : (m + 1) * local, i * lanes : (i + 1) * lanes] = o_ref[m, i]
        for copy in first:
            copy.wait()
        att = att_ref[...]
        for b in range(nb):
            cols = slice(b * fb, (b + 1) * fb)
            y = nn(att, out_block(b))
            mid_ref[:, cols] = x_ref[:, cols].astype(F32) + y + out_bias_ref[:, cols]
        mid = mid_ref[...]
        xhat, _ = norm_stats(mid)
        h_ref[...] = (xhat * gain_ref[...] + shift_ref[...]).astype(BF)
        acc_ref[...] = mid + down_bias_ref[...]
        dh_ref[...] = jnp.zeros_like(dh_ref)
        d_down_bias_ref[...] = jnp.sum(g_ref[...].astype(F32), axis=0, keepdims=True)
        for copy in rest:
            copy.wait()

    up = up_block()
    pre = nn(h_ref[...], up) + up_bias_ref[...]
    square = pre * pre
    gate = jnp.tanh(GELU_C * pre * (1.0 + GELU_A * square))
    half = 0.5 * (1.0 + gate)
    act = (pre * half).astype(BF)
    slope = half + 0.5 * pre * (1.0 - gate * gate) * (GELU_C * (1.0 + 3.0 * GELU_A * square))
    act_ref[...] = act
    dact = None
    for b in range(nb):
        cols = slice(b * fb, (b + 1) * fb)
        term = nt(g_ref[:, cols], down_block(b))
        dact = term if dact is None else dact + term
    pre_grad = (dact * slope).astype(BF)
    pre_grad_ref[0] = pre_grad
    d_up_bias_ref[...] = jnp.sum(pre_grad.astype(F32), axis=0, keepdims=True)
    for b in range(nb):
        cols = slice(b * fb, (b + 1) * fb)
        acc_ref[:, cols] += nn(act, down_block(b))
    dh_ref[...] += nt(pre_grad, up)

    @pl.when(step == pl.num_programs(0) - 1)
    def _():
        result_ref[...] = acc_ref[...].astype(BF)
        dh = dh_ref[...]
        xhat, rstd = norm_stats(mid_ref[...])
        d_gain_ref[...] = jnp.sum(dh * xhat, axis=0, keepdims=True)
        d_shift_ref[...] = jnp.sum(dh, axis=0, keepdims=True)
        d = dh * gain_ref[...]
        inner = d - jnp.mean(d, axis=-1, keepdims=True) - xhat * jnp.mean(d * xhat, axis=-1, keepdims=True)
        dmid = g_ref[...].astype(F32) + rstd * inner
        dmid_ref[...] = dmid
        branch = dmid.astype(BF)
        branch_ref[...] = branch
        d_out_bias_ref[...] = jnp.sum(branch.astype(F32), axis=0, keepdims=True)
        dout = None
        for b in range(nb):
            term = nt(branch[:, b * fb : (b + 1) * fb], out_block(b))
            dout = term if dout is None else dout + term
        dout = dout.astype(BF)
        for m in range(micros):
            for i in range(groups):
                dout_ref[m, i] = dout[m * local : (m + 1) * local, i * lanes : (i + 1) * lanes]


def middle(nb, n, place, o, x, g, pieces, out_bias, up_bias, down_bias, gain, shift):
    micros, groups, local, lanes = o.shape
    rows, width = x.shape
    fb = pieces[0].shape[-1]
    hidden = up_bias.shape[1]
    steps = hidden // fb
    per_b = steps // nb
    full = lambda dtype: jax.ShapeDtypeStruct((rows, width), dtype)
    vector = jax.ShapeDtypeStruct((1, width), F32)
    whole = lambda shape: pl.BlockSpec(shape, lambda i, place: (0,) * len(shape))
    kernel = functools.partial(middle_kernel, local=local, lanes=lanes)
    return pl.pallas_call(
        kernel,
        grid_spec=pltpu.PrefetchScalarGridSpec(
        num_scalar_prefetch=1,
        grid=(steps,),
        in_specs=[
            whole((micros, groups, local, lanes)),
            whole((rows, width)),
            whole((rows, width)),
            whole((1, width)),
            pl.BlockSpec((1, fb), lambda i, place: (0, i)),
            whole((1, width)),
            whole((1, width)),
            whole((1, width)),
        ]
        + [pl.BlockSpec(memory_space=pl.ANY)] * len(pieces),
        out_specs=[
            whole((rows, width)),
            whole((rows, width)),
            whole((rows, width)),
            whole((micros, groups, local, lanes)),
            whole((rows, width)),
            whole((rows, width)),
            pl.BlockSpec((rows, fb), lambda i, place: (0, i)),
            pl.BlockSpec((1, rows, fb), lambda i, place: ((i // per_b) ^ place[2 * n], 0, i % per_b)),
            whole((1, width)),
            pl.BlockSpec((1, fb), lambda i, place: (0, i)),
            whole((1, width)),
            whole((1, width)),
            whole((1, width)),
        ],
    scratch_shapes=[pltpu.VMEM((rows, width), F32)] * 3 + [pltpu.VMEM((nb,) + pieces[0].shape, BF), pltpu.SemaphoreType.DMA((2, nb))],
        ),
        out_shape=[
            full(BF),
            full(F32),
            full(BF),
            jax.ShapeDtypeStruct((micros, groups, local, lanes), BF),
            full(BF),
            full(BF),
            jax.ShapeDtypeStruct((rows, hidden), BF),
            jax.ShapeDtypeStruct((nb, rows, hidden // nb), BF),
            vector,
            jax.ShapeDtypeStruct((1, hidden), F32),
            vector,
            vector,
            vector,
        ],
        compiler_params=params(),
        cost_estimate=cost(8 * rows * width * hidden + 4 * rows * width * width, 50e6),
        name="middle",
    )(place, o, x, g, out_bias, up_bias, down_bias, gain, shift, *pieces)


def relative_transpose(ref, target_ref, k, me, n):
    kr = target_ref.shape[1] // n
    value = ref[...].T
    for s in range(n):
        at = pl.ds(pl.multiple_of((s ^ me) * kr, kr), kr)
        target_ref[k, at, :] = value[s * kr : (s + 1) * kr]


def ffn_grads_kernel(*refs, nb):
    groups = [refs[i * nb : (i + 1) * nb] for i in range(6)]
    act_refs, gc_refs, h_refs, gp_refs, att_refs, br_refs = groups
    out_ref, ht_ref, at_ref = refs[6 * nb :]
    step = pl.program_id(0)
    count, _, height, fb = out_ref.shape
    fr = act_refs[0].shape[1] // count
    per_b = gp_refs[0].shape[2] // fb
    kr = (height - fr) // (per_b + 1)

    @pl.when(step == 0)
    def _():
        for k in range(nb):
            ht_ref[k] = h_refs[k][...].T
            at_ref[k] = att_refs[k][...].T

    at = pl.ds(pl.multiple_of(step * count * kr, count * kr), count * kr)
    down, up, out = 0.0, 0.0, 0.0
    for k in range(nb):
        down += nn(act_refs[k][...].T, gc_refs[k][...])
        up += nn(ht_ref[k, at, :], gp_refs[k][0])
        out += nn(at_ref[k, at, :], br_refs[k][...])
    down, up, out = down.astype(BF), up.astype(BF), out.astype(BF)
    for i in range(count):
        out_ref[i, 0, :fr] = down[i * fr : (i + 1) * fr]
        for q in range(per_b):
            out_ref[i, 0, fr + q * kr : fr + (q + 1) * kr] = up[i * kr : (i + 1) * kr, q * fb : (q + 1) * fb]
        out_ref[i, 0, fr + per_b * kr :] = out[i * kr : (i + 1) * kr]


def ffn_grads(act, gc, h, gp, att, br, n):
    nb = len(act)
    rows, hidden = act[0].shape
    fb = gc[0].shape[1]
    width = h[0].shape[1]
    fr, kr = hidden // n, width // n
    per_b = hidden // nb // fb
    height = fr + (per_b + 1) * kr
    return pl.pallas_call(
        functools.partial(ffn_grads_kernel, nb=nb),
        grid=(4,),
        in_specs=[pl.BlockSpec((rows, hidden // 4), lambda i: (0, i))] * nb
        + [constant((rows, fb))] * nb
        + [constant((rows, width))] * nb
        + [constant((1, rows, hidden // nb))] * nb
        + [constant((rows, width))] * nb
        + [constant((rows, fb))] * nb,
        out_specs=pl.BlockSpec((n // 4, 1, height, fb), lambda i: (0, i, 0, 0)),
        out_shape=jax.ShapeDtypeStruct((n // 4, 4, height, fb), BF),
        scratch_shapes=[pltpu.VMEM((nb, width, rows), BF)] * 2,
        compiler_params=params(),
        cost_estimate=cost(4 * rows * width * hidden + 2 * rows * width * width, 40e6),
        name="ffn_grads",
    )(*act, *gc, *h, *gp, *att, *br)


def split_kernel(place_ref, grad_ref, *out_refs, n, local, lanes):
    micros, groups = grad_ref.shape[:2]
    core = place_ref[2 * n]
    count = out_refs[0].shape[1] // lanes
    for k, out_ref in enumerate(out_refs):
        for m in range(micros):
            for i in range(count):
                at = (core ^ k) * count + i
                block = grad_ref[m, at % groups, at // groups]
                out_ref[m * local : (m + 1) * local, i * lanes : (i + 1) * lanes] = block


def split_by_core(place, grad, nb, n):
    micros, groups, _, local, lanes = grad.shape
    shape = jax.ShapeDtypeStruct((micros * local, 3 * groups * lanes // nb), BF)
    return pl.pallas_call(
        functools.partial(split_kernel, n=n, local=local, lanes=lanes),
        in_specs=[SMEM, WHOLE],
        out_specs=[WHOLE] * nb,
        out_shape=[shape] * nb,
        compiler_params=params(),
        cost_estimate=cost(1e6, 6e6),
        name="split_by_core",
    )(place, grad)


def qkv_grad_kernel(place_ref, *refs, nb, n):
    h_refs, ga_refs = refs[:nb], refs[nb : 2 * nb]
    a_send_ref, a_keep_ref, b_send_ref, b_keep_ref, ht_ref = refs[2 * nb :]
    first = n // 8
    _, _, kh, fb = a_send_ref.shape

    @pl.when(pl.program_id(0) == 0)
    def _():
        for k in range(nb):
            relative_transpose(h_refs[k], ht_ref, k, place_ref[2 * n + 1], n)

    y = None
    for k in range(nb):
        term = nn(ht_ref[k], ga_refs[k][...])
        y = term if y is None else y + term
    y = y.astype(BF).reshape(4, 2 * first, 2, kh, fb)
    for z in range(4):
        for i in range(first):
            at = z * first + i
            a_send_ref[at, 0] = y[z, first + i, 0]
            a_keep_ref[at, 0] = y[z, i, 0]
            b_send_ref[at, 0] = y[z, 2 * i + 1, 1]
            b_keep_ref[at, 0] = y[z, 2 * i, 1]


def qkv_grad(place, h, ga, n):
    nb = len(h)
    rows, width = h[0].shape
    fb = ga[0].shape[1] // 3
    kh = width // n // 2
    half = jax.ShapeDtypeStruct((n // 2, 3, kh, fb), BF)
    return pl.pallas_call(
        functools.partial(qkv_grad_kernel, nb=nb, n=n),
        grid=(3,),
        in_specs=[SMEM]
        + [constant((rows, width))] * nb
        + [pl.BlockSpec((rows, fb), lambda t: (0, t))] * nb,
        out_specs=[pl.BlockSpec((n // 2, 1, kh, fb), lambda t: (0, t, 0, 0))] * 4,
        out_shape=[half] * 4,
        scratch_shapes=[pltpu.VMEM((nb, width, rows), BF)],
        compiler_params=params(),
        cost_estimate=cost(6 * rows * width * width, 15e6),
        name="qkv_grad",
    )(place, *h, *ga)


def input_grad_kernel(place_ref, x_ref, gain_ref, dmid_ref, *refs, nb):
    grad_refs = refs[:nb]
    *pieces, _, out_ref, d_gain_ref, d_shift_ref, dh_ref, wa_ref, wb_ref, sems = refs[nb:]
    step = pl.program_id(0)

    @pl.when(step == 0)
    def _():
        load_pieces(pieces, wa_ref, wb_ref, sems)

    total = None
    for k in range(nb):
        term = nt(grad_refs[k][...], qkv_block(k, step, place_ref, wa_ref, wb_ref))
        total = term if total is None else total + term

    @pl.when(step == 0)
    def _():
        dh_ref[...] = total

    @pl.when(step > 0)
    def _():
        dh_ref[...] += total

    @pl.when(step == pl.num_programs(0) - 1)
    def _():
        dh = dh_ref[...]
        xhat, rstd = norm_stats(x_ref[...].astype(F32))
        d_gain_ref[...] = jnp.sum(dh * xhat, axis=0, keepdims=True)
        d_shift_ref[...] = jnp.sum(dh, axis=0, keepdims=True)
        d = dh * gain_ref[...]
        inner = d - jnp.mean(d, axis=-1, keepdims=True) - xhat * jnp.mean(d * xhat, axis=-1, keepdims=True)
        out_ref[...] = dmid_ref[...] + rstd * inner


def input_grad(place, grads, pieces, x, gain, dmid, earlier, n):
    rows, width = x.shape
    nb = len(grads)
    fb = pieces[0].shape[-1]
    vector = jax.ShapeDtypeStruct((1, width), F32)
    return pl.pallas_call(
        functools.partial(input_grad_kernel, nb=nb),
        grid=(3,),
        in_specs=[SMEM, constant((rows, width)), constant((1, width)), constant((rows, width))]
        + [pl.BlockSpec((rows, fb), lambda t: (0, t))] * nb
        + [pl.BlockSpec(memory_space=pl.ANY)] * (len(pieces) + 1),
        out_specs=[constant((rows, width)), constant((1, width)), constant((1, width))],
        out_shape=[jax.ShapeDtypeStruct((rows, width), F32), vector, vector],
        scratch_shapes=[pltpu.VMEM((rows, width), F32)] + piece_scratch(pieces, nb, n),
        compiler_params=params(),
        cost_estimate=cost(6 * rows * width * width, 20e6),
        name="input_grad",
    )(place, x, gain, dmid, *grads, *pieces, earlier)


def swap_with(value, axis, k):
    size = lax.axis_size(axis)
    return lax.ppermute(value, axis, [(i, i ^ k) for i in range(size)])


def powers(size):
    return [1 << i for i in range(size.bit_length() - 1)]


def direct(shard, n):
    return [swap_with(shard, "seq", k * n // 4) for k in range(1, 4)]


def planes(n):
    quarter = n // 4
    return [[z * quarter + i for i in range(quarter)] for z in range(4)]


def lines(n):
    return [list(group) for group in zip(*planes(n))]


def gather_line(shard, n):
    return lax.all_gather(shard, "seq", axis_index_groups=lines(n))


def gather_plane(line, n):
    plane = lax.all_gather(line, "seq", axis_index_groups=planes(n))
    return plane.reshape((n,) + line.shape[1:])


def scatter_groups(grad, n):
    scatter = functools.partial(lax.psum_scatter, axis_name="seq", scatter_dimension=0)
    line = scatter(grad, axis_index_groups=planes(n))
    return scatter(line, axis_index_groups=lines(n)).astype(F32)


def halves(shard, arrived):
    both = jnp.stack([shard] + arrived)
    return both[:, 0], both[:, 1]


def together(*values):
    return lax.optimization_barrier(values)


def gather_cores(pieces, nb):
    out = list(pieces)
    for k in range(1, nb):
        out += [swap_with(piece, "batch", k) for piece in pieces]
    return out


def place_of(relative, bits, n):
    place = relative // (n // 4)
    for i, bit in enumerate(bits):
        place = place + jnp.where(relative & bit, 4 << i, 0)
    return place


def place_table(position, core, n):
    relative = jnp.arange(n, dtype=jnp.int32) ^ position
    bits = powers(n // 4)
    ends = jnp.stack([core, position]).astype(jnp.int32)
    return jnp.concatenate([place_of(relative, bits, n), place_of(relative, bits[::-1], n), ends])


def plus(value, arrived):
    return (value.astype(F32) + arrived.astype(F32)).astype(BF)


def reduce_first(a_send, b_send, n):
    return swap_with(a_send, "seq", n // 8), swap_with(b_send, "seq", 1)


def split_next(total):
    m = total.shape[1] // 2
    return total[:, :m], total[:, m:]


def reduce_steps(total, bit_of, n):
    total = total.reshape((4, n // 8) + total.shape[1:])
    while total.shape[1] > 1:
        keep, send = split_next(total)
        total = plus(keep, swap_with(send, "seq", bit_of(send.shape[1])))
    return total[:, 0]


def reduce_rest(a, b, n):
    a = reduce_steps(a, lambda m: m, n)
    b = reduce_steps(b, lambda m: 2 * m, n)
    return jnp.stack([a, b], axis=1)


def reduce_direct(total, n):
    return [swap_with(total[k], "seq", k * n // 4) for k in range(1, 4)]


def reduce_last(total, arrived):
    out = total[0].astype(F32)
    for term in arrived:
        out = out + term.astype(F32)
    return out[0], out[1]


def total_over(value, axis, steps):
    for k in steps:
        value = value + swap_with(value, axis, k)
    return value


def body(
    tokens,
    cotangent,
    lengths,
    random_blocks,
    query_key_value_weight,
    output_weight,
    up_weight,
    down_weight,
    out_bias,
    up_bias,
    down_bias,
    gain_attn,
    shift_attn,
    gain_ffn,
    shift_ffn,
):
    n = lax.axis_size("seq")
    nb = lax.axis_size("batch")
    position = lax.axis_index("seq")
    core = lax.axis_index("batch")
    micros, _, local, width = tokens.shape
    hidden = up_bias.shape[0]
    nblk = n * local // BLOCK
    bpd = local // BLOCK
    per = micros * H // n
    lanes = per * HD
    groups = H // per
    fb = width // nb
    kr = width // n
    kh = kr // 2
    fr = hidden // n
    per_b = hidden // width
    bits = powers(n // 4)
    row = lambda v: v.reshape(1, -1)
    place = place_table(position, core, n)

    shard = query_key_value_weight.reshape(2, kh, 3, fb).transpose(0, 2, 1, 3)
    stacked_up = up_weight.reshape(kr, per_b, fb).transpose(1, 0, 2).reshape(per_b * kr, fb)
    rest = jnp.concatenate([down_weight, stacked_up, output_weight])
    part_a, part_b = halves(shard, direct(shard, n))
    rest_line = gather_line(rest, n)
    for i, bit in enumerate(bits):
        found_a = swap_with(part_a, "seq", bit)
        found_b = swap_with(part_b, "seq", bits[-1 - i])
        if i < len(bits) - 1:
            part_a = jnp.concatenate([part_a, found_a])
            part_b = jnp.concatenate([part_b, found_b])
    qkv_pieces = gather_cores([part_a, found_a, part_b, found_b], nb)

    x = tokens.reshape(micros * local, width)
    g = cotangent.reshape(micros * local, width)
    micro = position * per // H
    head = position * per % H
    table = lax.dynamic_slice(
        random_blocks[:, 0], (micro, 0, head, 0), (1, nblk, per, NRAND)
    ).reshape(-1)
    limit = lax.dynamic_slice(lengths[:, 0], (micro,), (1,))

    def swap(value):
        return lax.all_to_all(value, "seq", split_axis=0, concat_axis=0, tiled=True)

    def over_cores(value):
        return [value] + [swap_with(value, "batch", k) for k in range(1, nb)]

    def columns_over_cores(value, cols):
        mine = lambda c: lax.dynamic_slice_in_dim(value, c * cols, cols, axis=1)
        return [mine(core)] + [swap_with(mine(core ^ k), "batch", k) for k in range(1, nb)]

    qkv, h1 = project(place, x, row(gain_attn), row(shift_attn), qkv_pieces, nb, n, micros, local, lanes)
    qkv, rest_line = together(qkv, rest_line)
    rest_plane = gather_plane(rest_line, n)
    qkv_all = swap(qkv.reshape(n, 3, local, lanes)).reshape(n, 3, bpd, BLOCK, lanes)
    mixed, lse = attend(qkv_all, table, limit, per)
    mixed, rest_plane = together(mixed, rest_plane)
    rest_pieces = gather_cores([rest_plane], nb)
    o = swap(mixed.reshape(n, local, lanes)).reshape(micros, groups, local, lanes)
    (
        result,
        dmid,
        branch,
        dout,
        att,
        h2,
        act,
        pre_grad,
        d_out_bias,
        d_up_bias,
        d_down_bias,
        d_gain_ffn,
        d_shift_ffn,
    ) = middle(
        nb,
        n,
        place,
        o,
        x,
        g,
        rest_pieces,
        row(out_bias),
        row(up_bias),
        row(down_bias),
        row(gain_ffn),
        row(shift_ffn),
    )
    h1_cores = over_cores(h1)
    dout_all = swap(dout.reshape(n, local, lanes)).reshape(n, bpd, BLOCK, lanes)

    rest_grad = ffn_grads(
        over_cores(act),
        columns_over_cores(g, fb),
        over_cores(h2),
        [pre_grad] + [swap_with(pre_grad[k : k + 1], "batch", k) for k in range(1, nb)],
        over_cores(att),
        columns_over_cores(branch, fb),
        n,
    )
    dout_all, rest_grad = together(dout_all, rest_grad)
    grad_rest = scatter_groups(rest_grad, n)
    grads = attend_back(qkv_all, dout_all, lse, table, limit, per)
    grads_back = swap(grads.reshape(n, 3, local, lanes)).reshape(micros, groups, 3, local, lanes)
    own_grads = split_by_core(place, grads_back, nb, n)
    grad_cores = [own_grads[0]] + [swap_with(own_grads[k], "batch", k) for k in range(1, nb)]
    a_send, a_keep, b_send, b_keep = qkv_grad(place, h1_cores, grad_cores, n)
    first_a, first_b = reduce_first(a_send, b_send, n)
    grad_x, d_gain_attn, d_shift_attn = input_grad(
        place, own_grads, qkv_pieces, x, row(gain_attn), dmid, a_keep, n
    )
    vectors = [d_out_bias, d_up_bias, d_down_bias, d_gain_attn, d_shift_attn, d_gain_ffn, d_shift_ffn]
    sums = jnp.concatenate(vectors, axis=1)
    sums, first_a, first_b = together(sums, first_a, first_b)
    qkv_reduced = reduce_rest(plus(a_keep, first_a), plus(b_keep, first_b), n)
    sums = total_over(total_over(sums, "batch", powers(nb)), "seq", powers(n)[-2:])
    qkv_reduced, sums = together(qkv_reduced, sums)
    sums = total_over(sums, "seq", powers(n // 4))[0]
    grad_a, grad_b = reduce_last(qkv_reduced, reduce_direct(qkv_reduced, n))
    grad_qkv = jnp.stack([grad_a, grad_b]).transpose(0, 2, 1, 3).reshape(kr, 3 * fb)
    grad_down = grad_rest[:fr]
    grad_up = grad_rest[fr:-kr].reshape(per_b, kr, fb).transpose(1, 0, 2).reshape(kr, per_b * fb)
    grad_out = grad_rest[-kr:]
    ends = []
    for vector in vectors[:-1]:
        ends.append((ends[-1] if ends else 0) + vector.shape[1])
    return (
        result.reshape(tokens.shape),
        grad_x.reshape(tokens.shape),
        grad_qkv,
        grad_out,
        grad_up,
        grad_down,
        *jnp.split(sums, ends),
    )


def solution(mesh):
    rows = P(None, "batch", "seq", None)
    weight = P("seq", "batch")
    return jax.shard_map(
        body,
        mesh=mesh,
        in_specs=(rows, rows, P(None, "batch"), P(None, "batch", None, None, None))
        + (weight,) * 4
        + (P(),) * 7,
        out_specs=(rows, rows) + (weight,) * 4 + (P(),) * 7,
        check_vma=False,
    )
```

```python
import functools

import jax
import jax.numpy as jnp
from jax import lax
from jax.experimental import pallas as pl
from jax.experimental.pallas import tpu as pltpu
from jax.sharding import PartitionSpec as P

H = 16
HD = 64
BLOCK = 64
NGLOB = 2
NRAND = 3

EPS = 1e-05
BIG = 1e30
SCALE = HD ** (-0.5)
GELU_C = 0.7978845608028654
GELU_A = 0.044715
BF = jnp.bfloat16
F32 = jnp.float32
VMEM_LIMIT = 56 * 1024 * 1024

WHOLE = pl.BlockSpec(memory_space=pltpu.VMEM)
SMEM = pl.BlockSpec(memory_space=pltpu.SMEM)


def nn(a, b):
    return lax.dot_general(a, b, (((1,), (0,)), ((), ())), preferred_element_type=F32)


def nt(a, b):
    return lax.dot_general(a, b, (((1,), (1,)), ((), ())), preferred_element_type=F32)


def tn(a, b):
    return lax.dot_general(a, b, (((0,), (0,)), ((), ())), preferred_element_type=F32)


def params():
    return pltpu.CompilerParams(vmem_limit_bytes=VMEM_LIMIT)


def cost(flops, nbytes, trans=0):
    return pl.CostEstimate(flops=int(flops), bytes_accessed=int(nbytes), transcendentals=int(trans))


def constant(shape):
    return pl.BlockSpec(shape, lambda i: (0,) * len(shape))


def norm_stats(value):
    centre = jnp.mean(value, axis=-1, keepdims=True)
    centered = value - centre
    spread = jnp.mean(centered * centered, axis=-1, keepdims=True)
    rstd = lax.rsqrt(spread + EPS)
    return centered * rstd, rstd


def load_pieces(refs, wa_ref, wb_ref, sems):
    parts = len(refs) // wa_ref.shape[0]
    copies = []
    at = 0
    for i, ref in enumerate(refs):
        if i % (parts // 2) == 0:
            at = 0
        target = (wa_ref, wb_ref)[i % parts // (parts // 2)].at[i // parts, pl.ds(at, ref.shape[0])]
        at += ref.shape[0]
        copies.append(pltpu.make_async_copy(ref, target, sems.at[i]))
    for copy in copies:
        copy.start()
    for copy in copies:
        copy.wait()


def qkv_block(core, part, place_ref, wa_ref, wb_ref):
    n = wa_ref.shape[1]
    rows = []
    for s in range(n):
        rows.append(wa_ref[core, place_ref[s], part])
        rows.append(wb_ref[core, place_ref[n + s], part])
    return jnp.concatenate(rows, axis=0)


def piece_scratch(pieces, nb, n):
    full = (nb, n) + pieces[0].shape[1:]
    return [pltpu.VMEM(full, BF), pltpu.VMEM(full, BF), pltpu.SemaphoreType.DMA((len(pieces),))]


def project_kernel(place_ref, x_ref, gain_ref, shift_ref, *refs, micros, local, lanes):
    *pieces, qkv_ref, h_ref, wa_ref, wb_ref, sems = refs
    fb = wa_ref.shape[4]

    @pl.when(pl.program_id(0) == 0)
    def _():
        xhat, _ = norm_stats(x_ref[...].astype(F32))
        h_ref[...] = (xhat * gain_ref[...] + shift_ref[...]).astype(BF)
        load_pieces(pieces, wa_ref, wb_ref, sems)

    core = (pl.program_id(0) // 3) ^ place_ref[2 * wa_ref.shape[1]]
    y = nn(h_ref[...], qkv_block(core, pl.program_id(0) % 3, place_ref, wa_ref, wb_ref)).astype(BF)
    for m in range(micros):
        for i in range(fb // lanes):
            qkv_ref[m, i, 0] = y[m * local : (m + 1) * local, i * lanes : (i + 1) * lanes]


def project(place, x, gain, shift, pieces, nb, n, micros, local, lanes):
    fb = pieces[0].shape[-1]
    rows, width = x.shape
    groups = width // lanes
    kernel = functools.partial(project_kernel, micros=micros, local=local, lanes=lanes)
    return pl.pallas_call(
        kernel,
        grid=(3 * nb,),
        in_specs=[SMEM, constant((rows, width)), constant((1, width)), constant((1, width))]
        + [pl.BlockSpec(memory_space=pl.ANY)] * len(pieces),
        out_specs=[
            pl.BlockSpec((micros, fb // lanes, 1, local, lanes), lambda g: (0, g % nb, g // nb, 0, 0)),
            constant((rows, width)),
        ],
        out_shape=[
            jax.ShapeDtypeStruct((micros, groups, 3, local, lanes), BF),
            jax.ShapeDtypeStruct((rows, width), BF),
        ],
        scratch_shapes=piece_scratch(pieces, nb, n),
        compiler_params=params(),
        cost_estimate=cost(6 * rows * width * width, 14 * width * width),
        name="project",
    )(place, x, gain, shift, *pieces)


def lane_item(shape):
    return lax.broadcasted_iota(jnp.int32, shape, len(shape) - 1) // HD


def block_diagonal(value, per):
    if per == 1:
        return value
    item = lane_item(value.shape)
    zero = jnp.zeros_like(value)
    return jnp.concatenate([jnp.where(item == i, value, zero) for i in range(per)], axis=0)


def take_diagonal(full, per):
    if per == 1:
        return full
    item = lane_item((BLOCK, full.shape[1]))
    out = full[:BLOCK]
    for i in range(1, per):
        out = jnp.where(item == i, full[i * BLOCK : (i + 1) * BLOCK], out)
    return out


def pick(ref, part, blocks, bpd):
    out = ref[blocks[0] // bpd, part, blocks[0] % bpd]
    item = lane_item(out.shape)
    for i in range(1, len(blocks)):
        out = jnp.where(item == i, ref[blocks[i] // bpd, part, blocks[i] % bpd], out)
    return out


def key_lists(b, table_ref, limit, nblk, per):
    penalty = lambda ok: jnp.where(ok, 0.0, -BIG)
    shared = [0, 1, b - 1, b, jnp.minimum(b + 1, nblk - 1)]
    lists = [[s] for s in shared]
    inside = lambda block: block * BLOCK < limit
    biases = [None, None, penalty(inside(b - 1)), penalty(inside(b)), penalty(inside(b + 1) & (b + 1 < nblk))]
    biases = [[bias] * per for bias in biases]
    for r in range(NRAND):
        blocks = [table_ref[b * per * NRAND + i * NRAND + r] for i in range(per)]
        lists.append(blocks)
        biases.append([penalty(inside(block)) for block in blocks])
    return lists, biases


def add_biases(s, biases):
    item = lane_item((1, s.shape[1]))
    parts = []
    for j, bias in enumerate(biases):
        part = s[j * BLOCK : (j + 1) * BLOCK]
        if bias[0] is not None:
            row = bias[0]
            for i in range(1, len(bias)):
                row = row if bias[i] is bias[0] else jnp.where(item == i, bias[i], row)
            part = part + row
        parts.append(part)
    return jnp.concatenate(parts, axis=0)


def global_keys(ref, part, c, bpd, chunk):
    span = chunk // (bpd * BLOCK)
    return ref[pl.ds(c * span, span), part].reshape(chunk, ref.shape[4])


def to_row(square):
    eye = lax.broadcasted_iota(jnp.int32, square.shape, 0) == lax.broadcasted_iota(jnp.int32, square.shape, 1)
    return jnp.sum(jnp.where(eye, square, 0.0), axis=0, keepdims=True)


def with_ones(values):
    return jnp.concatenate([values, jnp.ones_like(values)], axis=1)


def fold(value, width, combine):
    out = value[:, :width]
    for at in range(width, value.shape[1], width):
        out = combine(out, value[:, at : at + width])
    return out


def attend_kernel(table_ref, limit_ref, qkv_ref, out_ref, lse_ref, s_ref, *, per, bpd, nblk):
    limit = limit_ref[0]
    lanes = per * HD
    rows = per * BLOCK
    chunk = 2 * bpd * BLOCK
    chunks = nblk * BLOCK // chunk
    tile = 2 * BLOCK

    def query(b):
        q = qkv_ref[b // bpd, 0, b % bpd] * jnp.asarray(SCALE, BF)
        return block_diagonal(q, per)

    both = jnp.concatenate([query(g) for g in range(NGLOB)], axis=0)
    key_id = lax.broadcasted_iota(jnp.int32, (1, chunk), 1)

    def score(c, top):
        s = nt(both, global_keys(qkv_ref, 1, c, bpd, chunk))
        s = s + jnp.where(c * chunk + key_id < limit, 0.0, -BIG)
        s_ref[c] = s
        return jnp.maximum(top, fold(s, tile, jnp.maximum))

    top = lax.fori_loop(0, chunks, score, jnp.full((NGLOB * rows, tile), -BIG, F32))
    top = jnp.max(top, axis=1, keepdims=True)

    def mix(c, acc):
        p = jnp.exp(s_ref[c] - top)
        return acc + nn(p.astype(BF), with_ones(global_keys(qkv_ref, 2, c, bpd, chunk)))

    acc = lax.fori_loop(0, chunks, mix, jnp.zeros((NGLOB * rows, 2 * lanes), F32))
    lse = top + jnp.log(acc[:, lanes:])
    acc = acc[:, :lanes] * (1.0 / acc[:, lanes:])
    for g in range(NGLOB):
        at = slice(g * rows, (g + 1) * rows)
        lse_ref[pl.ds(g, 1), :] = to_row(lse[at])
        out_ref[g // bpd, g % bpd] = take_diagonal(acc[at], per).astype(BF)

    def sparse(b, carry):
        lists, biases = key_lists(b, table_ref, limit, nblk, per)
        keys = jnp.concatenate([pick(qkv_ref, 1, blocks, bpd) for blocks in lists], axis=0)
        values = jnp.concatenate([pick(qkv_ref, 2, blocks, bpd) for blocks in lists], axis=0)
        s = nt(query(b), keys)
        which = lax.broadcasted_iota(jnp.int32, (1, tile), 1) < BLOCK
        parts = []
        for i in range(per):
            for j in range(0, len(lists), 2):
                part = s[i * BLOCK : (i + 1) * BLOCK, j * BLOCK : (j + 2) * BLOCK]
                one, two = biases[j][i], biases[j + 1][i]
                if one is not None or two is not None:
                    part = part + jnp.where(which, 0.0 if one is None else one, 0.0 if two is None else two)
                parts.append(part)
        half = len(lists) // 2
        s = [jnp.concatenate([parts[i * half + j] for i in range(per)], axis=0) for j in range(half)]
        top = jnp.max(functools.reduce(jnp.maximum, s), axis=1, keepdims=True)
        p = [jnp.exp(part - top) for part in s]
        mixed = nn(jnp.concatenate([part.astype(BF) for part in p], axis=1), with_ones(values))
        sums = mixed[:, lanes:]
        lse_ref[pl.ds(b, 1), :] = to_row(top + jnp.log(sums))
        out_ref[b // bpd, b % bpd] = take_diagonal(mixed[:, :lanes] * (1.0 / sums), per).astype(BF)
        return carry

    for b in range(NGLOB, 4):
        sparse(b, 0)
    lax.fori_loop(4, nblk, sparse, 0, unroll=4)


def attend(qkv, table, limit, per):
    n, _, bpd, _, lanes = qkv.shape
    nblk = n * bpd
    kernel = functools.partial(attend_kernel, per=per, bpd=bpd, nblk=nblk)
    return pl.pallas_call(
        kernel,
        in_specs=[SMEM, SMEM, WHOLE],
        out_specs=[WHOLE, WHOLE],
        out_shape=[
            jax.ShapeDtypeStruct((n, bpd, BLOCK, lanes), BF),
            jax.ShapeDtypeStruct((nblk, lanes), F32),
        ],
        scratch_shapes=[pltpu.VMEM((n // 2, NGLOB * per * BLOCK, 2 * bpd * BLOCK), F32)],
        compiler_params=params(),
        cost_estimate=cost(40e9, 4e6, 1e7),
        name="attend",
    )(table, limit, qkv)


def attend_back_kernel(
    table_ref, limit_ref, qkv_ref, dout_ref, lse_ref, grad_ref, dk_ref, dv_ref, w_ref, dw_ref, *, per, bpd, nblk
):
    limit = limit_ref[0]
    lanes = per * HD
    chunk = 2 * bpd * BLOCK
    span = 2
    chunks = nblk * BLOCK // chunk
    scale_low = jnp.asarray(SCALE, BF)

    def query(b):
        return block_diagonal(qkv_ref[b // bpd, 0, b % bpd] * scale_low, per)

    def upstream(b):
        return block_diagonal(dout_ref[b // bpd, b % bpd], per)

    both = jnp.concatenate([query(g) for g in range(NGLOB)], axis=0)
    dboth = jnp.concatenate([upstream(g) for g in range(NGLOB)], axis=0)
    lse = jnp.concatenate([lse_ref[pl.ds(g, 1), :] for g in range(NGLOB)], axis=1)
    rowid = lax.broadcasted_iota(jnp.int32, (chunk, NGLOB * lanes), 0)

    def first(c, centre):
        s = nt(global_keys(qkv_ref, 1, c, bpd, chunk), both)
        s = jnp.where(c * chunk + rowid < limit, s, -BIG)
        w = jnp.exp(s - lse)
        dw = nt(global_keys(qkv_ref, 2, c, bpd, chunk), dboth)
        w_ref[pl.ds(c * chunk, chunk), :] = w
        dw_ref[pl.ds(c * chunk, chunk), :] = dw
        return centre + jnp.sum(w * dw, axis=0, keepdims=True)

    centre = lax.fori_loop(0, chunks, first, jnp.zeros((1, NGLOB * lanes), F32))

    def second(c, acc):
        w = w_ref[pl.ds(c * chunk, chunk), :]
        ds = (w * (dw_ref[pl.ds(c * chunk, chunk), :] - centre)).astype(BF)
        dk_ref[pl.ds(c * span, span)] = nn(ds, both).reshape(span, bpd, BLOCK, lanes)
        dv_ref[pl.ds(c * span, span)] = nn(w.astype(BF), dboth).reshape(span, bpd, BLOCK, lanes)
        return acc + tn(ds, global_keys(qkv_ref, 1, c, bpd, chunk))

    acc = lax.fori_loop(0, chunks, second, jnp.zeros((NGLOB * lanes, lanes), F32))
    for g in range(NGLOB):
        dq = take_diagonal(acc[g * lanes : (g + 1) * lanes], per) * SCALE
        grad_ref[g // bpd, 0, g % bpd] = dq.astype(BF)

    def sparse(b, carry):
        lists, biases = key_lists(b, table_ref, limit, nblk, per)
        keys = jnp.concatenate([pick(qkv_ref, 1, blocks, bpd) for blocks in lists], axis=0)
        values = jnp.concatenate([pick(qkv_ref, 2, blocks, bpd) for blocks in lists], axis=0)
        q = query(b)
        do = upstream(b)
        zero = jnp.zeros_like(q)
        sides = jnp.concatenate(
            [jnp.concatenate([q, zero], axis=1), jnp.concatenate([zero, do], axis=1)], axis=0
        )
        both_scores = nt(jnp.concatenate([keys, values], axis=1), sides)
        s = add_biases(both_scores[:, : q.shape[0]], biases)
        dw = both_scores[:, q.shape[0] :]
        w = jnp.exp(s - lse_ref[pl.ds(b, 1), :])
        centre = jnp.sum(w * dw, axis=0, keepdims=True)
        ds = (w * (dw - centre)).astype(BF)
        grad_ref[b // bpd, 0, b % bpd] = (take_diagonal(tn(ds, keys), per) * SCALE).astype(BF)
        both_grads = nn(jnp.concatenate([ds, w.astype(BF)], axis=1), sides)
        dk, dv = both_grads[:, :lanes], both_grads[:, lanes:]
        item = lane_item((BLOCK, lanes))
        for ref, full in ((dk_ref, dk), (dv_ref, dv)):
            for k, blocks in enumerate(lists):
                part = full[k * BLOCK : (k + 1) * BLOCK]
                for i, block in enumerate(blocks):
                    term = part if len(blocks) == 1 else jnp.where(item == i, part, 0.0)
                    ref[block // bpd, block % bpd] += term
        return carry

    for b in range(NGLOB, 4):
        sparse(b, 0)
    lax.fori_loop(4, nblk, sparse, 0, unroll=4)

    def finish(c, carry):
        grad_ref[c, 1] = dk_ref[c].astype(BF)
        grad_ref[c, 2] = dv_ref[c].astype(BF)
        return carry

    lax.fori_loop(0, nblk // bpd, finish, 0)


def attend_back(qkv, dout, lse, table, limit, per):
    n, _, bpd, _, lanes = qkv.shape
    nblk = n * bpd
    kernel = functools.partial(attend_back_kernel, per=per, bpd=bpd, nblk=nblk)
    return pl.pallas_call(
        kernel,
        in_specs=[SMEM, SMEM, WHOLE, WHOLE, WHOLE],
        out_specs=WHOLE,
        out_shape=jax.ShapeDtypeStruct((n, 3, bpd, BLOCK, lanes), BF),
        scratch_shapes=[
            pltpu.VMEM((n, bpd, BLOCK, lanes), F32),
            pltpu.VMEM((n, bpd, BLOCK, lanes), F32),
            pltpu.VMEM((nblk * BLOCK, NGLOB * lanes), F32),
            pltpu.VMEM((nblk * BLOCK, NGLOB * lanes), F32),
        ],
        compiler_params=params(),
        cost_estimate=cost(80e9, 8e6, 1e7),
        name="attend_back",
    )(table, limit, qkv, dout, lse)


MIDDLE_REFS = 16


def rest_places(n):
    return [s % (n // 4) * 4 + s // (n // 4) for s in range(n)]


def middle_kernel(
    place_ref,
    o_ref,
    x_ref,
    g_ref,
    out_bias_ref,
    up_bias_ref,
    down_bias_ref,
    gain_ref,
    shift_ref,
    *refs,
    local,
    lanes,
):
    *pieces, w_ref, sems = refs
    count = len(pieces) - MIDDLE_REFS
    pieces, others = pieces[:count], pieces[count:]
    (
    result_ref,
    dmid_ref,
    branch_ref,
    dout_ref,
    att_ref,
    h_ref,
    act_ref,
    pre_grad_ref,
    d_out_bias_ref,
    d_up_bias_ref,
    d_down_bias_ref,
    d_gain_ref,
    d_shift_ref,
    mid_ref,
    acc_ref,
    dh_ref,
    ) = others
    step = pl.program_id(0)
    micros, groups = o_ref.shape[:2]
    nb, n, height, fb = w_ref.shape
    width = x_ref.shape[1]
    kr = width // n
    per_b = pl.num_programs(0) // nb
    fr = per_b * kr
    nd = fb // fr
    me_core = place_ref[2 * n]
    at = rest_places(n)

    def out_block(b):
        rows = [w_ref[b ^ me_core, at[s], 2 * fr :] for s in range(n)]
        return jnp.concatenate(rows, axis=0)

    def down_block(b):
        rows = []
        for h in range(nd):
            s = step * nd + h
            rows.append(w_ref[b ^ me_core, s % (n // 4) * 4 + s // (n // 4), :fr])
        return jnp.concatenate(rows, axis=0)

    def up_block():
        core = (step // per_b) ^ me_core
        rows = pl.ds(pl.multiple_of(fr + step % per_b * kr, kr), kr)
        return jnp.concatenate([w_ref[core, at[s], rows] for s in range(n)], axis=0)

    def copies(part, rows):
        found = []
        for k, piece in enumerate(pieces):
            copy = pltpu.make_async_copy(piece.at[:, rows], w_ref.at[k, :, rows], sems.at[part, k])
            copy.start()
            found.append(copy)
        return found

    @pl.when(step == 0)
    def _():
        first = copies(0, pl.ds(2 * fr, kr))
        rest = copies(1, pl.ds(0, 2 * fr))
        for m in range(micros):
            for i in range(groups):
                att_ref[m * local : (m + 1) * local, i * lanes : (i + 1) * lanes] = o_ref[m, i]
        for copy in first:
            copy.wait()
        att = att_ref[...]
        for b in range(nb):
            cols = slice(b * fb, (b + 1) * fb)
            y = nn(att, out_block(b))
            mid_ref[:, cols] = x_ref[:, cols].astype(F32) + y + out_bias_ref[:, cols]
        mid = mid_ref[...]
        xhat, _ = norm_stats(mid)
        h_ref[...] = (xhat * gain_ref[...] + shift_ref[...]).astype(BF)
        acc_ref[...] = mid + down_bias_ref[...]
        dh_ref[...] = jnp.zeros_like(dh_ref)
        d_down_bias_ref[...] = jnp.sum(g_ref[...].astype(F32), axis=0, keepdims=True)
        for copy in rest:
            copy.wait()

    up = up_block()
    pre = nn(h_ref[...], up) + up_bias_ref[...]
    square = pre * pre
    gate = jnp.tanh(GELU_C * pre * (1.0 + GELU_A * square))
    half = 0.5 * (1.0 + gate)
    act = (pre * half).astype(BF)
    slope = half + 0.5 * pre * (1.0 - gate * gate) * (GELU_C * (1.0 + 3.0 * GELU_A * square))
    act_ref[...] = act
    dact = None
    for b in range(nb):
        cols = slice(b * fb, (b + 1) * fb)
        term = nt(g_ref[:, cols], down_block(b))
        dact = term if dact is None else dact + term
    pre_grad = (dact * slope).astype(BF)
    pre_grad_ref[0] = pre_grad
    d_up_bias_ref[...] = jnp.sum(pre_grad.astype(F32), axis=0, keepdims=True)
    for b in range(nb):
        cols = slice(b * fb, (b + 1) * fb)
        acc_ref[:, cols] += nn(act, down_block(b))
    dh_ref[...] += nt(pre_grad, up)

    @pl.when(step == pl.num_programs(0) - 1)
    def _():
        result_ref[...] = acc_ref[...].astype(BF)
        dh = dh_ref[...]
        xhat, rstd = norm_stats(mid_ref[...])
        d_gain_ref[...] = jnp.sum(dh * xhat, axis=0, keepdims=True)
        d_shift_ref[...] = jnp.sum(dh, axis=0, keepdims=True)
        d = dh * gain_ref[...]
        inner = d - jnp.mean(d, axis=-1, keepdims=True) - xhat * jnp.mean(d * xhat, axis=-1, keepdims=True)
        dmid = g_ref[...].astype(F32) + rstd * inner
        dmid_ref[...] = dmid
        branch = dmid.astype(BF)
        branch_ref[...] = branch
        d_out_bias_ref[...] = jnp.sum(branch.astype(F32), axis=0, keepdims=True)
        dout = None
        for b in range(nb):
            term = nt(branch[:, b * fb : (b + 1) * fb], out_block(b))
            dout = term if dout is None else dout + term
        dout = dout.astype(BF)
        for m in range(micros):
            for i in range(groups):
                dout_ref[m, i] = dout[m * local : (m + 1) * local, i * lanes : (i + 1) * lanes]


def middle(nb, n, place, o, x, g, pieces, out_bias, up_bias, down_bias, gain, shift):
    micros, groups, local, lanes = o.shape
    rows, width = x.shape
    fb = pieces[0].shape[-1]
    hidden = up_bias.shape[1]
    steps = hidden // fb
    per_b = steps // nb
    full = lambda dtype: jax.ShapeDtypeStruct((rows, width), dtype)
    vector = jax.ShapeDtypeStruct((1, width), F32)
    whole = lambda shape: pl.BlockSpec(shape, lambda i, place: (0,) * len(shape))
    kernel = functools.partial(middle_kernel, local=local, lanes=lanes)
    return pl.pallas_call(
        kernel,
        grid_spec=pltpu.PrefetchScalarGridSpec(
        num_scalar_prefetch=1,
        grid=(steps,),
        in_specs=[
            whole((micros, groups, local, lanes)),
            whole((rows, width)),
            whole((rows, width)),
            whole((1, width)),
            pl.BlockSpec((1, fb), lambda i, place: (0, i)),
            whole((1, width)),
            whole((1, width)),
            whole((1, width)),
        ]
        + [pl.BlockSpec(memory_space=pl.ANY)] * len(pieces),
        out_specs=[
            whole((rows, width)),
            whole((rows, width)),
            whole((rows, width)),
            whole((micros, groups, local, lanes)),
            whole((rows, width)),
            whole((rows, width)),
            pl.BlockSpec((rows, fb), lambda i, place: (0, i)),
            pl.BlockSpec((1, rows, fb), lambda i, place: ((i // per_b) ^ place[2 * n], 0, i % per_b)),
            whole((1, width)),
            pl.BlockSpec((1, fb), lambda i, place: (0, i)),
            whole((1, width)),
            whole((1, width)),
            whole((1, width)),
        ],
    scratch_shapes=[pltpu.VMEM((rows, width), F32)] * 3 + [pltpu.VMEM((nb,) + pieces[0].shape, BF), pltpu.SemaphoreType.DMA((2, nb))],
        ),
        out_shape=[
            full(BF),
            full(F32),
            full(BF),
            jax.ShapeDtypeStruct((micros, groups, local, lanes), BF),
            full(BF),
            full(BF),
            jax.ShapeDtypeStruct((rows, hidden), BF),
            jax.ShapeDtypeStruct((nb, rows, hidden // nb), BF),
            vector,
            jax.ShapeDtypeStruct((1, hidden), F32),
            vector,
            vector,
            vector,
        ],
        compiler_params=params(),
        cost_estimate=cost(8 * rows * width * hidden + 4 * rows * width * width, 50e6),
        name="middle",
    )(place, o, x, g, out_bias, up_bias, down_bias, gain, shift, *pieces)


def relative_transpose(ref, target_ref, k, me, n):
    kr = target_ref.shape[1] // n
    value = ref[...].T
    for s in range(n):
        at = pl.ds(pl.multiple_of((s ^ me) * kr, kr), kr)
        target_ref[k, at, :] = value[s * kr : (s + 1) * kr]


def ffn_grads_kernel(*refs, nb):
    groups = [refs[i * nb : (i + 1) * nb] for i in range(6)]
    act_refs, gc_refs, h_refs, gp_refs, att_refs, br_refs = groups
    out_ref, ht_ref, at_ref = refs[6 * nb :]
    step = pl.program_id(0)
    count, _, height, fb = out_ref.shape
    fr = act_refs[0].shape[1] // count
    per_b = gp_refs[0].shape[2] // fb
    kr = (height - fr) // (per_b + 1)

    @pl.when(step == 0)
    def _():
        for k in range(nb):
            ht_ref[k] = h_refs[k][...].T
            at_ref[k] = att_refs[k][...].T

    at = pl.ds(pl.multiple_of(step * count * kr, count * kr), count * kr)
    down, up, out = 0.0, 0.0, 0.0
    for k in range(nb):
        down += nn(act_refs[k][...].T, gc_refs[k][...])
        up += nn(ht_ref[k, at, :], gp_refs[k][0])
        out += nn(at_ref[k, at, :], br_refs[k][...])
    down, up, out = down.astype(BF), up.astype(BF), out.astype(BF)
    for i in range(count):
        out_ref[i, 0, :fr] = down[i * fr : (i + 1) * fr]
        for q in range(per_b):
            out_ref[i, 0, fr + q * kr : fr + (q + 1) * kr] = up[i * kr : (i + 1) * kr, q * fb : (q + 1) * fb]
        out_ref[i, 0, fr + per_b * kr :] = out[i * kr : (i + 1) * kr]


def ffn_grads(act, gc, h, gp, att, br, n):
    nb = len(act)
    rows, hidden = act[0].shape
    fb = gc[0].shape[1]
    width = h[0].shape[1]
    fr, kr = hidden // n, width // n
    per_b = hidden // nb // fb
    height = fr + (per_b + 1) * kr
    return pl.pallas_call(
        functools.partial(ffn_grads_kernel, nb=nb),
        grid=(4,),
        in_specs=[pl.BlockSpec((rows, hidden // 4), lambda i: (0, i))] * nb
        + [constant((rows, fb))] * nb
        + [constant((rows, width))] * nb
        + [constant((1, rows, hidden // nb))] * nb
        + [constant((rows, width))] * nb
        + [constant((rows, fb))] * nb,
        out_specs=pl.BlockSpec((n // 4, 1, height, fb), lambda i: (0, i, 0, 0)),
        out_shape=jax.ShapeDtypeStruct((n // 4, 4, height, fb), BF),
        scratch_shapes=[pltpu.VMEM((nb, width, rows), BF)] * 2,
        compiler_params=params(),
        cost_estimate=cost(4 * rows * width * hidden + 2 * rows * width * width, 40e6),
        name="ffn_grads",
    )(*act, *gc, *h, *gp, *att, *br)


def split_kernel(place_ref, grad_ref, *out_refs, n, local, lanes):
    micros, groups = grad_ref.shape[:2]
    core = place_ref[2 * n]
    count = out_refs[0].shape[1] // lanes
    for k, out_ref in enumerate(out_refs):
        for m in range(micros):
            for i in range(count):
                at = (core ^ k) * count + i
                block = grad_ref[m, at % groups, at // groups]
                out_ref[m * local : (m + 1) * local, i * lanes : (i + 1) * lanes] = block


def split_by_core(place, grad, nb, n):
    micros, groups, _, local, lanes = grad.shape
    shape = jax.ShapeDtypeStruct((micros * local, 3 * groups * lanes // nb), BF)
    return pl.pallas_call(
        functools.partial(split_kernel, n=n, local=local, lanes=lanes),
        in_specs=[SMEM, WHOLE],
        out_specs=[WHOLE] * nb,
        out_shape=[shape] * nb,
        compiler_params=params(),
        cost_estimate=cost(1e6, 6e6),
        name="split_by_core",
    )(place, grad)


def qkv_grad_kernel(place_ref, *refs, nb, n):
    h_refs, ga_refs = refs[:nb], refs[nb : 2 * nb]
    a_send_ref, a_keep_ref, b_send_ref, b_keep_ref, ht_ref = refs[2 * nb :]
    first = n // 8
    _, _, kh, fb = a_send_ref.shape

    @pl.when(pl.program_id(0) == 0)
    def _():
        for k in range(nb):
            relative_transpose(h_refs[k], ht_ref, k, place_ref[2 * n + 1], n)

    y = None
    for k in range(nb):
        term = nn(ht_ref[k], ga_refs[k][...])
        y = term if y is None else y + term
    y = y.astype(BF).reshape(4, 2 * first, 2, kh, fb)
    for z in range(4):
        for i in range(first):
            at = z * first + i
            a_send_ref[at, 0] = y[z, first + i, 0]
            a_keep_ref[at, 0] = y[z, i, 0]
            b_send_ref[at, 0] = y[z, 2 * i + 1, 1]
            b_keep_ref[at, 0] = y[z, 2 * i, 1]


def qkv_grad(place, h, ga, n):
    nb = len(h)
    rows, width = h[0].shape
    fb = ga[0].shape[1] // 3
    kh = width // n // 2
    half = jax.ShapeDtypeStruct((n // 2, 3, kh, fb), BF)
    return pl.pallas_call(
        functools.partial(qkv_grad_kernel, nb=nb, n=n),
        grid=(3,),
        in_specs=[SMEM]
        + [constant((rows, width))] * nb
        + [pl.BlockSpec((rows, fb), lambda t: (0, t))] * nb,
        out_specs=[pl.BlockSpec((n // 2, 1, kh, fb), lambda t: (0, t, 0, 0))] * 4,
        out_shape=[half] * 4,
        scratch_shapes=[pltpu.VMEM((nb, width, rows), BF)],
        compiler_params=params(),
        cost_estimate=cost(6 * rows * width * width, 15e6),
        name="qkv_grad",
    )(place, *h, *ga)


def input_grad_kernel(place_ref, x_ref, gain_ref, dmid_ref, *refs, nb):
    grad_refs = refs[:nb]
    *pieces, _, out_ref, d_gain_ref, d_shift_ref, dh_ref, wa_ref, wb_ref, sems = refs[nb:]
    step = pl.program_id(0)

    @pl.when(step == 0)
    def _():
        load_pieces(pieces, wa_ref, wb_ref, sems)

    total = None
    for k in range(nb):
        term = nt(grad_refs[k][...], qkv_block(k, step, place_ref, wa_ref, wb_ref))
        total = term if total is None else total + term

    @pl.when(step == 0)
    def _():
        dh_ref[...] = total

    @pl.when(step > 0)
    def _():
        dh_ref[...] += total

    @pl.when(step == pl.num_programs(0) - 1)
    def _():
        dh = dh_ref[...]
        xhat, rstd = norm_stats(x_ref[...].astype(F32))
        d_gain_ref[...] = jnp.sum(dh * xhat, axis=0, keepdims=True)
        d_shift_ref[...] = jnp.sum(dh, axis=0, keepdims=True)
        d = dh * gain_ref[...]
        inner = d - jnp.mean(d, axis=-1, keepdims=True) - xhat * jnp.mean(d * xhat, axis=-1, keepdims=True)
        out_ref[...] = dmid_ref[...] + rstd * inner


def input_grad(place, grads, pieces, x, gain, dmid, earlier, n):
    rows, width = x.shape
    nb = len(grads)
    fb = pieces[0].shape[-1]
    vector = jax.ShapeDtypeStruct((1, width), F32)
    return pl.pallas_call(
        functools.partial(input_grad_kernel, nb=nb),
        grid=(3,),
        in_specs=[SMEM, constant((rows, width)), constant((1, width)), constant((rows, width))]
        + [pl.BlockSpec((rows, fb), lambda t: (0, t))] * nb
        + [pl.BlockSpec(memory_space=pl.ANY)] * (len(pieces) + 1),
        out_specs=[constant((rows, width)), constant((1, width)), constant((1, width))],
        out_shape=[jax.ShapeDtypeStruct((rows, width), F32), vector, vector],
        scratch_shapes=[pltpu.VMEM((rows, width), F32)] + piece_scratch(pieces, nb, n),
        compiler_params=params(),
        cost_estimate=cost(6 * rows * width * width, 20e6),
        name="input_grad",
    )(place, x, gain, dmid, *grads, *pieces, earlier)


def swap_with(value, axis, k):
    size = lax.axis_size(axis)
    return lax.ppermute(value, axis, [(i, i ^ k) for i in range(size)])


def powers(size):
    return [1 << i for i in range(size.bit_length() - 1)]


def direct(shard, n):
    return [swap_with(shard, "seq", k * n // 4) for k in range(1, 4)]


def planes(n):
    quarter = n // 4
    return [[z * quarter + i for i in range(quarter)] for z in range(4)]


def lines(n):
    return [list(group) for group in zip(*planes(n))]


def gather_line(shard, n):
    return lax.all_gather(shard, "seq", axis_index_groups=lines(n))


def gather_plane(line, n):
    plane = lax.all_gather(line, "seq", axis_index_groups=planes(n))
    return plane.reshape((n,) + line.shape[1:])


def scatter_groups(grad, groups):
    return lax.psum_scatter(grad, "seq", scatter_dimension=0, axis_index_groups=groups)


def halves(shard, arrived):
    both = jnp.stack([shard] + arrived)
    return both[:, 0], both[:, 1]


def together(*values):
    return lax.optimization_barrier(values)


def gather_cores(pieces, nb):
    out = list(pieces)
    for k in range(1, nb):
        out += [swap_with(piece, "batch", k) for piece in pieces]
    return out


def place_of(relative, bits, n):
    place = relative // (n // 4)
    for i, bit in enumerate(bits):
        place = place + jnp.where(relative & bit, 4 << i, 0)
    return place


def place_table(position, core, n):
    relative = jnp.arange(n, dtype=jnp.int32) ^ position
    bits = powers(n // 4)
    ends = jnp.stack([core, position]).astype(jnp.int32)
    return jnp.concatenate([place_of(relative, bits, n), place_of(relative, bits[::-1], n), ends])


def plus(value, arrived):
    return (value.astype(F32) + arrived.astype(F32)).astype(BF)


def reduce_first(a_send, b_send, n):
    return swap_with(a_send, "seq", n // 8), swap_with(b_send, "seq", 1)


def split_next(total):
    m = total.shape[1] // 2
    return total[:, :m], total[:, m:]


def reduce_steps(total, bit_of, n):
    total = total.reshape((4, n // 8) + total.shape[1:])
    while total.shape[1] > 1:
        keep, send = split_next(total)
        total = plus(keep, swap_with(send, "seq", bit_of(send.shape[1])))
    return total[:, 0]


def reduce_rest(a, b, n):
    a = reduce_steps(a, lambda m: m, n)
    b = reduce_steps(b, lambda m: 2 * m, n)
    return jnp.stack([a, b], axis=1)


def reduce_direct(total, n):
    return [swap_with(total[k], "seq", k * n // 4) for k in range(1, 4)]


def reduce_last(total, arrived):
    out = total[0].astype(F32)
    for term in arrived:
        out = out + term.astype(F32)
    return out[0], out[1]


def total_over(value, axis, steps):
    for k in steps:
        value = value + swap_with(value, axis, k)
    return value


def body(
    tokens,
    cotangent,
    lengths,
    random_blocks,
    query_key_value_weight,
    output_weight,
    up_weight,
    down_weight,
    out_bias,
    up_bias,
    down_bias,
    gain_attn,
    shift_attn,
    gain_ffn,
    shift_ffn,
):
    n = lax.axis_size("seq")
    nb = lax.axis_size("batch")
    position = lax.axis_index("seq")
    core = lax.axis_index("batch")
    micros, _, local, width = tokens.shape
    hidden = up_bias.shape[0]
    nblk = n * local // BLOCK
    bpd = local // BLOCK
    per = micros * H // n
    lanes = per * HD
    groups = H // per
    fb = width // nb
    kr = width // n
    kh = kr // 2
    fr = hidden // n
    per_b = hidden // width
    bits = powers(n // 4)
    row = lambda v: v.reshape(1, -1)
    place = place_table(position, core, n)

    shard = query_key_value_weight.reshape(2, kh, 3, fb).transpose(0, 2, 1, 3)
    stacked_up = up_weight.reshape(kr, per_b, fb).transpose(1, 0, 2).reshape(per_b * kr, fb)
    rest = jnp.concatenate([down_weight, stacked_up, output_weight])
    part_a, part_b = halves(shard, direct(shard, n))
    part_a, part_b, rest = together(part_a, part_b, rest)
    rest_line = gather_line(rest, n)
    for i, bit in enumerate(bits):
        found_a = swap_with(part_a, "seq", bit)
        found_b = swap_with(part_b, "seq", bits[-1 - i])
        if i < len(bits) - 1:
            part_a = jnp.concatenate([part_a, found_a])
            part_b = jnp.concatenate([part_b, found_b])
    qkv_pieces = gather_cores([part_a, found_a, part_b, found_b], nb)

    x = tokens.reshape(micros * local, width)
    g = cotangent.reshape(micros * local, width)
    micro = position * per // H
    head = position * per % H
    table = lax.dynamic_slice(
        random_blocks[:, 0], (micro, 0, head, 0), (1, nblk, per, NRAND)
    ).reshape(-1)
    limit = lax.dynamic_slice(lengths[:, 0], (micro,), (1,))

    def swap(value):
        return lax.all_to_all(value, "seq", split_axis=0, concat_axis=0, tiled=True)

    def over_cores(value):
        return [value] + [swap_with(value, "batch", k) for k in range(1, nb)]

    def columns_over_cores(value, cols):
        mine = lambda c: lax.dynamic_slice_in_dim(value, c * cols, cols, axis=1)
        return [mine(core)] + [swap_with(mine(core ^ k), "batch", k) for k in range(1, nb)]

    qkv, h1 = project(place, x, row(gain_attn), row(shift_attn), qkv_pieces, nb, n, micros, local, lanes)
    qkv, rest_line = together(qkv, rest_line)
    rest_plane = gather_plane(rest_line, n)
    qkv_all = swap(qkv.reshape(n, 3, local, lanes)).reshape(n, 3, bpd, BLOCK, lanes)
    mixed, lse = attend(qkv_all, table, limit, per)
    o = swap(mixed.reshape(n, local, lanes)).reshape(micros, groups, local, lanes)
    o, rest_plane = together(o, rest_plane)
    rest_pieces = gather_cores([rest_plane], nb)
    (
        result,
        dmid,
        branch,
        dout,
        att,
        h2,
        act,
        pre_grad,
        d_out_bias,
        d_up_bias,
        d_down_bias,
        d_gain_ffn,
        d_shift_ffn,
    ) = middle(
        nb,
        n,
        place,
        o,
        x,
        g,
        rest_pieces,
        row(out_bias),
        row(up_bias),
        row(down_bias),
        row(gain_ffn),
        row(shift_ffn),
    )
    h1_cores = over_cores(h1)
    dout_all = swap(dout.reshape(n, local, lanes)).reshape(n, bpd, BLOCK, lanes)

    rest_grad = ffn_grads(
        over_cores(act),
        columns_over_cores(g, fb),
        over_cores(h2),
        [pre_grad] + [swap_with(pre_grad[k : k + 1], "batch", k) for k in range(1, nb)],
        over_cores(att),
        columns_over_cores(branch, fb),
        n,
    )
    dout_all, rest_grad = together(dout_all, rest_grad)
    rest_line = scatter_groups(rest_grad, planes(n))
    grads = attend_back(qkv_all, dout_all, lse, table, limit, per)
    grads_back = swap(grads.reshape(n, 3, local, lanes)).reshape(micros, groups, 3, local, lanes)
    own_grads = split_by_core(place, grads_back, nb, n)
    grad_cores = [own_grads[0]] + [swap_with(own_grads[k], "batch", k) for k in range(1, nb)]
    a_send, a_keep, b_send, b_keep = qkv_grad(place, h1_cores, grad_cores, n)
    a_keep, rest_line = together(a_keep, rest_line)
    grad_rest = scatter_groups(rest_line, lines(n)).astype(F32)
    first_a, first_b = reduce_first(a_send, b_send, n)
    grad_x, d_gain_attn, d_shift_attn = input_grad(
        place, own_grads, qkv_pieces, x, row(gain_attn), dmid, a_keep, n
    )
    vectors = [d_out_bias, d_up_bias, d_down_bias, d_gain_attn, d_shift_attn, d_gain_ffn, d_shift_ffn]
    sums = jnp.concatenate(vectors, axis=1)
    sums, first_a, first_b = together(sums, first_a, first_b)
    qkv_reduced = reduce_rest(plus(a_keep, first_a), plus(b_keep, first_b), n)
    sums = total_over(total_over(sums, "batch", powers(nb)), "seq", powers(n)[-2:])
    qkv_reduced, sums = together(qkv_reduced, sums)
    sums = total_over(sums, "seq", powers(n // 4))[0]
    grad_a, grad_b = reduce_last(qkv_reduced, reduce_direct(qkv_reduced, n))
    grad_qkv = jnp.stack([grad_a, grad_b]).transpose(0, 2, 1, 3).reshape(kr, 3 * fb)
    grad_down = grad_rest[:fr]
    grad_up = grad_rest[fr:-kr].reshape(per_b, kr, fb).transpose(1, 0, 2).reshape(kr, per_b * fb)
    grad_out = grad_rest[-kr:]
    ends = []
    for vector in vectors[:-1]:
        ends.append((ends[-1] if ends else 0) + vector.shape[1])
    return (
        result.reshape(tokens.shape),
        grad_x.reshape(tokens.shape),
        grad_qkv,
        grad_out,
        grad_up,
        grad_down,
        *jnp.split(sums, ends),
    )


def solution(mesh):
    rows = P(None, "batch", "seq", None)
    weight = P("seq", "batch")
    return jax.shard_map(
        body,
        mesh=mesh,
        in_specs=(rows, rows, P(None, "batch"), P(None, "batch", None, None, None))
        + (weight,) * 4
        + (P(),) * 7,
        out_specs=(rows, rows) + (weight,) * 4 + (P(),) * 7,
        check_vma=False,
    )
```

```python
import functools

import jax
import jax.numpy as jnp
from jax import lax
from jax.experimental import pallas as pl
from jax.experimental.pallas import tpu as pltpu
from jax.sharding import PartitionSpec as P

H = 16
HD = 64
BLOCK = 64
NGLOB = 2
NRAND = 3

EPS = 1e-05
BIG = 1e30
SCALE = HD ** (-0.5)
GELU_C = 0.7978845608028654
GELU_A = 0.044715
BF = jnp.bfloat16
F32 = jnp.float32
VMEM_LIMIT = 56 * 1024 * 1024

WHOLE = pl.BlockSpec(memory_space=pltpu.VMEM)
SMEM = pl.BlockSpec(memory_space=pltpu.SMEM)


def nn(a, b):
    return lax.dot_general(a, b, (((1,), (0,)), ((), ())), preferred_element_type=F32)


def nt(a, b):
    return lax.dot_general(a, b, (((1,), (1,)), ((), ())), preferred_element_type=F32)


def tn(a, b):
    return lax.dot_general(a, b, (((0,), (0,)), ((), ())), preferred_element_type=F32)


def params():
    return pltpu.CompilerParams(vmem_limit_bytes=VMEM_LIMIT)


def cost(flops, nbytes, trans=0):
    return pl.CostEstimate(flops=int(flops), bytes_accessed=int(nbytes), transcendentals=int(trans))


def constant(shape):
    return pl.BlockSpec(shape, lambda i: (0,) * len(shape))


def norm_stats(value):
    centre = jnp.mean(value, axis=-1, keepdims=True)
    centered = value - centre
    spread = jnp.mean(centered * centered, axis=-1, keepdims=True)
    rstd = lax.rsqrt(spread + EPS)
    return centered * rstd, rstd


def load_pieces(refs, wa_ref, wb_ref, sems):
    parts = len(refs) // wa_ref.shape[0]
    copies = []
    at = 0
    for i, ref in enumerate(refs):
        if i % (parts // 2) == 0:
            at = 0
        target = (wa_ref, wb_ref)[i % parts // (parts // 2)].at[i // parts, pl.ds(at, ref.shape[0])]
        at += ref.shape[0]
        copies.append(pltpu.make_async_copy(ref, target, sems.at[i]))
    for copy in copies:
        copy.start()
    return copies


def finish(copies):
    for copy in copies:
        copy.wait()


def qkv_block(core, part, place_ref, wa_ref, wb_ref):
    n = wa_ref.shape[1]
    rows = []
    for s in range(n):
        rows.append(wa_ref[core, place_ref[s], part])
        rows.append(wb_ref[core, place_ref[n + s], part])
    return jnp.concatenate(rows, axis=0)


def piece_scratch(pieces, nb, n):
    full = (nb, n) + pieces[0].shape[1:]
    return [pltpu.VMEM(full, BF), pltpu.VMEM(full, BF), pltpu.SemaphoreType.DMA((len(pieces),))]


def project_kernel(place_ref, x_ref, gain_ref, shift_ref, *refs, micros, local, lanes):
    *pieces, qkv_ref, h_ref, wa_ref, wb_ref, sems = refs
    fb = wa_ref.shape[4]

    @pl.when(pl.program_id(0) == 0)
    def _():
        copies = load_pieces(pieces, wa_ref, wb_ref, sems)
        xhat, _ = norm_stats(x_ref[...].astype(F32))
        h_ref[...] = (xhat * gain_ref[...] + shift_ref[...]).astype(BF)
        finish(copies)

    core = (pl.program_id(0) // 3) ^ place_ref[2 * wa_ref.shape[1]]
    y = nn(h_ref[...], qkv_block(core, pl.program_id(0) % 3, place_ref, wa_ref, wb_ref)).astype(BF)
    for m in range(micros):
        for i in range(fb // lanes):
            qkv_ref[m, i, 0] = y[m * local : (m + 1) * local, i * lanes : (i + 1) * lanes]


def project(place, x, gain, shift, pieces, nb, n, micros, local, lanes):
    fb = pieces[0].shape[-1]
    rows, width = x.shape
    groups = width // lanes
    kernel = functools.partial(project_kernel, micros=micros, local=local, lanes=lanes)
    return pl.pallas_call(
        kernel,
        grid=(3 * nb,),
        in_specs=[SMEM, constant((rows, width)), constant((1, width)), constant((1, width))]
        + [pl.BlockSpec(memory_space=pl.ANY)] * len(pieces),
        out_specs=[
            pl.BlockSpec((micros, fb // lanes, 1, local, lanes), lambda g: (0, g % nb, g // nb, 0, 0)),
            constant((rows, width)),
        ],
        out_shape=[
            jax.ShapeDtypeStruct((micros, groups, 3, local, lanes), BF),
            jax.ShapeDtypeStruct((rows, width), BF),
        ],
        scratch_shapes=piece_scratch(pieces, nb, n),
        compiler_params=params(),
        cost_estimate=cost(6 * rows * width * width, 14 * width * width),
        name="project",
    )(place, x, gain, shift, *pieces)


def lane_item(shape):
    return lax.broadcasted_iota(jnp.int32, shape, len(shape) - 1) // HD


def block_diagonal(value, per):
    if per == 1:
        return value
    item = lane_item(value.shape)
    zero = jnp.zeros_like(value)
    return jnp.concatenate([jnp.where(item == i, value, zero) for i in range(per)], axis=0)


def take_diagonal(full, per):
    if per == 1:
        return full
    item = lane_item((BLOCK, full.shape[1]))
    out = full[:BLOCK]
    for i in range(1, per):
        out = jnp.where(item == i, full[i * BLOCK : (i + 1) * BLOCK], out)
    return out


def pick(ref, part, blocks, bpd):
    out = ref[blocks[0] // bpd, part, blocks[0] % bpd]
    item = lane_item(out.shape)
    for i in range(1, len(blocks)):
        out = jnp.where(item == i, ref[blocks[i] // bpd, part, blocks[i] % bpd], out)
    return out


def key_lists(b, table_ref, limit, nblk, per):
    penalty = lambda ok: jnp.where(ok, 0.0, -BIG)
    shared = [0, 1, b - 1, b, jnp.minimum(b + 1, nblk - 1)]
    lists = [[s] for s in shared]
    inside = lambda block: block * BLOCK < limit
    biases = [None, None, penalty(inside(b - 1)), penalty(inside(b)), penalty(inside(b + 1) & (b + 1 < nblk))]
    biases = [[bias] * per for bias in biases]
    for r in range(NRAND):
        blocks = [table_ref[b * per * NRAND + i * NRAND + r] for i in range(per)]
        lists.append(blocks)
        biases.append([penalty(inside(block)) for block in blocks])
    return lists, biases


def add_biases(s, biases):
    item = lane_item((1, s.shape[1]))
    parts = []
    for j, bias in enumerate(biases):
        part = s[j * BLOCK : (j + 1) * BLOCK]
        if bias[0] is not None:
            row = bias[0]
            for i in range(1, len(bias)):
                row = row if bias[i] is bias[0] else jnp.where(item == i, bias[i], row)
            part = part + row
        parts.append(part)
    return jnp.concatenate(parts, axis=0)


def global_keys(ref, part, c, bpd, chunk):
    span = chunk // (bpd * BLOCK)
    return ref[pl.ds(c * span, span), part].reshape(chunk, ref.shape[4])


def to_row(square):
    eye = lax.broadcasted_iota(jnp.int32, square.shape, 0) == lax.broadcasted_iota(jnp.int32, square.shape, 1)
    return jnp.sum(jnp.where(eye, square, 0.0), axis=0, keepdims=True)


def with_ones(values):
    return jnp.concatenate([values, jnp.ones_like(values)], axis=1)


def fold(value, width, combine):
    out = value[:, :width]
    for at in range(width, value.shape[1], width):
        out = combine(out, value[:, at : at + width])
    return out


def attend_kernel(table_ref, limit_ref, qkv_ref, out_ref, lse_ref, s_ref, *, per, bpd, nblk):
    limit = limit_ref[0]
    lanes = per * HD
    rows = per * BLOCK
    chunk = 2 * bpd * BLOCK
    chunks = nblk * BLOCK // chunk
    tile = 2 * BLOCK

    def query(b):
        q = qkv_ref[b // bpd, 0, b % bpd] * jnp.asarray(SCALE, BF)
        return block_diagonal(q, per)

    both = jnp.concatenate([query(g) for g in range(NGLOB)], axis=0)
    key_id = lax.broadcasted_iota(jnp.int32, (1, chunk), 1)

    def score(c, top):
        s = nt(both, global_keys(qkv_ref, 1, c, bpd, chunk))
        s = s + jnp.where(c * chunk + key_id < limit, 0.0, -BIG)
        s_ref[c] = s
        return jnp.maximum(top, fold(s, tile, jnp.maximum))

    top = lax.fori_loop(0, chunks, score, jnp.full((NGLOB * rows, tile), -BIG, F32))
    top = jnp.max(top, axis=1, keepdims=True)

    def mix(c, acc):
        p = jnp.exp(s_ref[c] - top)
        return acc + nn(p.astype(BF), with_ones(global_keys(qkv_ref, 2, c, bpd, chunk)))

    acc = lax.fori_loop(0, chunks, mix, jnp.zeros((NGLOB * rows, 2 * lanes), F32))
    lse = top + jnp.log(acc[:, lanes:])
    acc = acc[:, :lanes] * (1.0 / acc[:, lanes:])
    for g in range(NGLOB):
        at = slice(g * rows, (g + 1) * rows)
        lse_ref[pl.ds(g, 1), :] = to_row(lse[at])
        out_ref[g // bpd, g % bpd] = take_diagonal(acc[at], per).astype(BF)

    def sparse(b, carry):
        lists, biases = key_lists(b, table_ref, limit, nblk, per)
        keys = jnp.concatenate([pick(qkv_ref, 1, blocks, bpd) for blocks in lists], axis=0)
        values = jnp.concatenate([pick(qkv_ref, 2, blocks, bpd) for blocks in lists], axis=0)
        s = nt(query(b), keys)
        which = lax.broadcasted_iota(jnp.int32, (1, tile), 1) < BLOCK
        parts = []
        for i in range(per):
            for j in range(0, len(lists), 2):
                part = s[i * BLOCK : (i + 1) * BLOCK, j * BLOCK : (j + 2) * BLOCK]
                one, two = biases[j][i], biases[j + 1][i]
                if one is not None or two is not None:
                    part = part + jnp.where(which, 0.0 if one is None else one, 0.0 if two is None else two)
                parts.append(part)
        half = len(lists) // 2
        s = [jnp.concatenate([parts[i * half + j] for i in range(per)], axis=0) for j in range(half)]
        top = jnp.max(functools.reduce(jnp.maximum, s), axis=1, keepdims=True)
        p = [jnp.exp(part - top) for part in s]
        mixed = nn(jnp.concatenate([part.astype(BF) for part in p], axis=1), with_ones(values))
        sums = mixed[:, lanes:]
        lse_ref[pl.ds(b, 1), :] = to_row(top + jnp.log(sums))
        out_ref[b // bpd, b % bpd] = take_diagonal(mixed[:, :lanes] * (1.0 / sums), per).astype(BF)
        return carry

    for b in range(NGLOB, 4):
        sparse(b, 0)
    lax.fori_loop(4, nblk, sparse, 0, unroll=4)


def attend(qkv, table, limit, per):
    n, _, bpd, _, lanes = qkv.shape
    nblk = n * bpd
    kernel = functools.partial(attend_kernel, per=per, bpd=bpd, nblk=nblk)
    return pl.pallas_call(
        kernel,
        in_specs=[SMEM, SMEM, WHOLE],
        out_specs=[WHOLE, WHOLE],
        out_shape=[
            jax.ShapeDtypeStruct((n, bpd, BLOCK, lanes), BF),
            jax.ShapeDtypeStruct((nblk, lanes), F32),
        ],
        scratch_shapes=[pltpu.VMEM((n // 2, NGLOB * per * BLOCK, 2 * bpd * BLOCK), F32)],
        compiler_params=params(),
        cost_estimate=cost(40e9, 4e6, 1e7),
        name="attend",
    )(table, limit, qkv)


def attend_back_kernel(
    table_ref, limit_ref, qkv_ref, dout_ref, lse_ref, grad_ref, dk_ref, dv_ref, w_ref, dw_ref, *, per, bpd, nblk
):
    limit = limit_ref[0]
    lanes = per * HD
    chunk = 2 * bpd * BLOCK
    span = 2
    chunks = nblk * BLOCK // chunk
    scale_low = jnp.asarray(SCALE, BF)

    def query(b):
        return block_diagonal(qkv_ref[b // bpd, 0, b % bpd] * scale_low, per)

    def upstream(b):
        return block_diagonal(dout_ref[b // bpd, b % bpd], per)

    both = jnp.concatenate([query(g) for g in range(NGLOB)], axis=0)
    dboth = jnp.concatenate([upstream(g) for g in range(NGLOB)], axis=0)
    lse = jnp.concatenate([lse_ref[pl.ds(g, 1), :] for g in range(NGLOB)], axis=1)
    rowid = lax.broadcasted_iota(jnp.int32, (chunk, NGLOB * lanes), 0)

    def first(c, centre):
        s = nt(global_keys(qkv_ref, 1, c, bpd, chunk), both)
        s = jnp.where(c * chunk + rowid < limit, s, -BIG)
        w = jnp.exp(s - lse)
        dw = nt(global_keys(qkv_ref, 2, c, bpd, chunk), dboth)
        w_ref[pl.ds(c * chunk, chunk), :] = w
        dw_ref[pl.ds(c * chunk, chunk), :] = dw
        return centre + jnp.sum(w * dw, axis=0, keepdims=True)

    centre = lax.fori_loop(0, chunks, first, jnp.zeros((1, NGLOB * lanes), F32))

    def second(c, acc):
        w = w_ref[pl.ds(c * chunk, chunk), :]
        ds = (w * (dw_ref[pl.ds(c * chunk, chunk), :] - centre)).astype(BF)
        dk_ref[pl.ds(c * span, span)] = nn(ds, both).reshape(span, bpd, BLOCK, lanes)
        dv_ref[pl.ds(c * span, span)] = nn(w.astype(BF), dboth).reshape(span, bpd, BLOCK, lanes)
        return acc + tn(ds, global_keys(qkv_ref, 1, c, bpd, chunk))

    acc = lax.fori_loop(0, chunks, second, jnp.zeros((NGLOB * lanes, lanes), F32))
    for g in range(NGLOB):
        dq = take_diagonal(acc[g * lanes : (g + 1) * lanes], per) * SCALE
        grad_ref[g // bpd, 0, g % bpd] = dq.astype(BF)

    def sparse(b, carry):
        lists, biases = key_lists(b, table_ref, limit, nblk, per)
        keys = jnp.concatenate([pick(qkv_ref, 1, blocks, bpd) for blocks in lists], axis=0)
        values = jnp.concatenate([pick(qkv_ref, 2, blocks, bpd) for blocks in lists], axis=0)
        q = query(b)
        do = upstream(b)
        zero = jnp.zeros_like(q)
        sides = jnp.concatenate(
            [jnp.concatenate([q, zero], axis=1), jnp.concatenate([zero, do], axis=1)], axis=0
        )
        both_scores = nt(jnp.concatenate([keys, values], axis=1), sides)
        s = add_biases(both_scores[:, : q.shape[0]], biases)
        dw = both_scores[:, q.shape[0] :]
        w = jnp.exp(s - lse_ref[pl.ds(b, 1), :])
        centre = jnp.sum(w * dw, axis=0, keepdims=True)
        ds = (w * (dw - centre)).astype(BF)
        grad_ref[b // bpd, 0, b % bpd] = (take_diagonal(tn(ds, keys), per) * SCALE).astype(BF)
        both_grads = nn(jnp.concatenate([ds, w.astype(BF)], axis=1), sides)
        dk, dv = both_grads[:, :lanes], both_grads[:, lanes:]
        item = lane_item((BLOCK, lanes))
        for ref, full in ((dk_ref, dk), (dv_ref, dv)):
            for k, blocks in enumerate(lists):
                part = full[k * BLOCK : (k + 1) * BLOCK]
                for i, block in enumerate(blocks):
                    term = part if len(blocks) == 1 else jnp.where(item == i, part, 0.0)
                    ref[block // bpd, block % bpd] += term
        return carry

    for b in range(NGLOB, 4):
        sparse(b, 0)
    lax.fori_loop(4, nblk, sparse, 0, unroll=4)

    def finish(c, carry):
        grad_ref[c, 1] = dk_ref[c].astype(BF)
        grad_ref[c, 2] = dv_ref[c].astype(BF)
        return carry

    lax.fori_loop(0, nblk // bpd, finish, 0)


def attend_back(qkv, dout, lse, table, limit, per):
    n, _, bpd, _, lanes = qkv.shape
    nblk = n * bpd
    kernel = functools.partial(attend_back_kernel, per=per, bpd=bpd, nblk=nblk)
    return pl.pallas_call(
        kernel,
        in_specs=[SMEM, SMEM, WHOLE, WHOLE, WHOLE],
        out_specs=WHOLE,
        out_shape=jax.ShapeDtypeStruct((n, 3, bpd, BLOCK, lanes), BF),
        scratch_shapes=[
            pltpu.VMEM((n, bpd, BLOCK, lanes), F32),
            pltpu.VMEM((n, bpd, BLOCK, lanes), F32),
            pltpu.VMEM((nblk * BLOCK, NGLOB * lanes), F32),
            pltpu.VMEM((nblk * BLOCK, NGLOB * lanes), F32),
        ],
        compiler_params=params(),
        cost_estimate=cost(80e9, 8e6, 1e7),
        name="attend_back",
    )(table, limit, qkv, dout, lse)


MIDDLE_REFS = 16


def rest_places(n):
    return [s % (n // 4) * 4 + s // (n // 4) for s in range(n)]


def middle_kernel(
    place_ref,
    o_ref,
    x_ref,
    g_ref,
    out_bias_ref,
    up_bias_ref,
    down_bias_ref,
    gain_ref,
    shift_ref,
    *refs,
    local,
    lanes,
):
    *pieces, w_ref, sems = refs
    count = len(pieces) - MIDDLE_REFS
    pieces, others = pieces[:count], pieces[count:]
    (
    result_ref,
    dmid_ref,
    branch_ref,
    dout_ref,
    att_ref,
    h_ref,
    act_ref,
    pre_grad_ref,
    d_out_bias_ref,
    d_up_bias_ref,
    d_down_bias_ref,
    d_gain_ref,
    d_shift_ref,
    mid_ref,
    acc_ref,
    dh_ref,
    ) = others
    step = pl.program_id(0)
    micros, groups = o_ref.shape[:2]
    nb, n, height, fb = w_ref.shape
    width = x_ref.shape[1]
    kr = width // n
    per_b = pl.num_programs(0) // nb
    fr = per_b * kr
    nd = fb // fr
    me_core = place_ref[2 * n]
    at = rest_places(n)

    def out_block(b):
        rows = [w_ref[b ^ me_core, at[s], 2 * fr :] for s in range(n)]
        return jnp.concatenate(rows, axis=0)

    def down_block(b):
        rows = []
        for h in range(nd):
            s = step * nd + h
            rows.append(w_ref[b ^ me_core, s % (n // 4) * 4 + s // (n // 4), :fr])
        return jnp.concatenate(rows, axis=0)

    def up_block():
        core = (step // per_b) ^ me_core
        rows = pl.ds(pl.multiple_of(fr + step % per_b * kr, kr), kr)
        return jnp.concatenate([w_ref[core, at[s], rows] for s in range(n)], axis=0)

    def copies(part, rows):
        found = []
        for k, piece in enumerate(pieces):
            copy = pltpu.make_async_copy(piece.at[:, rows], w_ref.at[k, :, rows], sems.at[part, k])
            copy.start()
            found.append(copy)
        return found

    @pl.when(step == 0)
    def _():
        first = copies(0, pl.ds(2 * fr, kr))
        rest = copies(1, pl.ds(0, 2 * fr))
        for m in range(micros):
            for i in range(groups):
                att_ref[m * local : (m + 1) * local, i * lanes : (i + 1) * lanes] = o_ref[m, i]
        for copy in first:
            copy.wait()
        att = att_ref[...]
        for b in range(nb):
            cols = slice(b * fb, (b + 1) * fb)
            y = nn(att, out_block(b))
            mid_ref[:, cols] = x_ref[:, cols].astype(F32) + y + out_bias_ref[:, cols]
        mid = mid_ref[...]
        xhat, _ = norm_stats(mid)
        h_ref[...] = (xhat * gain_ref[...] + shift_ref[...]).astype(BF)
        acc_ref[...] = mid + down_bias_ref[...]
        dh_ref[...] = jnp.zeros_like(dh_ref)
        d_down_bias_ref[...] = jnp.sum(g_ref[...].astype(F32), axis=0, keepdims=True)
        for copy in rest:
            copy.wait()

    up = up_block()
    pre = nn(h_ref[...], up) + up_bias_ref[...]
    square = pre * pre
    gate = jnp.tanh(GELU_C * pre * (1.0 + GELU_A * square))
    half = 0.5 * (1.0 + gate)
    act = (pre * half).astype(BF)
    slope = half + 0.5 * pre * (1.0 - gate * gate) * (GELU_C * (1.0 + 3.0 * GELU_A * square))
    act_ref[...] = act
    dact = None
    for b in range(nb):
        cols = slice(b * fb, (b + 1) * fb)
        term = nt(g_ref[:, cols], down_block(b))
        dact = term if dact is None else dact + term
    pre_grad = (dact * slope).astype(BF)
    pre_grad_ref[0] = pre_grad
    d_up_bias_ref[...] = jnp.sum(pre_grad.astype(F32), axis=0, keepdims=True)
    for b in range(nb):
        cols = slice(b * fb, (b + 1) * fb)
        acc_ref[:, cols] += nn(act, down_block(b))
    dh_ref[...] += nt(pre_grad, up)

    @pl.when(step == pl.num_programs(0) - 1)
    def _():
        result_ref[...] = acc_ref[...].astype(BF)
        dh = dh_ref[...]
        xhat, rstd = norm_stats(mid_ref[...])
        d_gain_ref[...] = jnp.sum(dh * xhat, axis=0, keepdims=True)
        d_shift_ref[...] = jnp.sum(dh, axis=0, keepdims=True)
        d = dh * gain_ref[...]
        inner = d - jnp.mean(d, axis=-1, keepdims=True) - xhat * jnp.mean(d * xhat, axis=-1, keepdims=True)
        dmid = g_ref[...].astype(F32) + rstd * inner
        dmid_ref[...] = dmid
        branch = dmid.astype(BF)
        branch_ref[...] = branch
        d_out_bias_ref[...] = jnp.sum(branch.astype(F32), axis=0, keepdims=True)
        dout = None
        for b in range(nb):
            term = nt(branch[:, b * fb : (b + 1) * fb], out_block(b))
            dout = term if dout is None else dout + term
        dout = dout.astype(BF)
        for m in range(micros):
            for i in range(groups):
                dout_ref[m, i] = dout[m * local : (m + 1) * local, i * lanes : (i + 1) * lanes]


def middle(nb, n, place, o, x, g, pieces, out_bias, up_bias, down_bias, gain, shift):
    micros, groups, local, lanes = o.shape
    rows, width = x.shape
    fb = pieces[0].shape[-1]
    hidden = up_bias.shape[1]
    steps = hidden // fb
    per_b = steps // nb
    full = lambda dtype: jax.ShapeDtypeStruct((rows, width), dtype)
    vector = jax.ShapeDtypeStruct((1, width), F32)
    whole = lambda shape: pl.BlockSpec(shape, lambda i, place: (0,) * len(shape))
    kernel = functools.partial(middle_kernel, local=local, lanes=lanes)
    return pl.pallas_call(
        kernel,
        grid_spec=pltpu.PrefetchScalarGridSpec(
        num_scalar_prefetch=1,
        grid=(steps,),
        in_specs=[
            whole((micros, groups, local, lanes)),
            whole((rows, width)),
            whole((rows, width)),
            whole((1, width)),
            pl.BlockSpec((1, fb), lambda i, place: (0, i)),
            whole((1, width)),
            whole((1, width)),
            whole((1, width)),
        ]
        + [pl.BlockSpec(memory_space=pl.ANY)] * len(pieces),
        out_specs=[
            whole((rows, width)),
            whole((rows, width)),
            whole((rows, width)),
            whole((micros, groups, local, lanes)),
            whole((rows, width)),
            whole((rows, width)),
            pl.BlockSpec((rows, fb), lambda i, place: (0, i)),
            pl.BlockSpec((1, rows, fb), lambda i, place: ((i // per_b) ^ place[2 * n], 0, i % per_b)),
            whole((1, width)),
            pl.BlockSpec((1, fb), lambda i, place: (0, i)),
            whole((1, width)),
            whole((1, width)),
            whole((1, width)),
        ],
    scratch_shapes=[pltpu.VMEM((rows, width), F32)] * 3 + [pltpu.VMEM((nb,) + pieces[0].shape, BF), pltpu.SemaphoreType.DMA((2, nb))],
        ),
        out_shape=[
            full(BF),
            full(F32),
            full(BF),
            jax.ShapeDtypeStruct((micros, groups, local, lanes), BF),
            full(BF),
            full(BF),
            jax.ShapeDtypeStruct((rows, hidden), BF),
            jax.ShapeDtypeStruct((nb, rows, hidden // nb), BF),
            vector,
            jax.ShapeDtypeStruct((1, hidden), F32),
            vector,
            vector,
            vector,
        ],
        compiler_params=params(),
        cost_estimate=cost(8 * rows * width * hidden + 4 * rows * width * width, 50e6),
        name="middle",
    )(place, o, x, g, out_bias, up_bias, down_bias, gain, shift, *pieces)


def relative_transpose(ref, target_ref, k, me, n):
    kr = target_ref.shape[1] // n
    value = ref[...].T
    for s in range(n):
        at = pl.ds(pl.multiple_of((s ^ me) * kr, kr), kr)
        target_ref[k, at, :] = value[s * kr : (s + 1) * kr]


def ffn_grads_kernel(*refs, nb):
    groups = [refs[i * nb : (i + 1) * nb] for i in range(6)]
    act_refs, gc_refs, h_refs, gp_refs, att_refs, br_refs = groups
    out_ref, ht_ref, at_ref = refs[6 * nb :]
    step = pl.program_id(0)
    count, _, height, fb = out_ref.shape
    fr = act_refs[0].shape[1] // count
    per_b = gp_refs[0].shape[2] // fb
    kr = (height - fr) // (per_b + 1)

    @pl.when(step == 0)
    def _():
        for k in range(nb):
            ht_ref[k] = h_refs[k][...].T
            at_ref[k] = att_refs[k][...].T

    at = pl.ds(pl.multiple_of(step * count * kr, count * kr), count * kr)
    down, up, out = 0.0, 0.0, 0.0
    for k in range(nb):
        down += nn(act_refs[k][...].T, gc_refs[k][...])
        up += nn(ht_ref[k, at, :], gp_refs[k][0])
        out += nn(at_ref[k, at, :], br_refs[k][...])
    down, up, out = down.astype(BF), up.astype(BF), out.astype(BF)
    for i in range(count):
        out_ref[i, 0, :fr] = down[i * fr : (i + 1) * fr]
        for q in range(per_b):
            out_ref[i, 0, fr + q * kr : fr + (q + 1) * kr] = up[i * kr : (i + 1) * kr, q * fb : (q + 1) * fb]
        out_ref[i, 0, fr + per_b * kr :] = out[i * kr : (i + 1) * kr]


def ffn_grads(act, gc, h, gp, att, br, n):
    nb = len(act)
    rows, hidden = act[0].shape
    fb = gc[0].shape[1]
    width = h[0].shape[1]
    fr, kr = hidden // n, width // n
    per_b = hidden // nb // fb
    height = fr + (per_b + 1) * kr
    return pl.pallas_call(
        functools.partial(ffn_grads_kernel, nb=nb),
        grid=(4,),
        in_specs=[pl.BlockSpec((rows, hidden // 4), lambda i: (0, i))] * nb
        + [constant((rows, fb))] * nb
        + [constant((rows, width))] * nb
        + [constant((1, rows, hidden // nb))] * nb
        + [constant((rows, width))] * nb
        + [constant((rows, fb))] * nb,
        out_specs=pl.BlockSpec((n // 4, 1, height, fb), lambda i: (0, i, 0, 0)),
        out_shape=jax.ShapeDtypeStruct((n // 4, 4, height, fb), BF),
        scratch_shapes=[pltpu.VMEM((nb, width, rows), BF)] * 2,
        compiler_params=params(),
        cost_estimate=cost(4 * rows * width * hidden + 2 * rows * width * width, 40e6),
        name="ffn_grads",
    )(*act, *gc, *h, *gp, *att, *br)


def split_kernel(place_ref, grad_ref, *out_refs, n, lanes):
    groups = grad_ref.shape[1]
    core = place_ref[2 * n]
    count = out_refs[0].shape[1] // lanes
    for k, out_ref in enumerate(out_refs):
        for i in range(count):
            at = (core ^ k) * count + i
            out_ref[:, i * lanes : (i + 1) * lanes] = grad_ref[0, at % groups, at // groups]


def split_by_core(place, grad, nb, n):
    micros, groups, _, local, lanes = grad.shape
    cols = 3 * groups * lanes // nb
    return pl.pallas_call(
        functools.partial(split_kernel, n=n, lanes=lanes),
        grid=(micros,),
        in_specs=[SMEM, pl.BlockSpec((1, groups, 3, local, lanes), lambda m: (m, 0, 0, 0, 0))],
        out_specs=[pl.BlockSpec((local, cols), lambda m: (m, 0))] * nb,
        out_shape=[jax.ShapeDtypeStruct((micros * local, cols), BF)] * nb,
        compiler_params=params(),
        cost_estimate=cost(1e6, 6e6),
        name="split_by_core",
    )(place, grad)


def qkv_grad_kernel(place_ref, *refs, nb, n):
    h_refs, ga_refs = refs[:nb], refs[nb : 2 * nb]
    a_send_ref, a_keep_ref, b_send_ref, b_keep_ref, ht_ref = refs[2 * nb :]
    first = n // 8
    _, _, kh, fb = a_send_ref.shape

    @pl.when(pl.program_id(0) == 0)
    def _():
        for k in range(nb):
            relative_transpose(h_refs[k], ht_ref, k, place_ref[2 * n + 1], n)

    y = None
    for k in range(nb):
        term = nn(ht_ref[k], ga_refs[k][...])
        y = term if y is None else y + term
    y = y.astype(BF).reshape(4, 2 * first, 2, kh, fb)
    for z in range(4):
        for i in range(first):
            at = z * first + i
            a_send_ref[at, 0] = y[z, first + i, 0]
            a_keep_ref[at, 0] = y[z, i, 0]
            b_send_ref[at, 0] = y[z, 2 * i + 1, 1]
            b_keep_ref[at, 0] = y[z, 2 * i, 1]


def qkv_grad(place, h, ga, n):
    nb = len(h)
    rows, width = h[0].shape
    fb = ga[0].shape[1] // 3
    kh = width // n // 2
    half = jax.ShapeDtypeStruct((n // 2, 3, kh, fb), BF)
    return pl.pallas_call(
        functools.partial(qkv_grad_kernel, nb=nb, n=n),
        grid=(3,),
        in_specs=[SMEM]
        + [constant((rows, width))] * nb
        + [pl.BlockSpec((rows, fb), lambda t: (0, t))] * nb,
        out_specs=[pl.BlockSpec((n // 2, 1, kh, fb), lambda t: (0, t, 0, 0))] * 4,
        out_shape=[half] * 4,
        scratch_shapes=[pltpu.VMEM((nb, width, rows), BF)],
        compiler_params=params(),
        cost_estimate=cost(6 * rows * width * width, 15e6),
        name="qkv_grad",
    )(place, *h, *ga)


def input_grad_kernel(place_ref, x_ref, gain_ref, dmid_ref, *refs, nb):
    grad_refs = refs[:nb]
    *pieces, _, out_ref, d_gain_ref, d_shift_ref, dh_ref, wa_ref, wb_ref, sems = refs[nb:]
    step = pl.program_id(0)

    @pl.when(step == 0)
    def _():
        finish(load_pieces(pieces, wa_ref, wb_ref, sems))

    total = None
    for k in range(nb):
        term = nt(grad_refs[k][...], qkv_block(k, step, place_ref, wa_ref, wb_ref))
        total = term if total is None else total + term

    @pl.when(step == 0)
    def _():
        dh_ref[...] = total

    @pl.when(step > 0)
    def _():
        dh_ref[...] += total

    @pl.when(step == pl.num_programs(0) - 1)
    def _():
        dh = dh_ref[...]
        xhat, rstd = norm_stats(x_ref[...].astype(F32))
        d_gain_ref[...] = jnp.sum(dh * xhat, axis=0, keepdims=True)
        d_shift_ref[...] = jnp.sum(dh, axis=0, keepdims=True)
        d = dh * gain_ref[...]
        inner = d - jnp.mean(d, axis=-1, keepdims=True) - xhat * jnp.mean(d * xhat, axis=-1, keepdims=True)
        out_ref[...] = dmid_ref[...] + rstd * inner


def input_grad(place, grads, pieces, x, gain, dmid, earlier, n):
    rows, width = x.shape
    nb = len(grads)
    fb = pieces[0].shape[-1]
    vector = jax.ShapeDtypeStruct((1, width), F32)
    return pl.pallas_call(
        functools.partial(input_grad_kernel, nb=nb),
        grid=(3,),
        in_specs=[SMEM, constant((rows, width)), constant((1, width)), constant((rows, width))]
        + [pl.BlockSpec((rows, fb), lambda t: (0, t))] * nb
        + [pl.BlockSpec(memory_space=pl.ANY)] * (len(pieces) + 1),
        out_specs=[constant((rows, width)), constant((1, width)), constant((1, width))],
        out_shape=[jax.ShapeDtypeStruct((rows, width), F32), vector, vector],
        scratch_shapes=[pltpu.VMEM((rows, width), F32)] + piece_scratch(pieces, nb, n),
        compiler_params=params(),
        cost_estimate=cost(6 * rows * width * width, 20e6),
        name="input_grad",
    )(place, x, gain, dmid, *grads, *pieces, earlier)


def swap_with(value, axis, k):
    size = lax.axis_size(axis)
    return lax.ppermute(value, axis, [(i, i ^ k) for i in range(size)])


def powers(size):
    return [1 << i for i in range(size.bit_length() - 1)]


def direct(shard, n):
    return [swap_with(shard, "seq", k * n // 4) for k in range(1, 4)]


def planes(n):
    quarter = n // 4
    return [[z * quarter + i for i in range(quarter)] for z in range(4)]


def lines(n):
    return [list(group) for group in zip(*planes(n))]


def gather_line(shard, n):
    return lax.all_gather(shard, "seq", axis_index_groups=lines(n))


def gather_plane(line, n):
    plane = lax.all_gather(line, "seq", axis_index_groups=planes(n))
    return plane.reshape((n,) + line.shape[1:])


def scatter_groups(grad, groups):
    return lax.psum_scatter(grad, "seq", scatter_dimension=0, axis_index_groups=groups)


def halves(shard, arrived):
    both = jnp.stack([shard] + arrived)
    return both[:, 0], both[:, 1]


def together(*values):
    return lax.optimization_barrier(values)


def gather_cores(pieces, nb):
    out = list(pieces)
    for k in range(1, nb):
        out += [swap_with(piece, "batch", k) for piece in pieces]
    return out


def place_of(relative, bits, n):
    place = relative // (n // 4)
    for i, bit in enumerate(bits):
        place = place + jnp.where(relative & bit, 4 << i, 0)
    return place


def place_table(position, core, n):
    relative = jnp.arange(n, dtype=jnp.int32) ^ position
    bits = powers(n // 4)
    ends = jnp.stack([core, position]).astype(jnp.int32)
    return jnp.concatenate([place_of(relative, bits, n), place_of(relative, bits[::-1], n), ends])


def plus(value, arrived):
    return (value.astype(F32) + arrived.astype(F32)).astype(BF)


def reduce_first(a_send, b_send, n):
    return swap_with(a_send, "seq", n // 8), swap_with(b_send, "seq", 1)


def split_next(total):
    m = total.shape[1] // 2
    return total[:, :m], total[:, m:]


def reduce_steps(total, bit_of, n):
    total = total.reshape((4, n // 8) + total.shape[1:])
    while total.shape[1] > 1:
        keep, send = split_next(total)
        total = plus(keep, swap_with(send, "seq", bit_of(send.shape[1])))
    return total[:, 0]


def reduce_rest(a, b, n):
    a = reduce_steps(a, lambda m: m, n)
    b = reduce_steps(b, lambda m: 2 * m, n)
    return jnp.stack([a, b], axis=1)


def reduce_direct(total, n):
    return [swap_with(total[k], "seq", k * n // 4) for k in range(1, 4)]


def reduce_last(total, arrived):
    out = total[0].astype(F32)
    for term in arrived:
        out = out + term.astype(F32)
    return out[0], out[1]


def total_over(value, axis, steps):
    for k in steps:
        value = value + swap_with(value, axis, k)
    return value


def body(
    tokens,
    cotangent,
    lengths,
    random_blocks,
    query_key_value_weight,
    output_weight,
    up_weight,
    down_weight,
    out_bias,
    up_bias,
    down_bias,
    gain_attn,
    shift_attn,
    gain_ffn,
    shift_ffn,
):
    n = lax.axis_size("seq")
    nb = lax.axis_size("batch")
    position = lax.axis_index("seq")
    core = lax.axis_index("batch")
    micros, _, local, width = tokens.shape
    hidden = up_bias.shape[0]
    nblk = n * local // BLOCK
    bpd = local // BLOCK
    per = micros * H // n
    lanes = per * HD
    groups = H // per
    fb = width // nb
    kr = width // n
    kh = kr // 2
    fr = hidden // n
    per_b = hidden // width
    bits = powers(n // 4)
    row = lambda v: v.reshape(1, -1)
    place = place_table(position, core, n)

    shard = query_key_value_weight.reshape(2, kh, 3, fb).transpose(0, 2, 1, 3)
    stacked_up = up_weight.reshape(kr, per_b, fb).transpose(1, 0, 2).reshape(per_b * kr, fb)
    rest = jnp.concatenate([down_weight, stacked_up, output_weight])
    part_a, part_b = halves(shard, direct(shard, n))
    part_a, part_b, rest = together(part_a, part_b, rest)
    rest_line = gather_line(rest, n)
    for i, bit in enumerate(bits):
        found_a = swap_with(part_a, "seq", bit)
        found_b = swap_with(part_b, "seq", bits[-1 - i])
        if i < len(bits) - 1:
            part_a = jnp.concatenate([part_a, found_a])
            part_b = jnp.concatenate([part_b, found_b])
    qkv_pieces = gather_cores([part_a, found_a, part_b, found_b], nb)

    x = tokens.reshape(micros * local, width)
    g = cotangent.reshape(micros * local, width)
    micro = position * per // H
    head = position * per % H
    table = lax.dynamic_slice(
        random_blocks[:, 0], (micro, 0, head, 0), (1, nblk, per, NRAND)
    ).reshape(-1)
    limit = lax.dynamic_slice(lengths[:, 0], (micro,), (1,))

    def swap(value):
        return lax.all_to_all(value, "seq", split_axis=0, concat_axis=0, tiled=True)

    def over_cores(value):
        return [value] + [swap_with(value, "batch", k) for k in range(1, nb)]

    def columns_over_cores(value, cols):
        mine = lambda c: lax.dynamic_slice_in_dim(value, c * cols, cols, axis=1)
        return [mine(core)] + [swap_with(mine(core ^ k), "batch", k) for k in range(1, nb)]

    qkv, h1 = project(place, x, row(gain_attn), row(shift_attn), qkv_pieces, nb, n, micros, local, lanes)
    qkv, rest_line = together(qkv, rest_line)
    rest_plane = gather_plane(rest_line, n)
    qkv_all = swap(qkv.reshape(n, 3, local, lanes)).reshape(n, 3, bpd, BLOCK, lanes)
    g_cores, h1_cores = columns_over_cores(g, fb), over_cores(h1)
    qkv_all, g_cores, h1_cores = together(qkv_all, g_cores, h1_cores)
    mixed, lse = attend(qkv_all, table, limit, per)
    o = swap(mixed.reshape(n, local, lanes)).reshape(micros, groups, local, lanes)
    o, rest_plane = together(o, rest_plane)
    rest_pieces = gather_cores([rest_plane], nb)
    (
        result,
        dmid,
        branch,
        dout,
        att,
        h2,
        act,
        pre_grad,
        d_out_bias,
        d_up_bias,
        d_down_bias,
        d_gain_ffn,
        d_shift_ffn,
    ) = middle(
        nb,
        n,
        place,
        o,
        x,
        g,
        rest_pieces,
        row(out_bias),
        row(up_bias),
        row(down_bias),
        row(gain_ffn),
        row(shift_ffn),
    )
    dout_all = swap(dout.reshape(n, local, lanes)).reshape(n, bpd, BLOCK, lanes)

    rest_grad = ffn_grads(
        over_cores(act),
        g_cores,
        over_cores(h2),
        [pre_grad] + [swap_with(pre_grad[k : k + 1], "batch", k) for k in range(1, nb)],
        over_cores(att),
        columns_over_cores(branch, fb),
        n,
    )
    dout_all, rest_grad = together(dout_all, rest_grad)
    rest_line = scatter_groups(rest_grad, planes(n))
    grads = attend_back(qkv_all, dout_all, lse, table, limit, per)
    grads_back = swap(grads.reshape(n, 3, local, lanes)).reshape(micros, groups, 3, local, lanes)
    own_grads = split_by_core(place, grads_back, nb, n)
    grad_cores = [own_grads[0]] + [swap_with(own_grads[k], "batch", k) for k in range(1, nb)]
    a_send, a_keep, b_send, b_keep = qkv_grad(place, h1_cores, grad_cores, n)
    a_keep, rest_line = together(a_keep, rest_line)
    grad_rest = scatter_groups(rest_line, lines(n)).astype(F32)
    first_a, first_b = reduce_first(a_send, b_send, n)
    grad_x, d_gain_attn, d_shift_attn = input_grad(
        place, own_grads, qkv_pieces, x, row(gain_attn), dmid, a_keep, n
    )
    vectors = [d_out_bias, d_up_bias, d_down_bias, d_gain_attn, d_shift_attn, d_gain_ffn, d_shift_ffn]
    sums = jnp.concatenate(vectors, axis=1)
    sums, first_a, first_b = together(sums, first_a, first_b)
    qkv_reduced = reduce_rest(plus(a_keep, first_a), plus(b_keep, first_b), n)
    sums = total_over(total_over(sums, "batch", powers(nb)), "seq", powers(n // 4))
    qkv_reduced, sums = together(qkv_reduced, sums)
    grad_down = grad_rest[:fr]
    grad_up = grad_rest[fr:-kr].reshape(per_b, kr, fb).transpose(1, 0, 2).reshape(kr, per_b * fb)
    grad_out = grad_rest[-kr:]
    arrived = reduce_direct(qkv_reduced, n)
    near, far, diagonal = direct(sums, n)
    *arrived, grad_down, grad_up, grad_out = together(*arrived, grad_down, grad_up, grad_out)
    grad_a, grad_b = reduce_last(qkv_reduced, arrived)
    grad_qkv = jnp.stack([grad_a, grad_b]).transpose(0, 2, 1, 3).reshape(kr, 3 * fb)
    sums = ((sums + near) + (far + diagonal))[0]
    ends = []
    for vector in vectors[:-1]:
        ends.append((ends[-1] if ends else 0) + vector.shape[1])
    return (
        result.reshape(tokens.shape),
        grad_x.reshape(tokens.shape),
        grad_qkv,
        grad_out,
        grad_up,
        grad_down,
        *jnp.split(sums, ends),
    )


def solution(mesh):
    rows = P(None, "batch", "seq", None)
    weight = P("seq", "batch")
    return jax.shard_map(
        body,
        mesh=mesh,
        in_specs=(rows, rows, P(None, "batch"), P(None, "batch", None, None, None))
        + (weight,) * 4
        + (P(),) * 7,
        out_specs=(rows, rows) + (weight,) * 4 + (P(),) * 7,
        check_vma=False,
    )
```

```python
import functools

import jax
import jax.numpy as jnp
from jax import lax
from jax.experimental import pallas as pl
from jax.experimental.pallas import tpu as pltpu
from jax.sharding import PartitionSpec as P

H = 16
HD = 64
BLOCK = 64
NGLOB = 2
NRAND = 3

EPS = 1e-05
BIG = 1e30
SCALE = HD ** (-0.5)
GELU_C = 0.7978845608028654
GELU_A = 0.044715
BF = jnp.bfloat16
F32 = jnp.float32
VMEM_LIMIT = 56 * 1024 * 1024

WHOLE = pl.BlockSpec(memory_space=pltpu.VMEM)
SMEM = pl.BlockSpec(memory_space=pltpu.SMEM)


def nn(a, b):
    return lax.dot_general(a, b, (((1,), (0,)), ((), ())), preferred_element_type=F32)


def nt(a, b):
    return lax.dot_general(a, b, (((1,), (1,)), ((), ())), preferred_element_type=F32)


def tn(a, b):
    return lax.dot_general(a, b, (((0,), (0,)), ((), ())), preferred_element_type=F32)


def params():
    return pltpu.CompilerParams(vmem_limit_bytes=VMEM_LIMIT)


def cost(flops, nbytes, trans=0):
    return pl.CostEstimate(flops=int(flops), bytes_accessed=int(nbytes), transcendentals=int(trans))


def constant(shape):
    return pl.BlockSpec(shape, lambda i: (0,) * len(shape))


def norm_stats(value):
    centre = jnp.mean(value, axis=-1, keepdims=True)
    centered = value - centre
    spread = jnp.mean(centered * centered, axis=-1, keepdims=True)
    rstd = lax.rsqrt(spread + EPS)
    return centered * rstd, rstd


def load_pieces(refs, wa_ref, wb_ref, sems):
    parts = len(refs) // wa_ref.shape[0]
    copies = []
    at = 0
    for i, ref in enumerate(refs):
        if i % (parts // 2) == 0:
            at = 0
        target = (wa_ref, wb_ref)[i % parts // (parts // 2)].at[i // parts, pl.ds(at, ref.shape[0])]
        at += ref.shape[0]
        copies.append(pltpu.make_async_copy(ref, target, sems.at[i]))
    for copy in copies:
        copy.start()
    return copies


def finish(copies):
    for copy in copies:
        copy.wait()


def qkv_block(core, part, place_ref, wa_ref, wb_ref):
    n = wa_ref.shape[1]
    rows = []
    for s in range(n):
        rows.append(wa_ref[core, place_ref[s], part])
        rows.append(wb_ref[core, place_ref[n + s], part])
    return jnp.concatenate(rows, axis=0)


def piece_scratch(pieces, nb, n):
    full = (nb, n) + pieces[0].shape[1:]
    return [pltpu.VMEM(full, BF), pltpu.VMEM(full, BF), pltpu.SemaphoreType.DMA((len(pieces),))]


def project_kernel(place_ref, x_ref, gain_ref, shift_ref, *refs, micros, local, lanes):
    *pieces, qkv_ref, h_ref, wa_ref, wb_ref, sems = refs
    fb = wa_ref.shape[4]

    @pl.when(pl.program_id(0) == 0)
    def _():
        copies = load_pieces(pieces, wa_ref, wb_ref, sems)
        xhat, _ = norm_stats(x_ref[...].astype(F32))
        h_ref[...] = (xhat * gain_ref[...] + shift_ref[...]).astype(BF)
        finish(copies)

    core = (pl.program_id(0) // 3) ^ place_ref[2 * wa_ref.shape[1]]
    y = nn(h_ref[...], qkv_block(core, pl.program_id(0) % 3, place_ref, wa_ref, wb_ref)).astype(BF)
    for m in range(micros):
        for i in range(fb // lanes):
            qkv_ref[m, i, 0] = y[m * local : (m + 1) * local, i * lanes : (i + 1) * lanes]


def project(place, x, gain, shift, pieces, nb, n, micros, local, lanes):
    fb = pieces[0].shape[-1]
    rows, width = x.shape
    groups = width // lanes
    kernel = functools.partial(project_kernel, micros=micros, local=local, lanes=lanes)
    return pl.pallas_call(
        kernel,
        grid=(3 * nb,),
        in_specs=[SMEM, constant((rows, width)), constant((1, width)), constant((1, width))]
        + [pl.BlockSpec(memory_space=pl.ANY)] * len(pieces),
        out_specs=[
            pl.BlockSpec((micros, fb // lanes, 1, local, lanes), lambda g: (0, g % nb, g // nb, 0, 0)),
            constant((rows, width)),
        ],
        out_shape=[
            jax.ShapeDtypeStruct((micros, groups, 3, local, lanes), BF),
            jax.ShapeDtypeStruct((rows, width), BF),
        ],
        scratch_shapes=piece_scratch(pieces, nb, n),
        compiler_params=params(),
        cost_estimate=cost(6 * rows * width * width, 14 * width * width),
        name="project",
    )(place, x, gain, shift, *pieces)


def lane_item(shape):
    return lax.broadcasted_iota(jnp.int32, shape, len(shape) - 1) // HD


def block_diagonal(value, per):
    if per == 1:
        return value
    item = lane_item(value.shape)
    zero = jnp.zeros_like(value)
    return jnp.concatenate([jnp.where(item == i, value, zero) for i in range(per)], axis=0)


def take_diagonal(full, per):
    if per == 1:
        return full
    item = lane_item((BLOCK, full.shape[1]))
    out = full[:BLOCK]
    for i in range(1, per):
        out = jnp.where(item == i, full[i * BLOCK : (i + 1) * BLOCK], out)
    return out


def pick(ref, part, blocks, bpd):
    out = ref[blocks[0] // bpd, part, blocks[0] % bpd]
    item = lane_item(out.shape)
    for i in range(1, len(blocks)):
        out = jnp.where(item == i, ref[blocks[i] // bpd, part, blocks[i] % bpd], out)
    return out


def key_lists(b, table_ref, limit, nblk, per):
    penalty = lambda ok: jnp.where(ok, 0.0, -BIG)
    shared = [0, 1, b - 1, b, jnp.minimum(b + 1, nblk - 1)]
    lists = [[s] for s in shared]
    inside = lambda block: block * BLOCK < limit
    biases = [None, None, penalty(inside(b - 1)), penalty(inside(b)), penalty(inside(b + 1) & (b + 1 < nblk))]
    biases = [[bias] * per for bias in biases]
    for r in range(NRAND):
        blocks = [table_ref[b * per * NRAND + i * NRAND + r] for i in range(per)]
        lists.append(blocks)
        biases.append([penalty(inside(block)) for block in blocks])
    return lists, biases


def add_biases(s, biases):
    item = lane_item((1, s.shape[1]))
    parts = []
    for j, bias in enumerate(biases):
        part = s[j * BLOCK : (j + 1) * BLOCK]
        if bias[0] is not None:
            row = bias[0]
            for i in range(1, len(bias)):
                row = row if bias[i] is bias[0] else jnp.where(item == i, bias[i], row)
            part = part + row
        parts.append(part)
    return jnp.concatenate(parts, axis=0)


def global_keys(ref, part, c, bpd, chunk):
    span = chunk // (bpd * BLOCK)
    return ref[pl.ds(c * span, span), part].reshape(chunk, ref.shape[4])


def to_row(square):
    eye = lax.broadcasted_iota(jnp.int32, square.shape, 0) == lax.broadcasted_iota(jnp.int32, square.shape, 1)
    return jnp.sum(jnp.where(eye, square, 0.0), axis=0, keepdims=True)


def with_ones(values):
    return jnp.concatenate([values, jnp.ones_like(values)], axis=1)


def fold(value, width, combine):
    out = value[:, :width]
    for at in range(width, value.shape[1], width):
        out = combine(out, value[:, at : at + width])
    return out


def attend_kernel(table_ref, limit_ref, qkv_ref, out_ref, lse_ref, s_ref, *, per, bpd, nblk):
    limit = limit_ref[0]
    lanes = per * HD
    rows = per * BLOCK
    chunk = 2 * bpd * BLOCK
    chunks = nblk * BLOCK // chunk
    tile = 2 * BLOCK

    def query(b):
        q = qkv_ref[b // bpd, 0, b % bpd] * jnp.asarray(SCALE, BF)
        return block_diagonal(q, per)

    both = jnp.concatenate([query(g) for g in range(NGLOB)], axis=0)
    key_id = lax.broadcasted_iota(jnp.int32, (1, chunk), 1)

    def score(c, top):
        s = nt(both, global_keys(qkv_ref, 1, c, bpd, chunk))
        s = s + jnp.where(c * chunk + key_id < limit, 0.0, -BIG)
        s_ref[c] = s
        return jnp.maximum(top, fold(s, tile, jnp.maximum))

    top = lax.fori_loop(0, chunks, score, jnp.full((NGLOB * rows, tile), -BIG, F32))
    top = jnp.max(top, axis=1, keepdims=True)

    def mix(c, acc):
        p = jnp.exp(s_ref[c] - top)
        return acc + nn(p.astype(BF), with_ones(global_keys(qkv_ref, 2, c, bpd, chunk)))

    acc = lax.fori_loop(0, chunks, mix, jnp.zeros((NGLOB * rows, 2 * lanes), F32))
    lse = top + jnp.log(acc[:, lanes:])
    acc = acc[:, :lanes] * (1.0 / acc[:, lanes:])
    for g in range(NGLOB):
        at = slice(g * rows, (g + 1) * rows)
        lse_ref[pl.ds(g, 1), :] = to_row(lse[at])
        out_ref[g // bpd, g % bpd] = take_diagonal(acc[at], per).astype(BF)

    def sparse(b, carry):
        lists, biases = key_lists(b, table_ref, limit, nblk, per)
        keys = jnp.concatenate([pick(qkv_ref, 1, blocks, bpd) for blocks in lists], axis=0)
        values = jnp.concatenate([pick(qkv_ref, 2, blocks, bpd) for blocks in lists], axis=0)
        s = nt(query(b), keys)
        which = lax.broadcasted_iota(jnp.int32, (1, tile), 1) < BLOCK
        parts = []
        for i in range(per):
            for j in range(0, len(lists), 2):
                part = s[i * BLOCK : (i + 1) * BLOCK, j * BLOCK : (j + 2) * BLOCK]
                one, two = biases[j][i], biases[j + 1][i]
                if one is not None or two is not None:
                    part = part + jnp.where(which, 0.0 if one is None else one, 0.0 if two is None else two)
                parts.append(part)
        half = len(lists) // 2
        s = [jnp.concatenate([parts[i * half + j] for i in range(per)], axis=0) for j in range(half)]
        top = jnp.max(functools.reduce(jnp.maximum, s), axis=1, keepdims=True)
        p = [jnp.exp(part - top) for part in s]
        mixed = nn(jnp.concatenate([part.astype(BF) for part in p], axis=1), with_ones(values))
        sums = mixed[:, lanes:]
        lse_ref[pl.ds(b, 1), :] = to_row(top + jnp.log(sums))
        out_ref[b // bpd, b % bpd] = take_diagonal(mixed[:, :lanes] * (1.0 / sums), per).astype(BF)
        return carry

    for b in range(NGLOB, 4):
        sparse(b, 0)
    lax.fori_loop(4, nblk, sparse, 0, unroll=4)


def attend(qkv, table, limit, per):
    n, _, bpd, _, lanes = qkv.shape
    nblk = n * bpd
    kernel = functools.partial(attend_kernel, per=per, bpd=bpd, nblk=nblk)
    return pl.pallas_call(
        kernel,
        in_specs=[SMEM, SMEM, WHOLE],
        out_specs=[WHOLE, WHOLE],
        out_shape=[
            jax.ShapeDtypeStruct((n, bpd, BLOCK, lanes), BF),
            jax.ShapeDtypeStruct((nblk, lanes), F32),
        ],
        scratch_shapes=[pltpu.VMEM((n // 2, NGLOB * per * BLOCK, 2 * bpd * BLOCK), F32)],
        compiler_params=params(),
        cost_estimate=cost(40e9, 4e6, 1e7),
        name="attend",
    )(table, limit, qkv)


def attend_back_kernel(
    table_ref, limit_ref, qkv_ref, dout_ref, lse_ref, grad_ref, dk_ref, dv_ref, w_ref, dw_ref, *, per, bpd, nblk
):
    limit = limit_ref[0]
    lanes = per * HD
    chunk = 2 * bpd * BLOCK
    span = 2
    chunks = nblk * BLOCK // chunk
    scale_low = jnp.asarray(SCALE, BF)

    def query(b):
        return block_diagonal(qkv_ref[b // bpd, 0, b % bpd] * scale_low, per)

    def upstream(b):
        return block_diagonal(dout_ref[b // bpd, b % bpd], per)

    both = jnp.concatenate([query(g) for g in range(NGLOB)], axis=0)
    dboth = jnp.concatenate([upstream(g) for g in range(NGLOB)], axis=0)
    lse = jnp.concatenate([lse_ref[pl.ds(g, 1), :] for g in range(NGLOB)], axis=1)
    rowid = lax.broadcasted_iota(jnp.int32, (chunk, NGLOB * lanes), 0)

    def first(c, centre):
        s = nt(global_keys(qkv_ref, 1, c, bpd, chunk), both)
        s = jnp.where(c * chunk + rowid < limit, s, -BIG)
        w = jnp.exp(s - lse)
        dw = nt(global_keys(qkv_ref, 2, c, bpd, chunk), dboth)
        w_ref[pl.ds(c * chunk, chunk), :] = w
        dw_ref[pl.ds(c * chunk, chunk), :] = dw
        return centre + jnp.sum(w * dw, axis=0, keepdims=True)

    centre = lax.fori_loop(0, chunks, first, jnp.zeros((1, NGLOB * lanes), F32))

    def second(c, acc):
        w = w_ref[pl.ds(c * chunk, chunk), :]
        ds = (w * (dw_ref[pl.ds(c * chunk, chunk), :] - centre)).astype(BF)
        dk_ref[pl.ds(c * span, span)] = nn(ds, both).reshape(span, bpd, BLOCK, lanes)
        dv_ref[pl.ds(c * span, span)] = nn(w.astype(BF), dboth).reshape(span, bpd, BLOCK, lanes)
        return acc + tn(ds, global_keys(qkv_ref, 1, c, bpd, chunk))

    acc = lax.fori_loop(0, chunks, second, jnp.zeros((NGLOB * lanes, lanes), F32))
    for g in range(NGLOB):
        dq = take_diagonal(acc[g * lanes : (g + 1) * lanes], per) * SCALE
        grad_ref[g // bpd, 0, g % bpd] = dq.astype(BF)

    def sparse(b, carry):
        lists, biases = key_lists(b, table_ref, limit, nblk, per)
        keys = jnp.concatenate([pick(qkv_ref, 1, blocks, bpd) for blocks in lists], axis=0)
        values = jnp.concatenate([pick(qkv_ref, 2, blocks, bpd) for blocks in lists], axis=0)
        q = query(b)
        do = upstream(b)
        zero = jnp.zeros_like(q)
        sides = jnp.concatenate(
            [jnp.concatenate([q, zero], axis=1), jnp.concatenate([zero, do], axis=1)], axis=0
        )
        both_scores = nt(jnp.concatenate([keys, values], axis=1), sides)
        s = add_biases(both_scores[:, : q.shape[0]], biases)
        dw = both_scores[:, q.shape[0] :]
        w = jnp.exp(s - lse_ref[pl.ds(b, 1), :])
        centre = jnp.sum(w * dw, axis=0, keepdims=True)
        ds = (w * (dw - centre)).astype(BF)
        grad_ref[b // bpd, 0, b % bpd] = (take_diagonal(tn(ds, keys), per) * SCALE).astype(BF)
        both_grads = nn(jnp.concatenate([ds, w.astype(BF)], axis=1), sides)
        dk, dv = both_grads[:, :lanes], both_grads[:, lanes:]
        item = lane_item((BLOCK, lanes))
        for ref, full in ((dk_ref, dk), (dv_ref, dv)):
            for k, blocks in enumerate(lists):
                part = full[k * BLOCK : (k + 1) * BLOCK]
                for i, block in enumerate(blocks):
                    term = part if len(blocks) == 1 else jnp.where(item == i, part, 0.0)
                    ref[block // bpd, block % bpd] += term
        return carry

    for b in range(NGLOB, 4):
        sparse(b, 0)
    lax.fori_loop(4, nblk, sparse, 0, unroll=4)

    def finish(c, carry):
        grad_ref[c, 1] = dk_ref[c].astype(BF)
        grad_ref[c, 2] = dv_ref[c].astype(BF)
        return carry

    lax.fori_loop(0, nblk // bpd, finish, 0)


def attend_back(qkv, dout, lse, table, limit, per):
    n, _, bpd, _, lanes = qkv.shape
    nblk = n * bpd
    kernel = functools.partial(attend_back_kernel, per=per, bpd=bpd, nblk=nblk)
    return pl.pallas_call(
        kernel,
        in_specs=[SMEM, SMEM, WHOLE, WHOLE, WHOLE],
        out_specs=WHOLE,
        out_shape=jax.ShapeDtypeStruct((n, 3, bpd, BLOCK, lanes), BF),
        scratch_shapes=[
            pltpu.VMEM((n, bpd, BLOCK, lanes), F32),
            pltpu.VMEM((n, bpd, BLOCK, lanes), F32),
            pltpu.VMEM((nblk * BLOCK, NGLOB * lanes), F32),
            pltpu.VMEM((nblk * BLOCK, NGLOB * lanes), F32),
        ],
        compiler_params=params(),
        cost_estimate=cost(80e9, 8e6, 1e7),
        name="attend_back",
    )(table, limit, qkv, dout, lse)


MIDDLE_REFS = 16


def rest_places(n):
    return [s % (n // 4) * 4 + s // (n // 4) for s in range(n)]


def middle_kernel(
    place_ref,
    o_ref,
    x_ref,
    g_ref,
    out_bias_ref,
    up_bias_ref,
    down_bias_ref,
    gain_ref,
    shift_ref,
    *refs,
    local,
    lanes,
):
    *pieces, w_ref, sems = refs
    count = len(pieces) - MIDDLE_REFS
    pieces, others = pieces[:count], pieces[count:]
    (
    result_ref,
    dmid_ref,
    branch_ref,
    dout_ref,
    att_ref,
    h_ref,
    act_ref,
    pre_grad_ref,
    d_out_bias_ref,
    d_up_bias_ref,
    d_down_bias_ref,
    d_gain_ref,
    d_shift_ref,
    mid_ref,
    acc_ref,
    dh_ref,
    ) = others
    step = pl.program_id(0)
    micros, groups = o_ref.shape[:2]
    nb, n, height, fb = w_ref.shape
    width = x_ref.shape[1]
    kr = width // n
    per_b = pl.num_programs(0) // nb
    fr = per_b * kr
    nd = fb // fr
    me_core = place_ref[2 * n]
    at = rest_places(n)

    def out_block(b):
        rows = [w_ref[b ^ me_core, at[s], 2 * fr :] for s in range(n)]
        return jnp.concatenate(rows, axis=0)

    def down_block(b):
        rows = []
        for h in range(nd):
            s = step * nd + h
            rows.append(w_ref[b ^ me_core, s % (n // 4) * 4 + s // (n // 4), :fr])
        return jnp.concatenate(rows, axis=0)

    def up_block():
        core = (step // per_b) ^ me_core
        rows = pl.ds(pl.multiple_of(fr + step % per_b * kr, kr), kr)
        return jnp.concatenate([w_ref[core, at[s], rows] for s in range(n)], axis=0)

    def copies(part, rows):
        found = []
        for k, piece in enumerate(pieces):
            copy = pltpu.make_async_copy(piece.at[:, rows], w_ref.at[k, :, rows], sems.at[part, k])
            copy.start()
            found.append(copy)
        return found

    @pl.when(step == 0)
    def _():
        first = copies(0, pl.ds(2 * fr, kr))
        rest = copies(1, pl.ds(0, 2 * fr))
        for m in range(micros):
            for i in range(groups):
                att_ref[m * local : (m + 1) * local, i * lanes : (i + 1) * lanes] = o_ref[m, i]
        for copy in first:
            copy.wait()
        att = att_ref[...]
        for b in range(nb):
            cols = slice(b * fb, (b + 1) * fb)
            y = nn(att, out_block(b))
            mid_ref[:, cols] = x_ref[:, cols].astype(F32) + y + out_bias_ref[:, cols]
        mid = mid_ref[...]
        xhat, _ = norm_stats(mid)
        h_ref[...] = (xhat * gain_ref[...] + shift_ref[...]).astype(BF)
        acc_ref[...] = mid + down_bias_ref[...]
        dh_ref[...] = jnp.zeros_like(dh_ref)
        d_down_bias_ref[...] = jnp.sum(g_ref[...].astype(F32), axis=0, keepdims=True)
        for copy in rest:
            copy.wait()

    up = up_block()
    pre = nn(h_ref[...], up) + up_bias_ref[...]
    square = pre * pre
    gate = jnp.tanh(GELU_C * pre * (1.0 + GELU_A * square))
    half = 0.5 * (1.0 + gate)
    act = (pre * half).astype(BF)
    slope = half + 0.5 * pre * (1.0 - gate * gate) * (GELU_C * (1.0 + 3.0 * GELU_A * square))
    act_ref[...] = act
    dact = None
    for b in range(nb):
        cols = slice(b * fb, (b + 1) * fb)
        term = nt(g_ref[:, cols], down_block(b))
        dact = term if dact is None else dact + term
    pre_grad = (dact * slope).astype(BF)
    pre_grad_ref[0] = pre_grad
    d_up_bias_ref[...] = jnp.sum(pre_grad.astype(F32), axis=0, keepdims=True)
    for b in range(nb):
        cols = slice(b * fb, (b + 1) * fb)
        acc_ref[:, cols] += nn(act, down_block(b))
    dh_ref[...] += nt(pre_grad, up)

    @pl.when(step == pl.num_programs(0) - 1)
    def _():
        result_ref[...] = acc_ref[...].astype(BF)
        dh = dh_ref[...]
        xhat, rstd = norm_stats(mid_ref[...])
        d_gain_ref[...] = jnp.sum(dh * xhat, axis=0, keepdims=True)
        d_shift_ref[...] = jnp.sum(dh, axis=0, keepdims=True)
        d = dh * gain_ref[...]
        inner = d - jnp.mean(d, axis=-1, keepdims=True) - xhat * jnp.mean(d * xhat, axis=-1, keepdims=True)
        dmid = g_ref[...].astype(F32) + rstd * inner
        dmid_ref[...] = dmid
        branch = dmid.astype(BF)
        branch_ref[...] = branch
        d_out_bias_ref[...] = jnp.sum(branch.astype(F32), axis=0, keepdims=True)
        dout = None
        for b in range(nb):
            term = nt(branch[:, b * fb : (b + 1) * fb], out_block(b))
            dout = term if dout is None else dout + term
        dout = dout.astype(BF)
        for m in range(micros):
            for i in range(groups):
                dout_ref[m, i] = dout[m * local : (m + 1) * local, i * lanes : (i + 1) * lanes]


def middle(nb, n, place, o, x, g, pieces, out_bias, up_bias, down_bias, gain, shift):
    micros, groups, local, lanes = o.shape
    rows, width = x.shape
    fb = pieces[0].shape[-1]
    hidden = up_bias.shape[1]
    steps = hidden // fb
    per_b = steps // nb
    full = lambda dtype: jax.ShapeDtypeStruct((rows, width), dtype)
    vector = jax.ShapeDtypeStruct((1, width), F32)
    whole = lambda shape: pl.BlockSpec(shape, lambda i, place: (0,) * len(shape))
    kernel = functools.partial(middle_kernel, local=local, lanes=lanes)
    return pl.pallas_call(
        kernel,
        grid_spec=pltpu.PrefetchScalarGridSpec(
        num_scalar_prefetch=1,
        grid=(steps,),
        in_specs=[
            whole((micros, groups, local, lanes)),
            whole((rows, width)),
            whole((rows, width)),
            whole((1, width)),
            pl.BlockSpec((1, fb), lambda i, place: (0, i)),
            whole((1, width)),
            whole((1, width)),
            whole((1, width)),
        ]
        + [pl.BlockSpec(memory_space=pl.ANY)] * len(pieces),
        out_specs=[
            whole((rows, width)),
            whole((rows, width)),
            whole((rows, width)),
            whole((micros, groups, local, lanes)),
            whole((rows, width)),
            whole((rows, width)),
            pl.BlockSpec((rows, fb), lambda i, place: (0, i)),
            pl.BlockSpec((1, rows, fb), lambda i, place: ((i // per_b) ^ place[2 * n], 0, i % per_b)),
            whole((1, width)),
            pl.BlockSpec((1, fb), lambda i, place: (0, i)),
            whole((1, width)),
            whole((1, width)),
            whole((1, width)),
        ],
    scratch_shapes=[pltpu.VMEM((rows, width), F32)] * 3 + [pltpu.VMEM((nb,) + pieces[0].shape, BF), pltpu.SemaphoreType.DMA((2, nb))],
        ),
        out_shape=[
            full(BF),
            full(F32),
            full(BF),
            jax.ShapeDtypeStruct((micros, groups, local, lanes), BF),
            full(BF),
            full(BF),
            jax.ShapeDtypeStruct((rows, hidden), BF),
            jax.ShapeDtypeStruct((nb, rows, hidden // nb), BF),
            vector,
            jax.ShapeDtypeStruct((1, hidden), F32),
            vector,
            vector,
            vector,
        ],
        compiler_params=params(),
        cost_estimate=cost(8 * rows * width * hidden + 4 * rows * width * width, 50e6),
        name="middle",
    )(place, o, x, g, out_bias, up_bias, down_bias, gain, shift, *pieces)


def relative_transpose(ref, target_ref, k, me, n):
    kr = target_ref.shape[1] // n
    value = ref[...].T
    for s in range(n):
        at = pl.ds(pl.multiple_of((s ^ me) * kr, kr), kr)
        target_ref[k, at, :] = value[s * kr : (s + 1) * kr]


def ffn_grads_kernel(*refs, nb):
    groups = [refs[i * nb : (i + 1) * nb] for i in range(6)]
    act_refs, gc_refs, h_refs, gp_refs, att_refs, br_refs = groups
    out_ref, ht_ref, at_ref = refs[6 * nb :]
    step = pl.program_id(0)
    count, _, height, fb = out_ref.shape
    fr = act_refs[0].shape[1] // count
    per_b = gp_refs[0].shape[2] // fb
    kr = (height - fr) // (per_b + 1)

    @pl.when(step == 0)
    def _():
        for k in range(nb):
            ht_ref[k] = h_refs[k][...].T
            at_ref[k] = att_refs[k][...].T

    at = pl.ds(pl.multiple_of(step * count * kr, count * kr), count * kr)
    down, up, out = 0.0, 0.0, 0.0
    for k in range(nb):
        down += nn(act_refs[k][...].T, gc_refs[k][...])
        up += nn(ht_ref[k, at, :], gp_refs[k][0])
        out += nn(at_ref[k, at, :], br_refs[k][...])
    down, up, out = down.astype(BF), up.astype(BF), out.astype(BF)
    for i in range(count):
        out_ref[i, 0, :fr] = down[i * fr : (i + 1) * fr]
        for q in range(per_b):
            out_ref[i, 0, fr + q * kr : fr + (q + 1) * kr] = up[i * kr : (i + 1) * kr, q * fb : (q + 1) * fb]
        out_ref[i, 0, fr + per_b * kr :] = out[i * kr : (i + 1) * kr]


def ffn_grads(act, gc, h, gp, att, br, n):
    nb = len(act)
    rows, hidden = act[0].shape
    fb = gc[0].shape[1]
    width = h[0].shape[1]
    fr, kr = hidden // n, width // n
    per_b = hidden // nb // fb
    height = fr + (per_b + 1) * kr
    return pl.pallas_call(
        functools.partial(ffn_grads_kernel, nb=nb),
        grid=(4,),
        in_specs=[pl.BlockSpec((rows, hidden // 4), lambda i: (0, i))] * nb
        + [constant((rows, fb))] * nb
        + [constant((rows, width))] * nb
        + [constant((1, rows, hidden // nb))] * nb
        + [constant((rows, width))] * nb
        + [constant((rows, fb))] * nb,
        out_specs=pl.BlockSpec((n // 4, 1, height, fb), lambda i: (0, i, 0, 0)),
        out_shape=jax.ShapeDtypeStruct((n // 4, 4, height, fb), BF),
        scratch_shapes=[pltpu.VMEM((nb, width, rows), BF)] * 2,
        compiler_params=params(),
        cost_estimate=cost(4 * rows * width * hidden + 2 * rows * width * width, 40e6),
        name="ffn_grads",
    )(*act, *gc, *h, *gp, *att, *br)


def split_kernel(place_ref, grad_ref, *out_refs, n, lanes):
    groups = grad_ref.shape[1]
    core = place_ref[2 * n]
    count = out_refs[0].shape[1] // lanes
    for k, out_ref in enumerate(out_refs):
        for i in range(count):
            at = (core ^ k) * count + i
            out_ref[:, i * lanes : (i + 1) * lanes] = grad_ref[0, at % groups, at // groups]


def split_by_core(place, grad, nb, n):
    micros, groups, _, local, lanes = grad.shape
    cols = 3 * groups * lanes // nb
    return pl.pallas_call(
        functools.partial(split_kernel, n=n, lanes=lanes),
        grid=(micros,),
        in_specs=[SMEM, pl.BlockSpec((1, groups, 3, local, lanes), lambda m: (m, 0, 0, 0, 0))],
        out_specs=[pl.BlockSpec((local, cols), lambda m: (m, 0))] * nb,
        out_shape=[jax.ShapeDtypeStruct((micros * local, cols), BF)] * nb,
        compiler_params=params(),
        cost_estimate=cost(1e6, 6e6),
        name="split_by_core",
    )(place, grad)


def turn_kernel(place_ref, *refs, nb, n):
    for k in range(nb):
        relative_transpose(refs[k], refs[nb], k, place_ref[2 * n + 1], n)


def turn(place, h, n):
    nb = len(h)
    rows, width = h[0].shape
    return pl.pallas_call(
        functools.partial(turn_kernel, nb=nb, n=n),
        in_specs=[SMEM] + [WHOLE] * nb,
        out_specs=WHOLE,
        out_shape=jax.ShapeDtypeStruct((nb, width, rows), BF),
        compiler_params=params(),
        cost_estimate=cost(1e6, 4e6),
        name="turn",
    )(place, *h)


def qkv_grad_kernel(ht_ref, *refs, nb, n):
    ga_refs = refs[:nb]
    a_send_ref, a_keep_ref, b_send_ref, b_keep_ref = refs[nb:]
    first = n // 8
    _, _, kh, fb = a_send_ref.shape

    y = None
    for k in range(nb):
        term = nn(ht_ref[k], ga_refs[k][...])
        y = term if y is None else y + term
    y = y.astype(BF).reshape(4, 2 * first, 2, kh, fb)
    for z in range(4):
        for i in range(first):
            at = z * first + i
            a_send_ref[at, 0] = y[z, first + i, 0]
            a_keep_ref[at, 0] = y[z, i, 0]
            b_send_ref[at, 0] = y[z, 2 * i + 1, 1]
            b_keep_ref[at, 0] = y[z, 2 * i, 1]


def qkv_grad(turned, ga, n):
    nb, width, rows = turned.shape
    fb = ga[0].shape[1] // 3
    kh = width // n // 2
    half = jax.ShapeDtypeStruct((n // 2, 3, kh, fb), BF)
    return pl.pallas_call(
        functools.partial(qkv_grad_kernel, nb=nb, n=n),
        grid=(3,),
        in_specs=[constant((nb, width, rows))]
        + [pl.BlockSpec((rows, fb), lambda t: (0, t))] * nb,
        out_specs=[pl.BlockSpec((n // 2, 1, kh, fb), lambda t: (0, t, 0, 0))] * 4,
        out_shape=[half] * 4,
        compiler_params=params(),
        cost_estimate=cost(6 * rows * width * width, 15e6),
        name="qkv_grad",
    )(turned, *ga)


def input_grad_kernel(place_ref, x_ref, gain_ref, dmid_ref, *refs, nb):
    grad_refs = refs[:nb]
    *pieces, _, out_ref, d_gain_ref, d_shift_ref, dh_ref, wa_ref, wb_ref, sems = refs[nb:]
    step = pl.program_id(0)

    @pl.when(step == 0)
    def _():
        finish(load_pieces(pieces, wa_ref, wb_ref, sems))

    total = None
    for k in range(nb):
        term = nt(grad_refs[k][...], qkv_block(k, step, place_ref, wa_ref, wb_ref))
        total = term if total is None else total + term

    @pl.when(step == 0)
    def _():
        dh_ref[...] = total

    @pl.when(step > 0)
    def _():
        dh_ref[...] += total

    @pl.when(step == pl.num_programs(0) - 1)
    def _():
        dh = dh_ref[...]
        xhat, rstd = norm_stats(x_ref[...].astype(F32))
        d_gain_ref[...] = jnp.sum(dh * xhat, axis=0, keepdims=True)
        d_shift_ref[...] = jnp.sum(dh, axis=0, keepdims=True)
        d = dh * gain_ref[...]
        inner = d - jnp.mean(d, axis=-1, keepdims=True) - xhat * jnp.mean(d * xhat, axis=-1, keepdims=True)
        out_ref[...] = dmid_ref[...] + rstd * inner


def input_grad(place, grads, pieces, x, gain, dmid, earlier, n):
    rows, width = x.shape
    nb = len(grads)
    fb = pieces[0].shape[-1]
    vector = jax.ShapeDtypeStruct((1, width), F32)
    return pl.pallas_call(
        functools.partial(input_grad_kernel, nb=nb),
        grid=(3,),
        in_specs=[SMEM, constant((rows, width)), constant((1, width)), constant((rows, width))]
        + [pl.BlockSpec((rows, fb), lambda t: (0, t))] * nb
        + [pl.BlockSpec(memory_space=pl.ANY)] * (len(pieces) + 1),
        out_specs=[constant((rows, width)), constant((1, width)), constant((1, width))],
        out_shape=[jax.ShapeDtypeStruct((rows, width), F32), vector, vector],
        scratch_shapes=[pltpu.VMEM((rows, width), F32)] + piece_scratch(pieces, nb, n),
        compiler_params=params(),
        cost_estimate=cost(6 * rows * width * width, 20e6),
        name="input_grad",
    )(place, x, gain, dmid, *grads, *pieces, earlier)


def swap_with(value, axis, k):
    size = lax.axis_size(axis)
    return lax.ppermute(value, axis, [(i, i ^ k) for i in range(size)])


def powers(size):
    return [1 << i for i in range(size.bit_length() - 1)]


def direct(shard, n):
    return [swap_with(shard, "seq", k * n // 4) for k in range(1, 4)]


def planes(n):
    quarter = n // 4
    return [[z * quarter + i for i in range(quarter)] for z in range(4)]


def lines(n):
    return [list(group) for group in zip(*planes(n))]


def gather_line(shard, n):
    return lax.all_gather(shard, "seq", axis_index_groups=lines(n))


def gather_plane(line, n):
    plane = lax.all_gather(line, "seq", axis_index_groups=planes(n))
    return plane.reshape((n,) + line.shape[1:])


def scatter_groups(grad, groups):
    return lax.psum_scatter(grad, "seq", scatter_dimension=0, axis_index_groups=groups)


def halves(shard, arrived):
    both = jnp.stack([shard] + arrived)
    return both[:, 0], both[:, 1]


def together(*values):
    return lax.optimization_barrier(values)


def gather_cores(pieces, nb):
    out = list(pieces)
    for k in range(1, nb):
        out += [swap_with(piece, "batch", k) for piece in pieces]
    return out


def place_of(relative, bits, n):
    place = relative // (n // 4)
    for i, bit in enumerate(bits):
        place = place + jnp.where(relative & bit, 4 << i, 0)
    return place


def place_table(position, core, n):
    relative = jnp.arange(n, dtype=jnp.int32) ^ position
    bits = powers(n // 4)
    ends = jnp.stack([core, position]).astype(jnp.int32)
    return jnp.concatenate([place_of(relative, bits, n), place_of(relative, bits[::-1], n), ends])


def plus(value, arrived):
    return (value.astype(F32) + arrived.astype(F32)).astype(BF)


def reduce_first(a_send, b_send, n):
    return swap_with(a_send, "seq", n // 8), swap_with(b_send, "seq", 1)


def split_next(total):
    m = total.shape[1] // 2
    return total[:, :m], total[:, m:]


def reduce_steps(total, bit_of, n):
    total = total.reshape((4, n // 8) + total.shape[1:])
    while total.shape[1] > 1:
        keep, send = split_next(total)
        total = plus(keep, swap_with(send, "seq", bit_of(send.shape[1])))
    return total[:, 0]


def reduce_rest(a, b, n):
    a = reduce_steps(a, lambda m: m, n)
    b = reduce_steps(b, lambda m: 2 * m, n)
    return jnp.stack([a, b], axis=1)


def reduce_direct(total, n):
    return [swap_with(total[k], "seq", k * n // 4) for k in range(1, 4)]


def reduce_last(total, arrived):
    out = total[0].astype(F32)
    for term in arrived:
        out = out + term.astype(F32)
    return out[0], out[1]


def total_over(value, axis, steps):
    for k in steps:
        value = value + swap_with(value, axis, k)
    return value


def body(
    tokens,
    cotangent,
    lengths,
    random_blocks,
    query_key_value_weight,
    output_weight,
    up_weight,
    down_weight,
    out_bias,
    up_bias,
    down_bias,
    gain_attn,
    shift_attn,
    gain_ffn,
    shift_ffn,
):
    n = lax.axis_size("seq")
    nb = lax.axis_size("batch")
    position = lax.axis_index("seq")
    core = lax.axis_index("batch")
    micros, _, local, width = tokens.shape
    hidden = up_bias.shape[0]
    nblk = n * local // BLOCK
    bpd = local // BLOCK
    per = micros * H // n
    lanes = per * HD
    groups = H // per
    fb = width // nb
    kr = width // n
    kh = kr // 2
    fr = hidden // n
    per_b = hidden // width
    bits = powers(n // 4)
    row = lambda v: v.reshape(1, -1)
    place = place_table(position, core, n)

    shard = query_key_value_weight.reshape(2, kh, 3, fb).transpose(0, 2, 1, 3)
    stacked_up = up_weight.reshape(kr, per_b, fb).transpose(1, 0, 2).reshape(per_b * kr, fb)
    rest = jnp.concatenate([down_weight, stacked_up, output_weight])
    part_a, part_b = halves(shard, direct(shard, n))
    part_a, part_b, rest = together(part_a, part_b, rest)
    rest_line = gather_line(rest, n)
    for i, bit in enumerate(bits):
        found_a = swap_with(part_a, "seq", bit)
        found_b = swap_with(part_b, "seq", bits[-1 - i])
        if i < len(bits) - 1:
            part_a = jnp.concatenate([part_a, found_a])
            part_b = jnp.concatenate([part_b, found_b])
    qkv_pieces = gather_cores([part_a, found_a, part_b, found_b], nb)

    x = tokens.reshape(micros * local, width)
    g = cotangent.reshape(micros * local, width)
    micro = position * per // H
    head = position * per % H
    table = lax.dynamic_slice(
        random_blocks[:, 0], (micro, 0, head, 0), (1, nblk, per, NRAND)
    ).reshape(-1)
    limit = lax.dynamic_slice(lengths[:, 0], (micro,), (1,))

    def swap(value):
        return lax.all_to_all(value, "seq", split_axis=0, concat_axis=0, tiled=True)

    def over_cores(value):
        return [value] + [swap_with(value, "batch", k) for k in range(1, nb)]

    def columns_over_cores(value, cols):
        mine = lambda c: lax.dynamic_slice_in_dim(value, c * cols, cols, axis=1)
        return [mine(core)] + [swap_with(mine(core ^ k), "batch", k) for k in range(1, nb)]

    qkv, h1 = project(place, x, row(gain_attn), row(shift_attn), qkv_pieces, nb, n, micros, local, lanes)
    qkv, rest_line = together(qkv, rest_line)
    rest_plane = gather_plane(rest_line, n)
    qkv_all = swap(qkv.reshape(n, 3, local, lanes)).reshape(n, 3, bpd, BLOCK, lanes)
    g_cores, h1_cores = columns_over_cores(g, fb), over_cores(h1)
    turned = turn(place, h1_cores, n)
    qkv_all, g_cores, turned = together(qkv_all, g_cores, turned)
    mixed, lse = attend(qkv_all, table, limit, per)
    o = swap(mixed.reshape(n, local, lanes)).reshape(micros, groups, local, lanes)
    o, rest_plane = together(o, rest_plane)
    rest_pieces = gather_cores([rest_plane], nb)
    (
        result,
        dmid,
        branch,
        dout,
        att,
        h2,
        act,
        pre_grad,
        d_out_bias,
        d_up_bias,
        d_down_bias,
        d_gain_ffn,
        d_shift_ffn,
    ) = middle(
        nb,
        n,
        place,
        o,
        x,
        g,
        rest_pieces,
        row(out_bias),
        row(up_bias),
        row(down_bias),
        row(gain_ffn),
        row(shift_ffn),
    )
    dout_all = swap(dout.reshape(n, local, lanes)).reshape(n, bpd, BLOCK, lanes)

    rest_grad = ffn_grads(
        over_cores(act),
        g_cores,
        over_cores(h2),
        [pre_grad] + [swap_with(pre_grad[k : k + 1], "batch", k) for k in range(1, nb)],
        over_cores(att),
        columns_over_cores(branch, fb),
        n,
    )
    dout_all, rest_grad = together(dout_all, rest_grad)
    rest_line = scatter_groups(rest_grad, planes(n))
    grads = attend_back(qkv_all, dout_all, lse, table, limit, per)
    grads_back = swap(grads.reshape(n, 3, local, lanes)).reshape(micros, groups, 3, local, lanes)
    own_grads = split_by_core(place, grads_back, nb, n)
    grad_cores = [own_grads[0]] + [swap_with(own_grads[k], "batch", k) for k in range(1, nb)]
    a_send, a_keep, b_send, b_keep = qkv_grad(turned, grad_cores, n)
    a_keep, rest_line = together(a_keep, rest_line)
    grad_rest = scatter_groups(rest_line, lines(n)).astype(F32)
    first_a, first_b = reduce_first(a_send, b_send, n)
    grad_x, d_gain_attn, d_shift_attn = input_grad(
        place, own_grads, qkv_pieces, x, row(gain_attn), dmid, a_keep, n
    )
    vectors = [d_out_bias, d_up_bias, d_down_bias, d_gain_attn, d_shift_attn, d_gain_ffn, d_shift_ffn]
    sums = jnp.concatenate(vectors, axis=1)
    sums, first_a, first_b = together(sums, first_a, first_b)
    qkv_reduced = reduce_rest(plus(a_keep, first_a), plus(b_keep, first_b), n)
    sums = total_over(total_over(sums, "batch", powers(nb)), "seq", powers(n // 4))
    qkv_reduced, sums = together(qkv_reduced, sums)
    grad_down = grad_rest[:fr]
    grad_up = grad_rest[fr:-kr].reshape(per_b, kr, fb).transpose(1, 0, 2).reshape(kr, per_b * fb)
    grad_out = grad_rest[-kr:]
    arrived = reduce_direct(qkv_reduced, n)
    near, far, diagonal = direct(sums, n)
    *arrived, grad_down, grad_up, grad_out = together(*arrived, grad_down, grad_up, grad_out)
    grad_a, grad_b = reduce_last(qkv_reduced, arrived)
    grad_qkv = jnp.stack([grad_a, grad_b]).transpose(0, 2, 1, 3).reshape(kr, 3 * fb)
    sums = ((sums + near) + (far + diagonal))[0]
    ends = []
    for vector in vectors[:-1]:
        ends.append((ends[-1] if ends else 0) + vector.shape[1])
    return (
        result.reshape(tokens.shape),
        grad_x.reshape(tokens.shape),
        grad_qkv,
        grad_out,
        grad_up,
        grad_down,
        *jnp.split(sums, ends),
    )


def solution(mesh):
    rows = P(None, "batch", "seq", None)
    weight = P("seq", "batch")
    return jax.shard_map(
        body,
        mesh=mesh,
        in_specs=(rows, rows, P(None, "batch"), P(None, "batch", None, None, None))
        + (weight,) * 4
        + (P(),) * 7,
        out_specs=(rows, rows) + (weight,) * 4 + (P(),) * 7,
        check_vma=False,
    )
```
